32 devices in a mesh: dp: 8 (over y, x, core), section: 4 (over z).
Axes of the slice: x: 2, y: 2, z: 4, core: 2. Of those that a mesh axis runs over, the one named last changes fastest.
Arguments:
- tokens: bfloat16 [16, 1024, 768], P('dp'), may hold values from -6 to 6
- span_start: int32 [16], P('dp'), may hold values from 0 to 511
- span_length: int32 [16], P('dp'), may hold values from 1 to 512
- time_step: int32 [16], P('dp'), may hold values from 0 to 511
- time_table: float32 [512, 128], replicated, may hold values from -6 to 6
- mask_embed: bfloat16 [768], replicated, may hold values from -6 to 6
- mod_weight: float32 [4, 128, 2304], P('section'), may hold values from -0.5 to 0.5
- mod_bias: float32 [4, 2304], P('section'), may hold values from -3 to 3
- norm_gain: float32 [4, 768], P('section'), may hold values from 0.5 to 1.5
- in_weight: bfloat16 [4, 768, 3072], P('section')
- in_bias: float32 [4, 3072], P('section'), may hold values from -2 to 2
- out_weight: bfloat16 [4, 3072, 768], P('section'), may hold values from -0.109375 to 0.109375
- out_bias: float32 [4, 768], P('section'), may hold values from -2 to 2
- cotangent: bfloat16 [16, 1024, 768], P('dp'), may hold values from -6 to 6
Outputs:
- hidden_states: bfloat16 [4, 16, 1024, 768], P('section', 'dp')
- stream_grads: bfloat16 [4, 16, 1024, 768], P('section', 'dp')
- time_table_grad: float32 [512, 128], replicated
- mask_embed_grad: float32 [768], replicated
- mod_weight_grad: float32 [4, 128, 2304], P('section')
- mod_bias_grad: float32 [4, 2304], P('section')
- norm_gain_grad: float32 [4, 768], P('section')
- in_weight_grad: float32 [4, 768, 3072], P('section')
- in_bias_grad: float32 [4, 3072], P('section')
- out_weight_grad: float32 [4, 3072, 768], P('section')
- out_bias_grad: float32 [4, 768], P('section')
The draws below stay inside these ranges and needn't reach their ends.
All inputs are finite; a program needn't handle non-finite values.
Results may differ from the reference program's by a relative error of at most 0.015.
The reference program's roundings to bfloat16 on the way count: a program that leaves them out, or rounds other values in their place, can miss the bound.
Values may be sent and summed in bfloat16 or wider, within the bound.
A program may use at most 256 MiB of HBM per device.

```python
import math
import jax
import jax.numpy as jnp
from jax import lax

D = 768
HEAD = 64
FF = 3072
COND = 128
LEN = 1024
SECTIONS = 4
TSTEPS = 512
SEQS = 16


def draw_in_weight(key, part):
    key = jax.random.fold_in(key, 11)
    shape = (SECTIONS, D, FF)
    base = jax.random.truncated_normal(key, -6.0, 6.0, shape, jnp.float32)
    column_block = lax.broadcasted_iota(jnp.int32, shape, 2) // D
    section_number = lax.broadcasted_iota(jnp.int32, shape, 0)
    factor = jnp.where(column_block == 3, 8.0, jnp.where(column_block < 2, 0.8, 1.0))
    factor = jnp.where(section_number % 2 == 0, factor, 1.0)
    return (base * factor * D ** (-0.5)).astype(jnp.bfloat16)


def set_ends(entries, rng, low, largest):
    shape = entries.shape
    spot = [jax.random.randint(jax.random.fold_in(rng, axis), (), 0, shape[axis]) for axis in range(len(shape))]
    entries = entries.at[tuple(spot)].set(low)
    longest = shape.index(max(shape))
    spot[longest] = (spot[longest] + 1) % shape[longest]
    return entries.at[tuple(spot)].set(largest)


def raised(result, stream_key, source, target, parts, factor):
    def block_of(dim):
        return (jnp.arange(result.shape[dim]) // (result.shape[dim] // parts)).reshape((-1,) + (1,) * (result.ndim - 1 - dim))

    one_side = jax.random.permutation(stream_key, parts)[block_of(target)]
    far = (block_of(target) + parts // 2) % parts
    return jnp.where((block_of(source) == one_side) | (block_of(source) == far), factor * result, result)


def shard_levels(rng, shape, cuts, smallest, high):
    loudness, own = 1.0, jax.random.fold_in(rng, 6)
    for dim, blocks in cuts:
        heights = jnp.exp(jax.random.uniform(jax.random.fold_in(own, dim), (blocks,), jnp.float32, smallest / len(cuts), high / len(cuts)))
        loudness = loudness * jnp.repeat(heights, shape[dim] // blocks).reshape([-1 if axis == dim else 1 for axis in range(len(shape))])
    return loudness


def gaussian(own_key, dims, scale, most, shards=(), dtype=jnp.bfloat16):
    gain = shard_levels(own_key, dims, shards, -0.22, 0.18) if shards else 1.0
    array = jax.random.normal(own_key, dims, jnp.float32) * scale * gain
    return jnp.minimum(jnp.maximum(array, -most), most).astype(dtype)


def heavy_noise(stream_key, extent, scale, most, shards, heavy, kind=jnp.bfloat16):
    result = scale * jax.random.normal(stream_key, extent, jnp.float32)
    if shards:
        result = result * shard_levels(stream_key, extent, shards, -0.22, 0.18)
    return jnp.clip(raised(result, jax.random.fold_in(stream_key, 3), *heavy), -most, most).astype(kind)


def setup_inputs(seed: int = 0) -> dict:
    seeds = jax.random.split(jax.random.key(seed), 15)
    tokens = gaussian(seeds[0], (SEQS, LEN, D), 1.0, 6.0, ((0, 8),))
    span_start = set_ends(jax.random.randint(seeds[1], (SEQS,), 0, LEN // 2), jax.random.fold_in(seeds[1], 1), 0, (LEN // 2) - 1).astype(jnp.int32)
    span_length = set_ends(jax.random.randint(seeds[2], (SEQS,), 1, LEN // 2 + 1), jax.random.fold_in(seeds[2], 1), 1, (LEN // 2 + 1) - 1).astype(jnp.int32)
    time_step = set_ends(jax.random.randint(seeds[3], (SEQS,), 0, TSTEPS), jax.random.fold_in(seeds[3], 1), 0, TSTEPS - 1).astype(jnp.int32)
    time_table = gaussian(seeds[4], (TSTEPS, COND), 1.0, 6.0, (), jnp.float32)
    mask_embed = gaussian(seeds[5], (D,), 1.0, 6.0)
    mod_weight = gaussian(seeds[6], (SECTIONS, COND, 3 * D), COND ** -0.5, 0.5, ((0, 4),), jnp.float32)
    mod_bias = gaussian(seeds[7], (SECTIONS, 3 * D), 0.5, 3.0, ((0, 4),), jnp.float32)
    norm_gain = jnp.clip(1.0 + 0.1 * jax.random.normal(seeds[8], (SECTIONS, D), jnp.float32), 0.5, 1.5)
    in_weight = draw_in_weight(jax.random.fold_in(seeds[14], 71), 0)
    in_bias = gaussian(seeds[10], (SECTIONS, FF), 0.3, 2.0, ((0, 4),), jnp.float32)
    out_weight = gaussian(seeds[11], (SECTIONS, FF, D), FF ** -0.5, 0.109375, ((0, 4),))
    out_bias = gaussian(seeds[12], (SECTIONS, D), 0.3, 2.0, ((0, 4),), jnp.float32)
    cotangent = heavy_noise(seeds[13], (SEQS, LEN, D), 1.0, 6.0, ((0, 8),), (0, 2, 8, 2.0))
    return {"tokens": tokens, "span_start": span_start, "span_length": span_length, "time_step": time_step, "time_table": time_table, "mask_embed": mask_embed, "mod_weight": mod_weight, "mod_bias": mod_bias, "norm_gain": norm_gain, "in_weight": in_weight, "in_bias": in_bias, "out_weight": out_weight, "out_bias": out_bias, "cotangent": cotangent}


@jax.custom_vjp
def low(v):
    return lax.optimization_barrier(v.astype(jnp.bfloat16)).astype(jnp.float32)

@jax.custom_vjp
def low_back(v):
    return v

def low_keep(v):
    return (low(v), None)

def low_pass(kept, grad):
    return (grad,)

def back_keep(v):
    return (v, None)

def back_low(kept, grad):
    return (low(grad),)
low.defvjp(low_keep, low_pass)
low_back.defvjp(back_keep, back_low)
EPS = 1e-06
HIGH = lax.Precision.HIGHEST

def highest_dot(left, right):
    return jnp.dot(left, right, precision=HIGH)

def rope_tables(length, head_size):
    half_head = head_size // 2
    position = lax.broadcasted_iota(jnp.float32, (length, half_head), 0)
    column = lax.broadcasted_iota(jnp.float32, (length, half_head), 1)
    angles = position * jnp.exp(column * (-2.0 * math.log(10000.0) / head_size))
    return (jnp.cos(angles)[:, None, :], jnp.sin(angles)[:, None, :])

def rotate(values, cosine_table, sine_table):
    half_head = values.shape[-1] // 2
    front_half = values[..., :half_head]
    back_half = values[..., half_head:]
    return jnp.concatenate([front_half * cosine_table - back_half * sine_table, back_half * cosine_table + front_half * sine_table], -1)

def modulated(current, modulation_row, gain_row):
    features = current.shape[1]
    shifting = modulation_row[:features]
    scaling = modulation_row[features:2 * features]
    gating = modulation_row[2 * features:]
    average = lax.optimization_barrier(jnp.mean(current, -1, keepdims=True))
    centered = current - average
    standard = centered * lax.rsqrt(lax.optimization_barrier(jnp.mean(centered * centered, -1, keepdims=True)) + EPS)
    modulated_rows = low(standard * gain_row * (1.0 + scaling) + shifting)
    return (modulated_rows, gating)

def attention_section(current, modulation_row, gain_row, first_matrix, first_bias):
    length, features = current.shape
    head_count = features // HEAD
    modulated_rows, gating = modulated(current, modulation_row, gain_row)
    projected = low_back(highest_dot(modulated_rows, first_matrix[:, :3 * features]) + first_bias[:3 * features])
    cosine_table, sine_table = rope_tables(length, HEAD)
    queries = low(rotate(projected[:, :features].reshape(length, head_count, HEAD), cosine_table, sine_table))
    key_rows = low(rotate(projected[:, features:2 * features].reshape(length, head_count, HEAD), cosine_table, sine_table))
    value_rows = low(projected[:, 2 * features:].reshape(length, head_count, HEAD))
    scores = low_back(jnp.einsum('qhd,khd->hqk', queries, key_rows, precision=HIGH) * HEAD ** (-0.5))
    row_max = lax.optimization_barrier(jnp.max(scores, -1, keepdims=True))
    exponents = jnp.exp(scores - row_max)
    weights = low(exponents / lax.optimization_barrier(jnp.sum(exponents, -1, keepdims=True)))
    mixed = low_back(low(jnp.einsum('hqk,khd->qhd', weights, value_rows, precision=HIGH).reshape(length, features)))
    branch = low_back(highest_dot(mixed, first_matrix[:, 3 * features:]) + first_bias[3 * features:])
    return current + gating * branch

def mlp_section(current, modulation_row, gain_row, first_matrix, first_bias, second_matrix, second_bias):
    modulated_rows, gating = modulated(current, modulation_row, gain_row)
    hidden = low_back(highest_dot(modulated_rows, first_matrix) + first_bias)
    activated = low(jax.nn.gelu(hidden, approximate=True))
    branch = low_back(highest_dot(activated, second_matrix) + second_bias)
    return current + gating * branch

def one_sequence(weights_set, sequence_row):
    time_rows, embed_row, mod_matrix, mod_rows, gains, first_matrix, first_bias, second_matrix, second_bias = weights_set
    tokens_row, start_at, span_size, step_at, probe_rows = sequence_row
    length = tokens_row.shape[0]
    position = lax.broadcasted_iota(jnp.int32, (length,), 0)
    in_span = (position >= start_at) & (position < start_at + span_size)
    current = jnp.where(in_span[:, None], embed_row[None, :], tokens_row)
    condition = jax.nn.silu(time_rows[step_at])
    results = []
    for section_number in range(SECTIONS):
        if section_number > 0:
            current = low_back(low(results[-1])) + probe_rows[section_number]
        modulation_row = highest_dot(condition, mod_matrix[section_number]) + mod_rows[section_number]
        if section_number % 2 == 0:
            section_out = attention_section(current, modulation_row, gains[section_number], first_matrix[section_number], first_bias[section_number])
        else:
            section_out = mlp_section(current, modulation_row, gains[section_number], first_matrix[section_number], first_bias[section_number], second_matrix[section_number], second_bias[section_number])
        results.append(section_out)
    return jnp.stack(results)

def reference(tokens, span_start, span_length, time_step, time_table, mask_embed, mod_weight, mod_bias, norm_gain, in_weight, in_bias, out_weight, out_bias, cotangent):
    weights_set = tuple((member.astype(jnp.float32) for member in (time_table, mask_embed, mod_weight, mod_bias, norm_gain, in_weight, in_bias, out_weight, out_bias)))
    sequences = tokens.shape[0]
    probes = jnp.zeros((sequences, SECTIONS, LEN, D), jnp.float32)
    checked = jax.checkpoint(one_sequence)

    def forward(tokens_full, weights_in, probe_in):

        def scan_step(carried, sequence_row):
            return (carried, checked(weights_in, sequence_row))
        carried_out, stacked_out = lax.scan(scan_step, jnp.zeros((), jnp.float32), (tokens_full, span_start, span_length, time_step, probe_in))
        return stacked_out
    stacked, pull_back = jax.vjp(forward, tokens.astype(jnp.float32), weights_set, probes)
    start_grads = jnp.zeros_like(stacked).at[:, SECTIONS - 1].set(cotangent.astype(jnp.float32))
    grad_tokens, grad_weights, grad_probes = pull_back(start_grads)
    hidden_states = jnp.transpose(stacked, (1, 0, 2, 3)).astype(jnp.bfloat16)
    stream_grads = jnp.transpose(grad_probes, (1, 0, 2, 3)).at[0].set(grad_tokens).astype(jnp.bfloat16)
    return (hidden_states, stream_grads, grad_weights[0], grad_weights[1], grad_weights[2], grad_weights[3], grad_weights[4], grad_weights[5], grad_weights[6], grad_weights[7], grad_weights[8])
```

```python
from functools import partial
import math

import jax
import jax.numpy as jnp
from jax import lax
from jax.experimental import pallas as pl
from jax.experimental.pallas import tpu as pltpu
from jax.sharding import PartitionSpec as P

HEAD = 64
HALF = HEAD // 2
EPS = 1e-06
HIGH = lax.Precision.HIGHEST
F32 = jnp.float32
BF16 = jnp.bfloat16
SCALE = HEAD ** (-0.5)
EXP2_SCALE = SCALE * math.log2(math.e)
GELU_C = math.sqrt(2.0 / math.pi)
VMEM_LIMIT = 56 << 20
AXES = ("dp", "section")


def dot_nn(left, right):
    return jnp.dot(left, right, preferred_element_type=F32)


def dot_nt(left, right):
    return lax.dot_general(left, right, (((1,), (1,)), ((), ())), preferred_element_type=F32)


def params(**more):
    return pltpu.CompilerParams(vmem_limit_bytes=VMEM_LIMIT, **more)


def shape(dims, dtype):
    return jax.ShapeDtypeStruct(dims, dtype)


def normalize(rows):
    average = jnp.mean(rows, -1, keepdims=True)
    centered = rows - average
    inverse_std = lax.rsqrt(jnp.mean(centered * centered, -1, keepdims=True) + EPS)
    return centered * inverse_std, inverse_std


MESH = pl.DeviceIdType.MESH
CHUNKS = 2


def pipeline_kernel(
    enter_ref, cot_ref, wide_ref, second_ref, mods_ref, gain_ref, keep_ref, bias_column_ref, bias_row_ref,
    out_bias_ref, cos_ref, sin_ref,
    states_ref, stream_ref, kept_first, kept_second, kept_rows, back_first, back_second, sums_ref,
    weights, streams, others, upstreams, up_others, mixed_got, first_buf, second_buf, branches, leaving,
    mixed_own, mixed_send, grad_send, grad_own, lse_ref,
    load_sem, pass_send, pass_recv, back_recv, swap_send, swap_recv, place_send, place_recv, store_sem, fetch_sem,
):
    section = lax.axis_index("section")
    sections = lax.axis_size("section")
    dp_index = lax.axis_index("dp")
    core = lax.rem(dp_index, 2)
    partner = dp_index + 1 - 2 * core
    micros, half, features = streams.shape
    width = mixed_own.shape[1]
    heads = width // HEAD
    length = 2 * half
    part_rows = half // CHUNKS
    attends = lax.rem(section, 2) == 0
    feeds = lax.rem(section, 2) == 1
    is_first = section == 0
    is_last = section == sections - 1
    hidden = wide_ref.shape[0]
    feed_step = half
    feed_parts = hidden // feed_step

    barrier = pltpu.get_barrier_semaphore()
    pl.semaphore_signal(barrier, inc=1, device_id=(partner, section), device_id_type=MESH)

    @pl.when(section > 0)
    def _():
        pl.semaphore_signal(barrier, inc=1, device_id=(dp_index, section - 1), device_id_type=MESH)

    @pl.when(section < sections - 1)
    def _():
        pl.semaphore_signal(barrier, inc=1, device_id=(dp_index, section + 1), device_id_type=MESH)

    def load_wide():
        return pltpu.make_async_copy(wide_ref, weights, load_sem.at[0])

    def second_at(part):
        return others.at[part] if part < micros else up_others.at[part - micros]

    def load_second(part):
        return pltpu.make_async_copy(
            second_ref.at[pl.ds(part * feed_step, feed_step)], second_at(part), load_sem.at[1 + part]
        )

    def load_enter(m):
        return pltpu.make_async_copy(enter_ref.at[m], streams.at[m], fetch_sem.at[1 + m])

    def load_cot(m):
        return pltpu.make_async_copy(cot_ref.at[m], upstreams.at[m], fetch_sem.at[1 + m])

    @pl.when(is_first)
    def _():
        for m in range(micros):
            load_enter(m).start()

    load_wide().start()

    @pl.when(feeds)
    def _():
        for part in range(feed_parts):
            load_second(part).start()

    @pl.when(is_last)
    def _():
        for m in range(micros):
            load_cot(m).start()

    load_wide().wait()

    @pl.when(feeds)
    def _():
        for part in range(feed_parts):
            load_second(part).wait()

    pl.semaphore_wait(
        barrier, 1 + jnp.where(section > 0, 1, 0) + jnp.where(section < sections - 1, 1, 0)
    )

    def rows_of(part):
        return slice(part * part_rows, (part + 1) * part_rows)

    def schedule(step):
        turns = jnp.where(is_last, 1, 0)
        forward = jnp.where(is_last, 1 - lax.rem(step, 2), jnp.where(step < micros, 1, 0))
        micro = jnp.where(is_last, step // 2, lax.rem(step, micros))
        del turns
        return forward == 1, micro

    def pass_on(step, part, micro, forward):
        slot = lax.rem(step, 2)
        source = leaving.at[slot, pl.ds(part * part_rows, part_rows)]
        if forward:
            return pltpu.make_async_remote_copy(
                source, streams.at[micro, pl.ds(part * part_rows, part_rows)],
                pass_send.at[slot, part], pass_recv.at[micro, part],
                device_id=(dp_index, section + 1), device_id_type=MESH,
            )
        return pltpu.make_async_remote_copy(
            source, upstreams.at[micro, pl.ds(part * part_rows, part_rows)],
            pass_send.at[slot, part], back_recv.at[micro, part],
            device_id=(dp_index, section - 1), device_id_type=MESH,
        )

    def place_target(target, micro):
        return target.at[micro // 2, pl.ds(core * half, half)]

    def place_local(step, micro, target):
        slot = lax.rem(step, 2)
        return pltpu.make_async_copy(leaving.at[slot], place_target(target, micro), place_send.at[slot])

    def place_remote(step, micro, target, index):
        slot = lax.rem(step, 2)
        return pltpu.make_async_remote_copy(
            leaving.at[slot], place_target(target, micro), place_send.at[slot],
            place_recv.at[index, micro // 2], device_id=(partner, section), device_id_type=MESH,
        )

    def send_part(step, part, micro, forward):
        reaches = section < sections - 1 if forward else section > 0

        @pl.when(reaches)
        def _():
            pass_on(step, part, micro, forward).start()

    def place_result(step, micro, forward):
        target, index = (states_ref, 0) if forward else (stream_ref, 1)
        mine = lax.rem(micro, 2) == core

        @pl.when(mine)
        def _():
            place_local(step, micro, target).start()

        @pl.when(jnp.logical_not(mine))
        def _():
            place_remote(step, micro, target, index).start()

    def leaving_free(step):
        was_forward, micro = schedule(step)
        mine = lax.rem(micro, 2) == core
        for forward, cond in ((True, was_forward), (False, jnp.logical_not(was_forward))):
            reaches = section < sections - 1 if forward else section > 0
            target, index = (states_ref, 0) if forward else (stream_ref, 1)

            @pl.when(cond & reaches)
            def _():
                for part in range(CHUNKS):
                    pass_on(step, part, micro, forward).wait_send()

            @pl.when(cond & mine)
            def _():
                place_local(step, micro, target).wait()

            @pl.when(cond & jnp.logical_not(mine))
            def _():
                place_remote(step, micro, target, index).wait_send()

    def swap(kind, source, target, micro):
        return pltpu.make_async_remote_copy(
            source, target, swap_send.at[kind], swap_recv.at[kind, micro],
            device_id=(partner, section), device_id_type=MESH,
        )

    def store_out(source, target, which):
        return pltpu.make_async_copy(source, target, store_sem.at[which])

    def stores_done():
        store_out(first_buf.at[0], kept_first.at[0], 0).wait()
        store_out(second_buf, kept_second.at[0], 1).wait()

    def arrive(micro, part, forward):
        local = is_first if forward else is_last

        if part == 0:

            @pl.when(local)
            def _():
                (load_enter if forward else load_cot)(micro).wait()

        @pl.when(jnp.logical_not(local))
        def _():
            pass_on(0, part, micro, forward).wait_recv()

    def attention_forward(step, micro):
        mod = mods_ref[pl.ds(micro * 8, 8), :]
        gain = gain_ref[...]
        slot = lax.rem(micro, 2)
        for part in range(CHUNKS):
            arrive(micro, part, True)
        exchange = swap(0, streams.at[micro], others.at[micro], micro)
        exchange.start()

        @pl.when(step > 0)
        def _():
            stores_done()

        def project(source, part):
            standard, _ = normalize(source[micro, rows_of(part % CHUNKS), :].astype(F32))
            rows = (standard * gain * (1.0 + mod[1:2]) + mod[0:1]).astype(BF16)
            place = (part // CHUNKS) * features
            second_buf[rows_of(part % CHUNKS), place : place + features] = rows
            projected = dot_nt(weights[: 3 * width, :], rows) + bias_column_ref[:, 0:1]
            columns = slice(part * part_rows, (part + 1) * part_rows)
            cosine = cos_ref[:, columns]
            sine = sin_ref[:, columns]
            for block in range(3):
                lanes = slice(block * length + part * part_rows, block * length + (part + 1) * part_rows)
                if block == 2:
                    first_buf[slot, :width, lanes] = projected[2 * width :].astype(BF16)
                    continue
                for head in range(heads):
                    base = block * width + head * HEAD
                    front = projected[base : base + HALF]
                    back = projected[base + HALF : base + HEAD]
                    at = head * HEAD
                    first_buf[slot, at : at + HALF, lanes] = (front * cosine - back * sine).astype(BF16)
                    first_buf[slot, at + HALF : at + HEAD, lanes] = (back * cosine + front * sine).astype(BF16)

        for part in range(CHUNKS):
            project(streams, part)
        exchange.wait_recv()
        for part in range(CHUNKS, 2 * CHUNKS):
            project(others, part)

        def scores_of(head):
            base = pl.multiple_of(head * HEAD, HEAD)
            key_rows = first_buf[slot, pl.ds(base, HEAD), length : 2 * length].T
            return dot_nn(key_rows, first_buf[slot, pl.ds(base, HEAD), :length])

        def finish(head, within, scores):
            base = pl.multiple_of(head * HEAD, HEAD)
            top = jnp.max(scores, 0, keepdims=True) * EXP2_SCALE
            spread = jnp.exp2(scores * EXP2_SCALE - top)
            total = jnp.sum(spread, 0, keepdims=True)
            mixed = dot_nn(first_buf[slot, pl.ds(base, HEAD), 2 * length :], spread.astype(BF16))
            lse_ref[micro, pl.ds(head, 1), :] = top + jnp.log2(total)
            return (mixed * (1.0 / total)).astype(BF16)

        def head_pair(pair, carried):
            scores = scores_of(2 * pair), scores_of(2 * pair + 1)
            mixed = jnp.concatenate([finish(2 * pair + i, i, scores[i]) for i in range(2)], 0)
            at = pl.multiple_of(pair * length, length)
            first_buf[slot, width:, pl.ds(at, length)] = mixed
            turned = mixed.T
            lanes = pl.multiple_of(pair * 2 * HEAD, 2 * HEAD)
            mixed_own[:, pl.ds(lanes, 2 * HEAD)] = turned[:half]
            mixed_send[:, pl.ds(lanes, 2 * HEAD)] = turned[half:]
            return carried

        lax.fori_loop(0, heads // 2, head_pair, 0)
        give = swap(1, mixed_send, mixed_got.at[micro], micro)
        give.start()
        store_out(first_buf.at[slot], kept_first.at[micro], 0).start()
        store_out(second_buf, kept_second.at[micro], 1).start()

        @pl.when(step >= 2)
        def _():
            leaving_free(step - 2)

        give.wait_recv()
        for part in range(CHUNKS):
            rows = rows_of(part)
            branch = (
                dot_nn(mixed_own[rows, :], weights[3 * width : 4 * width, :])
                + dot_nn(mixed_got[micro, rows, :], weights[4 * width : 5 * width, :])
                + bias_row_ref[:, 3 * features :]
            )
            branches[micro, rows, :] = branch.astype(BF16)
            result = streams[micro, rows, :].astype(F32) + mod[2:3] * branch
            leaving[lax.rem(step, 2), rows, :] = result.astype(BF16)
            send_part(step, part, micro, True)
        place_result(step, micro, True)
        exchange.wait_send()
        give.wait_send()

    def feed_forward(step, micro):
        mod = mods_ref[pl.ds(micro * 8, 8), :]
        gain = gain_ref[...]

        @pl.when(step > 0)
        def _():
            stores_done()

        @pl.when(step >= 2)
        def _():
            leaving_free(step - 2)

        row_store = pltpu.make_async_copy(up_others.at[2], kept_rows.at[micro], store_sem.at[2])
        for part in range(CHUNKS):
            rows = rows_of(part)
            arrive(micro, part, True)
            standard, _ = normalize(streams[micro, rows, :].astype(F32))
            entering = (standard * gain * (1.0 + mod[1:2]) + mod[0:1]).astype(BF16)
            up_others[2, rows, :] = entering
            branch = jnp.broadcast_to(out_bias_ref[...], (part_rows, features))
            for piece in range(feed_parts):
                lanes = slice(piece * feed_step, (piece + 1) * feed_step)
                value = dot_nt(entering, weights[lanes, :]) + bias_row_ref[:, lanes]
                square = value * value
                bend = jnp.tanh(GELU_C * value * (1.0 + 0.044715 * square))
                active = (0.5 * value * (1.0 + bend)).astype(BF16)
                second_buf[rows, lanes] = active
                first_buf[0, rows, lanes] = (
                    0.5 * (1.0 + bend)
                    + (0.5 * GELU_C) * value * (1.0 - bend * bend) * (1.0 + (3 * 0.044715) * square)
                ).astype(BF16)
                branch = branch + dot_nn(active, second_at(piece)[...])
            branches[micro, rows, :] = branch.astype(BF16)
            result = streams[micro, rows, :].astype(F32) + mod[2:3] * branch
            leaving[lax.rem(step, 2), rows, :] = result.astype(BF16)
            send_part(step, part, micro, True)
        place_result(step, micro, True)
        store_out(first_buf.at[0], kept_first.at[micro], 0).start()
        store_out(second_buf, kept_second.at[micro], 1).start()
        row_store.start()
        row_store.wait()

    def attention_backward(step, micro):
        mod = mods_ref[pl.ds(micro * 8, 8), :]
        gain = gain_ref[...]
        stores_done()
        fetch = pltpu.make_async_copy(kept_first.at[micro], first_buf.at[0], fetch_sem.at[0])
        fetch.start()
        for part in range(CHUNKS):
            arrive(micro, part, False)
        exchange = swap(2, upstreams.at[micro], up_others.at[micro], micro)
        exchange.start()
        grad_mixed_at = 2 * features

        def into_heads(source, part):
            grad_branch = (mod[2:3] * source[micro, rows_of(part % CHUNKS), :].astype(F32)).astype(BF16)
            place = (part // CHUNKS) * features
            second_buf[rows_of(part % CHUNKS), place : place + features] = grad_branch
            lanes = slice(grad_mixed_at + part * part_rows, grad_mixed_at + (part + 1) * part_rows)
            second_buf[:width, lanes] = dot_nt(weights[3 * width : 4 * width, :], grad_branch).astype(BF16)

        for part in range(CHUNKS):
            into_heads(upstreams, part)
        exchange.wait_recv()
        for part in range(CHUNKS, 2 * CHUNKS):
            into_heads(up_others, part)
        fetch.wait()
        cosine = cos_ref[...]
        sine = sin_ref[...]

        def turn_back(base, block, gradient):
            lanes = slice(block * length, (block + 1) * length)
            front = gradient[:HALF] * SCALE
            back = gradient[HALF:] * SCALE
            first_buf[1, pl.ds(base, HALF), lanes] = (front * cosine + back * sine).astype(BF16)
            first_buf[1, pl.ds(pl.multiple_of(base + HALF, HALF), HALF), lanes] = (
                back * cosine - front * sine
            ).astype(BF16)

        def one_head(head, mixed):
            base = pl.multiple_of(head * HEAD, HEAD)
            query = first_buf[0, pl.ds(base, HEAD), :length]
            key = first_buf[0, pl.ds(base, HEAD), length : 2 * length]
            value = first_buf[0, pl.ds(base, HEAD), 2 * length :]
            grad_mixed = second_buf[pl.ds(base, HEAD), grad_mixed_at : grad_mixed_at + length]
            delta = jnp.sum(grad_mixed.astype(F32) * mixed.astype(F32), 0, keepdims=True)
            scores = dot_nn(key.T, query)
            spread = jnp.exp2(scores * EXP2_SCALE - lse_ref[micro, pl.ds(head, 1), :])
            grad_spread = dot_nn(value.T, grad_mixed)
            grad_scores = (spread * (grad_spread - delta)).astype(BF16)
            grad_value = dot_nn(spread.astype(BF16), grad_mixed.T)
            grad_key = dot_nn(grad_scores, query.T)
            grad_query = dot_nn(key, grad_scores)
            turn_back(base, 0, grad_query)
            turn_back(base, 1, grad_key.T)
            first_buf[1, pl.ds(base, HEAD), 2 * length :] = grad_value.T.astype(BF16)

        def head_pair(pair, carried):
            at = pl.multiple_of(pair * length, length)
            mixed = first_buf[0, width:, pl.ds(at, length)]
            one_head(2 * pair, mixed[:HEAD])
            one_head(2 * pair + 1, mixed[HEAD:])
            return carried

        lax.fori_loop(0, heads // 2, head_pair, 0)

        def grad_rows_of(part):
            total = None
            for block in range(3):
                lanes = slice(block * length + part * part_rows, block * length + (part + 1) * part_rows)
                term = dot_nn(first_buf[1, :width, lanes].T, weights[block * width : (block + 1) * width, :])
                total = term if total is None else total + term
            return total

        for part in range(CHUNKS, 2 * CHUNKS):
            grad_send[rows_of(part - CHUNKS), :] = grad_rows_of(part).astype(BF16)
        give = swap(3, grad_send, others.at[micro], micro)
        give.start()
        store_out(first_buf.at[1], back_first.at[micro], 0).start()
        store_out(second_buf, back_second.at[micro], 1).start()
        for part in range(CHUNKS):
            grad_own[rows_of(part), :] = grad_rows_of(part)
        leaving_free(step - 2)
        give.wait_recv()
        for part in range(CHUNKS):
            rows = rows_of(part)
            finish_back(
                grad_own[rows, :] + others[micro, rows, :].astype(F32),
                streams[micro, rows, :].astype(F32),
                upstreams[micro, rows, :].astype(F32),
                branches[micro, rows, :].astype(F32),
                mod, gain, keep_ref[micro, rows, :] > 0.5,
                leaving, (lax.rem(step, 2), rows), sums_ref, micro, part == 0,
            )
            send_part(step, part, micro, False)
        place_result(step, micro, False)
        exchange.wait_send()
        give.wait_send()

    def feed_backward(step, micro):
        mod = mods_ref[pl.ds(micro * 8, 8), :]
        gain = gain_ref[...]
        stores_done()
        fetch = pltpu.make_async_copy(kept_first.at[micro], first_buf.at[0], fetch_sem.at[0])
        fetch.start()

        @pl.when(step >= 2)
        def _():
            leaving_free(step - 2)

        fetch.wait()
        for part in range(CHUNKS):
            rows = rows_of(part)
            arrive(micro, part, False)
            upstream = upstreams[micro, rows, :].astype(F32)
            grad_branch = (mod[2:3] * upstream).astype(BF16)
            second_buf[rows, :features] = grad_branch
            total = jnp.zeros((part_rows, features), F32)
            for piece in range(feed_parts):
                lanes = slice(piece * feed_step, (piece + 1) * feed_step)
                grad_active = dot_nt(grad_branch, second_at(piece)[...])
                grad_hidden = (grad_active * first_buf[0, rows, lanes].astype(F32)).astype(BF16)
                first_buf[1, rows, lanes] = grad_hidden
                total = total + dot_nn(grad_hidden, weights[lanes, :])
            finish_back(
                total,
                streams[micro, rows, :].astype(F32),
                upstream,
                branches[micro, rows, :].astype(F32),
                mod, gain, None,
                leaving, (lax.rem(step, 2), rows), sums_ref, micro, part == 0,
            )
            send_part(step, part, micro, False)
        place_result(step, micro, False)
        store_out(first_buf.at[1], back_first.at[micro], 0).start()
        store_out(second_buf, back_second.at[micro], 1).start()

    def one_step(step, carried):
        forward, micro = schedule(step)
        backward = jnp.logical_not(forward)

        @pl.when(attends & forward)
        def _():
            attention_forward(step, micro)

        @pl.when(attends & backward)
        def _():
            attention_backward(step, micro)

        @pl.when(feeds & forward)
        def _():
            feed_forward(step, micro)

        @pl.when(feeds & backward)
        def _():
            feed_backward(step, micro)

        return carried

    lax.fori_loop(0, 2 * micros, one_step, 0)
    stores_done()
    leaving_free(2 * micros - 2)
    leaving_free(2 * micros - 1)
    for index, target in enumerate((states_ref, stream_ref)):
        for slot in range(micros // 2):
            pltpu.make_async_remote_copy(
                leaving.at[0], target.at[slot, pl.ds((1 - core) * half, half)], place_send.at[0],
                place_recv.at[index, slot], device_id=(partner, section), device_id_type=MESH,
            ).wait_recv()


def finish_back(
    grad_rows, stream, upstream, branch, mod, gain, keep, leaving, place, sums_ref, micro, start,
):
    standard, inverse_std = normalize(stream)
    scaling = mod[1:2, :]
    grad_normed = grad_rows * (1.0 + scaling)
    grad_hat = grad_normed * gain
    grad_stream = upstream + inverse_std * (
        grad_hat
        - jnp.mean(grad_hat, -1, keepdims=True)
        - standard * jnp.mean(grad_hat * standard, -1, keepdims=True)
    )
    row_sum = lambda value: jnp.sum(value, 0, keepdims=True)
    with_standard = row_sum(grad_rows * standard)
    sums = [
        row_sum(grad_rows),
        with_standard * gain,
        row_sum(upstream * branch),
        with_standard * (1.0 + scaling),
    ]
    slot, rows = place
    if keep is None:
        sums.append(jnp.zeros_like(sums[0]))
        leaving[slot, rows, :] = grad_stream.astype(BF16)
    else:
        kept = jnp.where(keep, grad_stream, 0.0)
        sums.append(row_sum(grad_stream - kept))
        leaving[slot, rows, :] = kept.astype(BF16)
    sums = jnp.concatenate(sums + [jnp.zeros((3, sums[0].shape[1]), F32)], 0)
    if start:
        sums_ref[micro] = sums
    else:
        sums_ref[micro] += sums


def pipeline(enter, cot, wide, second, mods, gain, keep, bias_column, bias_row, out_bias, cosine, sine):
    micros, half, features = enter.shape
    length = 2 * half
    width = features // 2
    hidden = wide.shape[0]
    anywhere = pl.BlockSpec(memory_space=pl.ANY)
    inside = pl.BlockSpec(memory_space=pltpu.VMEM)
    seqs = micros // 2
    dma = pltpu.SemaphoreType.DMA
    rows = (micros, half, features)
    return pl.pallas_call(
        pipeline_kernel,
        in_specs=[anywhere] * 4 + [inside] * 8,
        out_specs=[anywhere] * 7 + [inside],
        out_shape=(
            shape((seqs, length, features), BF16),
            shape((seqs, length, features), BF16),
            shape((micros, half, hidden), BF16),
            shape((micros, half, hidden), BF16),
            shape(rows, BF16),
            shape((micros, half, hidden), BF16),
            shape((micros, half, hidden), BF16),
            shape((micros, 8, features), F32),
        ),
        scratch_shapes=[
            pltpu.VMEM((hidden, features), BF16),
            pltpu.VMEM(rows, BF16),
            pltpu.VMEM(rows, BF16),
            pltpu.VMEM(rows, BF16),
            pltpu.VMEM(rows, BF16),
            pltpu.VMEM((micros, half, width), BF16),
            pltpu.VMEM((2, half, hidden), BF16),
            pltpu.VMEM((half, hidden), BF16),
            pltpu.VMEM(rows, BF16),
            pltpu.VMEM((2, half, features), BF16),
            pltpu.VMEM((half, width), BF16),
            pltpu.VMEM((half, width), BF16),
            pltpu.VMEM((half, features), BF16),
            pltpu.VMEM((half, features), F32),
            pltpu.VMEM((micros, 8, length), F32),
            dma((1 + hidden // half,)),
            dma((2, CHUNKS)),
            dma((micros, CHUNKS)),
            dma((micros, CHUNKS)),
            dma((4,)),
            dma((4, micros)),
            dma((2,)),
            dma((2, seqs)),
            dma((3,)),
            dma((1 + micros,)),
        ],
        compiler_params=params(collective_id=0, has_side_effects=True),
        name="pipeline",
    )(enter, cot, wide, second, mods, gain, keep, bias_column, bias_row, out_bias, cosine, sine)


def rope_tables(length, core):
    half = length // 2
    place = lax.broadcasted_iota(jnp.int32, (HALF, length), 1)
    position = jnp.where(place < half, place + core * half, place - core * half).astype(F32)
    column = lax.broadcasted_iota(F32, (HALF, length), 0)
    angles = position * jnp.exp(column * (-2.0 * math.log(10000.0) / HEAD))
    return jnp.cos(angles), jnp.sin(angles)


def shards(
    tokens, span_start, span_length, time_step, time_table, mask_embed, mod_weight, mod_bias,
    norm_gain, in_weight, in_bias, out_weight, out_bias, cotangent,
):
    section = lax.axis_index("section")
    sections = lax.axis_size("section")
    dp_index = lax.axis_index("dp")
    dp_count = lax.axis_size("dp")
    core = dp_index % 2
    seqs, length, features = tokens.shape
    half = length // 2
    micro_count = 2 * seqs
    hidden = in_weight.shape[2]
    width = features // 2
    first = in_weight[0]
    second = out_weight[0]
    gain = norm_gain
    is_first = section == 0

    def flat(dp, sec):
        return dp * sections + sec

    def swap_cores(value, active):
        return lax.ppermute(
            value, AXES, [(flat(d, s), flat(d ^ 1, s)) for d in range(dp_count) for s in active]
        )

    every = list(range(sections))

    def by_owner(mine, theirs, count):
        out = []
        for i in range(count):
            out.append(jnp.where(core == 0, mine[i], theirs[i]))
            out.append(jnp.where(core == 0, theirs[i], mine[i]))
        return out

    position = lax.broadcasted_iota(jnp.int32, (seqs, length), 1)
    in_span = (position >= span_start[:, None]) & (position < (span_start + span_length)[:, None])
    start_rows = jnp.where(in_span[:, :, None], mask_embed[None, None, :], tokens)
    span_rows = in_span.astype(F32)

    def halves(array, axis):
        own = lax.dynamic_slice_in_dim(array, core * half, half, axis)
        other = lax.dynamic_slice_in_dim(array, (1 - core) * half, half, axis)
        return own, other

    step_onehot = (
        time_step[:, None] == lax.broadcasted_iota(jnp.int32, (seqs, time_table.shape[0]), 1)
    ).astype(F32)
    embedded = jnp.dot(step_onehot, time_table, precision=HIGH)
    conditions = jax.nn.silu(embedded)
    modulations = jnp.dot(conditions, mod_weight[0], precision=HIGH) + mod_bias[0]
    modulations = modulations.reshape(seqs, 3, features)
    span_own, span_other = halves(span_rows, 1)
    token_own, token_other = halves(start_rows, 1)
    cot_own, cot_other = halves(cotangent, 1)
    mods = by_owner(modulations, swap_cores(modulations, every), seqs)
    spans = by_owner(span_own, swap_cores(span_other, [0]), seqs)
    enter_rows = by_owner(
        token_own, [swap_cores(token_other[i], [0]) for i in range(seqs)], seqs
    )
    cot_rows = by_owner(cot_own, swap_cores(cot_other, [sections - 1]), seqs)

    cosine, sine = rope_tables(length, core)

    def head_columns(block, which):
        begin = block * features + which * width
        return lax.dynamic_slice_in_dim(first, begin, width, 1)

    weight_heads = jnp.concatenate([head_columns(block, core) for block in range(3)], 1).T
    bias_heads = jnp.concatenate(
        [lax.dynamic_slice_in_dim(in_bias[0], block * features + core * width, width, 0) for block in range(3)]
    )
    bias_heads = jnp.broadcast_to(bias_heads[:, None], (3 * width, 128))
    out_matrix = first[:, 3 * features :]
    out_own = lax.dynamic_slice_in_dim(out_matrix, core * width, width, 0)
    out_other = lax.dynamic_slice_in_dim(out_matrix, (1 - core) * width, width, 0)
    out_pair = jnp.concatenate([out_own, out_other], 0)
    out_row = in_bias[:, 3 * features :]

    keep = jnp.where(is_first, 1.0 - jnp.stack(spans), 1.0)[:, :, None]
    mods_rows = jnp.concatenate(
        [jnp.stack(mods), jnp.zeros((micro_count, 5, features), F32)], 1
    ).reshape(micro_count * 8, features)
    wide = lax.cond(
        section % 2 == 0,
        lambda: jnp.concatenate(
            [weight_heads, out_pair, jnp.zeros((hidden - 3 * width - 2 * width, features), BF16)], 0
        ),
        lambda: first.T,
    )
    states, stream, kept_first, kept_second, kept_rows, back_first, back_second, sums = pipeline(
        jnp.stack(enter_rows), jnp.stack(cot_rows), wide, second, mods_rows, gain, keep, bias_heads, in_bias,
        out_bias, cosine, sine,
    )
    states = states[None]
    stream = stream[None]

    mid = hidden // 2

    def attention_grads():
        rows = kept_second[:, :, : 2 * features].reshape(micro_count, half, 2, features)
        rows = rows.transpose(0, 2, 1, 3).reshape(micro_count * length, features)
        mixed = kept_first[:, width:].reshape(micro_count, half - width, 3, length)
        mixed = mixed.transpose(2, 1, 0, 3).reshape(width, micro_count * length)
        grad_branch = back_second[:, :, : 2 * features].reshape(micro_count, half, 2, features)
        grad_branch = grad_branch.transpose(0, 2, 1, 3).reshape(micro_count * length, features)
        grad_proj = back_first[:, :width].reshape(micro_count, width, 3, length)
        grad_proj = grad_proj.transpose(2, 1, 0, 3).reshape(3 * width, micro_count * length)
        own = jnp.concatenate([dot_nn(grad_proj, rows), dot_nn(mixed, grad_branch)], 0)
        zeros = jnp.zeros((mid, features), F32)
        bias_in = jnp.sum(grad_proj.astype(F32), 1).reshape(3, width)
        bias_out = jnp.sum(grad_branch.astype(F32).reshape(micro_count, 2, half, features)[:, 0], (0, 1))
        low = jnp.where(core == 0, bias_in, 0.0)
        high = jnp.where(core == 0, 0.0, bias_in)
        bias = jnp.concatenate([jnp.concatenate([low, high], 1).reshape(3 * features), bias_out])
        low_zeros = jnp.zeros((mid, features), BF16)
        return own, zeros, low_zeros, low_zeros, bias, jnp.zeros((features,), F32)

    def transposed_dot(left, right):
        return lax.dot_general(left, right, (((0,), (0,)), ((), ())), preferred_element_type=F32)

    def feed_grads():
        rows = kept_rows.reshape(micro_count * half, features)
        active = kept_second.reshape(micro_count * half, hidden)
        grad_branch = back_second[:, :, :features].reshape(micro_count * half, features)
        grad_hidden = back_first.reshape(micro_count * half, hidden)
        grad_first = transposed_dot(grad_hidden, rows)
        grad_second = transposed_dot(active, grad_branch)
        pick_half = lambda array, which: lax.dynamic_slice_in_dim(array, which * mid, mid, 0)
        return (
            pick_half(grad_first, core),
            pick_half(grad_second, core),
            pick_half(grad_first, 1 - core).astype(BF16),
            pick_half(grad_second, 1 - core).astype(BF16),
            jnp.sum(grad_hidden.astype(F32), 0),
            jnp.sum(grad_branch.astype(F32), 0),
        )

    own_first, own_second, send_first, send_second, bias_first, bias_second = lax.cond(
        section % 2 == 0, attention_grads, feed_grads
    )
    odd = [s for s in every if s % 2 == 1]
    own_first = own_first + swap_cores(send_first, odd).astype(F32)
    own_second = own_second + swap_cores(send_second, odd).astype(F32)

    bits = dp_count.bit_length() - 1
    chip_bits = list(range(1, bits))

    def swap_bit(value, bit, active):
        return lax.ppermute(
            value, AXES, [(flat(d, s), flat(d ^ (1 << bit), s)) for d in range(dp_count) for s in active]
        )

    def sum_over_chips(total, active):
        columns = total.shape[1] // 2
        results = []
        for part, order in enumerate((chip_bits, chip_bits[::-1])):
            piece = total[:, part * columns : (part + 1) * columns]
            for bit in order:
                size = piece.shape[0] // 2
                low = ((dp_index >> bit) & 1) == 0
                keep = jnp.where(low, piece[:size], piece[size:])
                send = jnp.where(low, piece[size:], piece[:size]).astype(BF16)
                piece = keep + swap_bit(send, bit, active).astype(F32)
            piece = piece.astype(BF16)
            for bit in order[::-1]:
                low = ((dp_index >> bit) & 1) == 0
                got = swap_bit(piece, bit, active)
                piece = jnp.where(
                    low, jnp.concatenate([piece, got], 0), jnp.concatenate([got, piece], 0)
                )
            results.append(piece)
        return jnp.concatenate(results, 1)

    sum_first = sum_over_chips(own_first, every)
    sum_second = sum_over_chips(own_second, odd)
    got_first = swap_cores(sum_first, every)
    got_second = swap_cores(sum_second, odd)
    low_first = jnp.where(core == 0, sum_first, got_first)
    high_first = jnp.where(core == 0, got_first, sum_first)
    low_second = jnp.where(core == 0, sum_second, got_second)
    high_second = jnp.where(core == 0, got_second, sum_second)

    def attention_whole():
        columns = []
        for block in range(3):
            for side in (low_first, high_first):
                columns.append(side[block * width : (block + 1) * width].T)
        out_rows = jnp.concatenate([low_first[3 * width :], high_first[3 * width :]], 0)
        return jnp.concatenate(columns + [out_rows], 1).astype(F32), jnp.zeros((hidden, features), F32)

    def feed_whole():
        return (
            jnp.concatenate([low_first, high_first], 0).T.astype(F32),
            jnp.concatenate([low_second, high_second], 0).astype(F32),
        )

    grad_in, grad_out = lax.cond(section % 2 == 0, attention_whole, feed_whole)

    small = jnp.concatenate(
        [sums[:, :3].reshape(-1), jnp.sum(sums[:, 3], 0), jnp.sum(sums[:, 4], 0), bias_first, bias_second]
    )
    packed = jnp.concatenate([small, time_step.astype(F32)])
    gathered = lax.all_gather(packed, "dp")
    pairs = gathered[:, : small.shape[0]].reshape(dp_count // 2, 2, -1).sum(1)
    count = micro_count * 3 * features
    grad_modulation = pairs[:, :count].reshape(dp_count // 2 * micro_count, 3 * features)
    rest = jnp.sum(pairs[:, count:], 0)
    steps_all = gathered[:, small.shape[0] :].astype(jnp.int32)
    steps_all = steps_all.reshape(dp_count // 2, 2, seqs).transpose(0, 2, 1).reshape(-1)
    onehot_all = (
        steps_all[:, None] == lax.broadcasted_iota(jnp.int32, (steps_all.shape[0], time_table.shape[0]), 1)
    ).astype(F32)
    embedded_all = jnp.dot(onehot_all, time_table, precision=HIGH)
    conditions_all, silu_pull = jax.vjp(jax.nn.silu, embedded_all)
    grad_mod_weight = jnp.dot(conditions_all.T, grad_modulation, precision=HIGH)
    grad_mod_bias = jnp.sum(grad_modulation, 0)
    grad_condition = lax.dot_general(
        grad_modulation, mod_weight[0], (((1,), (1,)), ((), ())), precision=HIGH, preferred_element_type=F32
    )
    grad_gain = rest[:features]
    embed_total = jnp.where(is_first, rest[features : 2 * features], 0.0)
    grad_bias_first = rest[2 * features : 2 * features + hidden]
    grad_bias_second = rest[2 * features + hidden :]
    across = lax.psum(jnp.concatenate([grad_condition.reshape(-1), embed_total]), "section")
    grad_condition = across[: grad_condition.size].reshape(grad_condition.shape)
    embed_total = across[grad_condition.size :]
    grad_embedded = silu_pull(grad_condition)[0]
    table_total = lax.dot_general(
        onehot_all, grad_embedded, (((0,), (0,)), ((), ())), precision=HIGH, preferred_element_type=F32
    )
    return (
        states,
        stream,
        table_total,
        embed_total,
        grad_mod_weight[None],
        grad_mod_bias[None],
        grad_gain[None],
        grad_in[None],
        grad_bias_first[None],
        grad_out[None],
        grad_bias_second[None],
    )


def solution(mesh):
    placed = (
        P("dp", None, None),
        P("dp"),
        P("dp"),
        P("dp"),
        P(),
        P(),
        P("section", None, None),
        P("section", None),
        P("section", None),
        P("section", None, None),
        P("section", None),
        P("section", None, None),
        P("section", None),
        P("dp", None, None),
    )
    return jax.shard_map(
        shards,
        mesh=mesh,
        in_specs=placed,
        out_specs=(
            P("section", "dp", None, None),
            P("section", "dp", None, None),
            P(),
            P(),
            P("section", None, None),
            P("section", None),
            P("section", None),
            P("section", None, None),
            P("section", None),
            P("section", None, None),
            P("section", None),
        ),
        check_vma=False,
    )
```

```python
from functools import partial
import math

import jax
import jax.numpy as jnp
from jax import lax
from jax.experimental import pallas as pl
from jax.experimental.pallas import tpu as pltpu
from jax.sharding import PartitionSpec as P

HEAD = 64
HALF = HEAD // 2
EPS = 1e-06
HIGH = lax.Precision.HIGHEST
F32 = jnp.float32
BF16 = jnp.bfloat16
SCALE = HEAD ** (-0.5)
EXP2_SCALE = SCALE * math.log2(math.e)
GELU_C = math.sqrt(2.0 / math.pi)
VMEM_LIMIT = 56 << 20
AXES = ("dp", "section")


def dot_nn(left, right):
    return jnp.dot(left, right, preferred_element_type=F32)


def dot_nt(left, right):
    return lax.dot_general(left, right, (((1,), (1,)), ((), ())), preferred_element_type=F32)


def params(**more):
    return pltpu.CompilerParams(vmem_limit_bytes=VMEM_LIMIT, **more)


def shape(dims, dtype):
    return jax.ShapeDtypeStruct(dims, dtype)


def normalize(rows):
    average = jnp.mean(rows, -1, keepdims=True)
    centered = rows - average
    inverse_std = lax.rsqrt(jnp.mean(centered * centered, -1, keepdims=True) + EPS)
    return centered * inverse_std, inverse_std


MESH = pl.DeviceIdType.MESH
CHUNKS = 2


def pipeline_kernel(
    enter_ref, cot_ref, wide_ref, second_ref, mods_ref, gain_ref, keep_ref, bias_column_ref, bias_row_ref,
    out_bias_ref, cos_ref, sin_ref,
    states_ref, stream_ref, kept_first, kept_second, kept_rows, back_first, back_second, sums_ref, bias_ref,
    weights, streams, others, upstreams, up_others, mixed_got, first_buf, second_buf, branches, leaving,
    mixed_own, mixed_send, grad_send, grad_own, lse_ref, bias_columns,
    load_sem, pass_send, pass_recv, back_recv, swap_send, swap_recv, place_send, place_recv, store_sem, fetch_sem,
):
    section = lax.axis_index("section")
    sections = lax.axis_size("section")
    dp_index = lax.axis_index("dp")
    core = lax.rem(dp_index, 2)
    partner = dp_index + 1 - 2 * core
    micros, half, features = streams.shape
    width = mixed_own.shape[1]
    heads = width // HEAD
    length = 2 * half
    part_rows = half // CHUNKS
    attends = lax.rem(section, 2) == 0
    feeds = lax.rem(section, 2) == 1
    is_first = section == 0
    is_last = section == sections - 1
    hidden = wide_ref.shape[0]
    feed_step = half
    feed_parts = hidden // feed_step

    barrier = pltpu.get_barrier_semaphore()
    pl.semaphore_signal(barrier, inc=1, device_id=(partner, section), device_id_type=MESH)

    @pl.when(section > 0)
    def _():
        pl.semaphore_signal(barrier, inc=1, device_id=(dp_index, section - 1), device_id_type=MESH)

    @pl.when(section < sections - 1)
    def _():
        pl.semaphore_signal(barrier, inc=1, device_id=(dp_index, section + 1), device_id_type=MESH)

    def load_wide():
        return pltpu.make_async_copy(wide_ref, weights, load_sem.at[0])

    def second_at(part):
        return others.at[part] if part < micros else up_others.at[part - micros]

    def load_second(part):
        return pltpu.make_async_copy(
            second_ref.at[pl.ds(part * feed_step, feed_step)], second_at(part), load_sem.at[1 + part]
        )

    def load_enter(m):
        return pltpu.make_async_copy(enter_ref.at[m], streams.at[m], fetch_sem.at[1 + m])

    def load_cot(m):
        return pltpu.make_async_copy(cot_ref.at[m], upstreams.at[m], fetch_sem.at[1 + m])

    @pl.when(is_first)
    def _():
        for m in range(micros):
            load_enter(m).start()

    load_wide().start()

    @pl.when(feeds)
    def _():
        for part in range(feed_parts):
            load_second(part).start()

    @pl.when(is_last)
    def _():
        for m in range(micros):
            load_cot(m).start()

    load_wide().wait()

    @pl.when(feeds)
    def _():
        for part in range(feed_parts):
            load_second(part).wait()

    pl.semaphore_wait(
        barrier, 1 + jnp.where(section > 0, 1, 0) + jnp.where(section < sections - 1, 1, 0)
    )

    bias_ref[...] = jnp.zeros_like(bias_ref)
    bias_columns[...] = jnp.zeros_like(bias_columns)

    def rows_of(part):
        return slice(part * part_rows, (part + 1) * part_rows)

    def schedule(step):
        turns = jnp.where(is_last, 1, 0)
        forward = jnp.where(is_last, 1 - lax.rem(step, 2), jnp.where(step < micros, 1, 0))
        micro = jnp.where(is_last, step // 2, lax.rem(step, micros))
        del turns
        return forward == 1, micro

    def pass_on(step, part, micro, forward):
        slot = lax.rem(step, 2)
        source = leaving.at[slot, pl.ds(part * part_rows, part_rows)]
        if forward:
            return pltpu.make_async_remote_copy(
                source, streams.at[micro, pl.ds(part * part_rows, part_rows)],
                pass_send.at[slot, part], pass_recv.at[micro, part],
                device_id=(dp_index, section + 1), device_id_type=MESH,
            )
        return pltpu.make_async_remote_copy(
            source, upstreams.at[micro, pl.ds(part * part_rows, part_rows)],
            pass_send.at[slot, part], back_recv.at[micro, part],
            device_id=(dp_index, section - 1), device_id_type=MESH,
        )

    def place_target(target, micro):
        return target.at[micro // 2, pl.ds(core * half, half)]

    def place_local(step, micro, target):
        slot = lax.rem(step, 2)
        return pltpu.make_async_copy(leaving.at[slot], place_target(target, micro), place_send.at[slot])

    def place_remote(step, micro, target, index):
        slot = lax.rem(step, 2)
        return pltpu.make_async_remote_copy(
            leaving.at[slot], place_target(target, micro), place_send.at[slot],
            place_recv.at[index, micro // 2], device_id=(partner, section), device_id_type=MESH,
        )

    def send_part(step, part, micro, forward):
        reaches = section < sections - 1 if forward else section > 0

        @pl.when(reaches)
        def _():
            pass_on(step, part, micro, forward).start()

    def place_result(step, micro, forward):
        target, index = (states_ref, 0) if forward else (stream_ref, 1)
        mine = lax.rem(micro, 2) == core

        @pl.when(mine)
        def _():
            place_local(step, micro, target).start()

        @pl.when(jnp.logical_not(mine))
        def _():
            place_remote(step, micro, target, index).start()

    def leaving_free(step):
        was_forward, micro = schedule(step)
        mine = lax.rem(micro, 2) == core
        for forward, cond in ((True, was_forward), (False, jnp.logical_not(was_forward))):
            reaches = section < sections - 1 if forward else section > 0
            target, index = (states_ref, 0) if forward else (stream_ref, 1)

            @pl.when(cond & reaches)
            def _():
                for part in range(CHUNKS):
                    pass_on(step, part, micro, forward).wait_send()

            @pl.when(cond & mine)
            def _():
                place_local(step, micro, target).wait()

            @pl.when(cond & jnp.logical_not(mine))
            def _():
                place_remote(step, micro, target, index).wait_send()

    def swap(kind, source, target, micro):
        return pltpu.make_async_remote_copy(
            source, target, swap_send.at[kind], swap_recv.at[kind, micro],
            device_id=(partner, section), device_id_type=MESH,
        )

    def store_out(source, target, which):
        return pltpu.make_async_copy(source, target, store_sem.at[which])

    def stores_done():
        store_out(first_buf.at[0], kept_first.at[0], 0).wait()
        store_out(second_buf, kept_second.at[0], 1).wait()

    def arrive(micro, part, forward):
        local = is_first if forward else is_last

        if part == 0:

            @pl.when(local)
            def _():
                (load_enter if forward else load_cot)(micro).wait()

        @pl.when(jnp.logical_not(local))
        def _():
            pass_on(0, part, micro, forward).wait_recv()

    def attention_forward(step, micro):
        mod = mods_ref[pl.ds(micro * 8, 8), :]
        gain = gain_ref[...]
        slot = lax.rem(micro, 2)
        for part in range(CHUNKS):
            arrive(micro, part, True)
        exchange = swap(0, streams.at[micro], others.at[micro], micro)
        exchange.start()

        @pl.when(step > 0)
        def _():
            stores_done()

        def project(source, part):
            standard, _ = normalize(source[micro, rows_of(part % CHUNKS), :].astype(F32))
            rows = (standard * gain * (1.0 + mod[1:2]) + mod[0:1]).astype(BF16)
            place = (part // CHUNKS) * features
            second_buf[rows_of(part % CHUNKS), place : place + features] = rows
            projected = dot_nt(weights[: 3 * width, :], rows) + bias_column_ref[:, 0:1]
            columns = slice(part * part_rows, (part + 1) * part_rows)
            cosine = cos_ref[:, columns]
            sine = sin_ref[:, columns]
            for block in range(3):
                lanes = slice(block * length + part * part_rows, block * length + (part + 1) * part_rows)
                if block == 2:
                    first_buf[slot, :width, lanes] = projected[2 * width :].astype(BF16)
                    continue
                for head in range(heads):
                    base = block * width + head * HEAD
                    front = projected[base : base + HALF]
                    back = projected[base + HALF : base + HEAD]
                    at = head * HEAD
                    first_buf[slot, at : at + HALF, lanes] = (front * cosine - back * sine).astype(BF16)
                    first_buf[slot, at + HALF : at + HEAD, lanes] = (back * cosine + front * sine).astype(BF16)

        for part in range(CHUNKS):
            project(streams, part)
        exchange.wait_recv()
        for part in range(CHUNKS, 2 * CHUNKS):
            project(others, part)

        def scores_of(head):
            base = pl.multiple_of(head * HEAD, HEAD)
            key_rows = first_buf[slot, pl.ds(base, HEAD), length : 2 * length].T
            return dot_nn(key_rows, first_buf[slot, pl.ds(base, HEAD), :length])

        def finish(head, within, scores):
            base = pl.multiple_of(head * HEAD, HEAD)
            top = jnp.max(scores, 0, keepdims=True) * EXP2_SCALE
            spread = jnp.exp2(scores * EXP2_SCALE - top)
            total = jnp.sum(spread, 0, keepdims=True)
            mixed = dot_nn(first_buf[slot, pl.ds(base, HEAD), 2 * length :], spread.astype(BF16))
            lse_ref[micro, pl.ds(head, 1), :] = top + jnp.log2(total)
            return (mixed * (1.0 / total)).astype(BF16)

        def head_pair(pair, carried):
            scores = scores_of(2 * pair), scores_of(2 * pair + 1)
            mixed = jnp.concatenate([finish(2 * pair + i, i, scores[i]) for i in range(2)], 0)
            at = pl.multiple_of(pair * length, length)
            first_buf[slot, width:, pl.ds(at, length)] = mixed
            turned = mixed.T
            lanes = pl.multiple_of(pair * 2 * HEAD, 2 * HEAD)
            mixed_own[:, pl.ds(lanes, 2 * HEAD)] = turned[:half]
            mixed_send[:, pl.ds(lanes, 2 * HEAD)] = turned[half:]
            return carried

        lax.fori_loop(0, heads // 2, head_pair, 0)
        give = swap(1, mixed_send, mixed_got.at[micro], micro)
        give.start()
        store_out(first_buf.at[slot], kept_first.at[micro], 0).start()
        store_out(second_buf, kept_second.at[micro], 1).start()

        @pl.when(step >= 2)
        def _():
            leaving_free(step - 2)

        give.wait_recv()
        for part in range(CHUNKS):
            rows = rows_of(part)
            branch = (
                dot_nn(mixed_own[rows, :], weights[3 * width : 4 * width, :])
                + dot_nn(mixed_got[micro, rows, :], weights[4 * width : 5 * width, :])
                + bias_row_ref[:, 3 * features :]
            )
            branches[micro, rows, :] = branch.astype(BF16)
            result = streams[micro, rows, :].astype(F32) + mod[2:3] * branch
            leaving[lax.rem(step, 2), rows, :] = result.astype(BF16)
            send_part(step, part, micro, True)
        place_result(step, micro, True)
        exchange.wait_send()
        give.wait_send()

    def feed_forward(step, micro):
        mod = mods_ref[pl.ds(micro * 8, 8), :]
        gain = gain_ref[...]

        @pl.when(step > 0)
        def _():
            stores_done()

        @pl.when(step >= 2)
        def _():
            leaving_free(step - 2)

        row_store = pltpu.make_async_copy(up_others.at[2], kept_rows.at[micro], store_sem.at[2])
        for part in range(CHUNKS):
            rows = rows_of(part)
            arrive(micro, part, True)
            standard, _ = normalize(streams[micro, rows, :].astype(F32))
            entering = (standard * gain * (1.0 + mod[1:2]) + mod[0:1]).astype(BF16)
            up_others[2, rows, :] = entering
            branch = jnp.broadcast_to(out_bias_ref[...], (part_rows, features))
            for piece in range(feed_parts):
                lanes = slice(piece * feed_step, (piece + 1) * feed_step)
                value = dot_nt(entering, weights[lanes, :]) + bias_row_ref[:, lanes]
                square = value * value
                bend = jnp.tanh(GELU_C * value * (1.0 + 0.044715 * square))
                active = (0.5 * value * (1.0 + bend)).astype(BF16)
                second_buf[rows, lanes] = active
                first_buf[0, rows, lanes] = (
                    0.5 * (1.0 + bend)
                    + (0.5 * GELU_C) * value * (1.0 - bend * bend) * (1.0 + (3 * 0.044715) * square)
                ).astype(BF16)
                branch = branch + dot_nn(active, second_at(piece)[...])
            branches[micro, rows, :] = branch.astype(BF16)
            result = streams[micro, rows, :].astype(F32) + mod[2:3] * branch
            leaving[lax.rem(step, 2), rows, :] = result.astype(BF16)
            send_part(step, part, micro, True)
        place_result(step, micro, True)
        store_out(first_buf.at[0], kept_first.at[micro], 0).start()
        store_out(second_buf, kept_second.at[micro], 1).start()
        row_store.start()
        row_store.wait()

    def attention_backward(step, micro):
        mod = mods_ref[pl.ds(micro * 8, 8), :]
        gain = gain_ref[...]
        stores_done()
        fetch = pltpu.make_async_copy(kept_first.at[micro], first_buf.at[0], fetch_sem.at[0])
        fetch.start()
        for part in range(CHUNKS):
            arrive(micro, part, False)
        exchange = swap(2, upstreams.at[micro], up_others.at[micro], micro)
        exchange.start()
        grad_mixed_at = 2 * features

        def into_heads(source, part):
            grad_branch = (mod[2:3] * source[micro, rows_of(part % CHUNKS), :].astype(F32)).astype(BF16)
            place = (part // CHUNKS) * features
            second_buf[rows_of(part % CHUNKS), place : place + features] = grad_branch
            if part < CHUNKS:
                bias_ref[0:1, 3 * features :] += jnp.sum(grad_branch.astype(F32), 0, keepdims=True)
            lanes = slice(grad_mixed_at + part * part_rows, grad_mixed_at + (part + 1) * part_rows)
            second_buf[:width, lanes] = dot_nt(weights[3 * width : 4 * width, :], grad_branch).astype(BF16)

        for part in range(CHUNKS):
            into_heads(upstreams, part)
        exchange.wait_recv()
        for part in range(CHUNKS, 2 * CHUNKS):
            into_heads(up_others, part)
        fetch.wait()
        cosine = cos_ref[...]
        sine = sin_ref[...]

        def turn_back(base, block, gradient):
            front = gradient[:HALF] * SCALE
            back = gradient[HALF:] * SCALE
            turned = jnp.concatenate([front * cosine + back * sine, back * cosine - front * sine], 0)
            put_back(base, block, turned.astype(BF16))

        def put_back(base, block, gradient):
            first_buf[1, pl.ds(base, HEAD), block * length : (block + 1) * length] = gradient
            bias_columns[block, pl.ds(base, HEAD), 0:1] += jnp.sum(gradient.astype(F32), 1, keepdims=True)

        def one_head(head, mixed):
            base = pl.multiple_of(head * HEAD, HEAD)
            query = first_buf[0, pl.ds(base, HEAD), :length]
            key = first_buf[0, pl.ds(base, HEAD), length : 2 * length]
            value = first_buf[0, pl.ds(base, HEAD), 2 * length :]
            grad_mixed = second_buf[pl.ds(base, HEAD), grad_mixed_at : grad_mixed_at + length]
            delta = jnp.sum(grad_mixed.astype(F32) * mixed.astype(F32), 0, keepdims=True)
            scores = dot_nn(key.T, query)
            spread = jnp.exp2(scores * EXP2_SCALE - lse_ref[micro, pl.ds(head, 1), :])
            grad_spread = dot_nn(value.T, grad_mixed)
            grad_scores = (spread * (grad_spread - delta)).astype(BF16)
            grad_value = dot_nn(spread.astype(BF16), grad_mixed.T)
            grad_key = dot_nn(grad_scores, query.T)
            grad_query = dot_nn(key, grad_scores)
            turn_back(base, 0, grad_query)
            turn_back(base, 1, grad_key.T)
            put_back(base, 2, grad_value.T.astype(BF16))

        def head_pair(pair, carried):
            at = pl.multiple_of(pair * length, length)
            mixed = first_buf[0, width:, pl.ds(at, length)]
            one_head(2 * pair, mixed[:HEAD])
            one_head(2 * pair + 1, mixed[HEAD:])
            return carried

        lax.fori_loop(0, heads // 2, head_pair, 0)

        def grad_rows_of(part):
            total = None
            for block in range(3):
                lanes = slice(block * length + part * part_rows, block * length + (part + 1) * part_rows)
                term = dot_nn(first_buf[1, :width, lanes].T, weights[block * width : (block + 1) * width, :])
                total = term if total is None else total + term
            return total

        for part in range(CHUNKS, 2 * CHUNKS):
            grad_send[rows_of(part - CHUNKS), :] = grad_rows_of(part).astype(BF16)
        give = swap(3, grad_send, others.at[micro], micro)
        give.start()
        store_out(first_buf.at[1], back_first.at[micro], 0).start()
        store_out(second_buf, back_second.at[micro], 1).start()
        for part in range(CHUNKS):
            grad_own[rows_of(part), :] = grad_rows_of(part)
        leaving_free(step - 2)
        give.wait_recv()
        for part in range(CHUNKS):
            rows = rows_of(part)
            finish_back(
                grad_own[rows, :] + others[micro, rows, :].astype(F32),
                streams[micro, rows, :].astype(F32),
                upstreams[micro, rows, :].astype(F32),
                branches[micro, rows, :].astype(F32),
                mod, gain, keep_ref[micro, rows, :] > 0.5,
                leaving, (lax.rem(step, 2), rows), sums_ref, micro, part == 0,
            )
            send_part(step, part, micro, False)
        place_result(step, micro, False)
        exchange.wait_send()
        give.wait_send()

    def feed_backward(step, micro):
        mod = mods_ref[pl.ds(micro * 8, 8), :]
        gain = gain_ref[...]
        stores_done()
        fetch = pltpu.make_async_copy(kept_first.at[micro], first_buf.at[0], fetch_sem.at[0])
        fetch.start()

        @pl.when(step >= 2)
        def _():
            leaving_free(step - 2)

        fetch.wait()
        for part in range(CHUNKS):
            rows = rows_of(part)
            arrive(micro, part, False)
            upstream = upstreams[micro, rows, :].astype(F32)
            grad_branch = (mod[2:3] * upstream).astype(BF16)
            second_buf[rows, :features] = grad_branch
            bias_ref[1:2, :features] += jnp.sum(grad_branch.astype(F32), 0, keepdims=True)
            total = jnp.zeros((part_rows, features), F32)
            for piece in range(feed_parts):
                lanes = slice(piece * feed_step, (piece + 1) * feed_step)
                grad_active = dot_nt(grad_branch, second_at(piece)[...])
                grad_hidden = (grad_active * first_buf[0, rows, lanes].astype(F32)).astype(BF16)
                first_buf[1, rows, lanes] = grad_hidden
                bias_ref[0:1, lanes] += jnp.sum(grad_hidden.astype(F32), 0, keepdims=True)
                total = total + dot_nn(grad_hidden, weights[lanes, :])
            finish_back(
                total,
                streams[micro, rows, :].astype(F32),
                upstream,
                branches[micro, rows, :].astype(F32),
                mod, gain, None,
                leaving, (lax.rem(step, 2), rows), sums_ref, micro, part == 0,
            )
            send_part(step, part, micro, False)
        place_result(step, micro, False)
        store_out(first_buf.at[1], back_first.at[micro], 0).start()
        store_out(second_buf, back_second.at[micro], 1).start()

    def one_step(step, carried):
        forward, micro = schedule(step)
        backward = jnp.logical_not(forward)

        @pl.when(attends & forward)
        def _():
            attention_forward(step, micro)

        @pl.when(attends & backward)
        def _():
            attention_backward(step, micro)

        @pl.when(feeds & forward)
        def _():
            feed_forward(step, micro)

        @pl.when(feeds & backward)
        def _():
            feed_backward(step, micro)

        return carried

    lax.fori_loop(0, 2 * micros, one_step, 0)

    @pl.when(attends)
    def _():
        for block in range(3):
            at = pl.multiple_of(block * features + core * width, 128)
            bias_ref[0:1, pl.ds(at, width)] = bias_columns[block].T[0:1]

    stores_done()
    leaving_free(2 * micros - 2)
    leaving_free(2 * micros - 1)
    for index, target in enumerate((states_ref, stream_ref)):
        for slot in range(micros // 2):
            pltpu.make_async_remote_copy(
                leaving.at[0], target.at[slot, pl.ds((1 - core) * half, half)], place_send.at[0],
                place_recv.at[index, slot], device_id=(partner, section), device_id_type=MESH,
            ).wait_recv()


def finish_back(
    grad_rows, stream, upstream, branch, mod, gain, keep, leaving, place, sums_ref, micro, start,
):
    standard, inverse_std = normalize(stream)
    scaling = mod[1:2, :]
    grad_normed = grad_rows * (1.0 + scaling)
    grad_hat = grad_normed * gain
    grad_stream = upstream + inverse_std * (
        grad_hat
        - jnp.mean(grad_hat, -1, keepdims=True)
        - standard * jnp.mean(grad_hat * standard, -1, keepdims=True)
    )
    row_sum = lambda value: jnp.sum(value, 0, keepdims=True)
    with_standard = row_sum(grad_rows * standard)
    sums = [
        row_sum(grad_rows),
        with_standard * gain,
        row_sum(upstream * branch),
        with_standard * (1.0 + scaling),
    ]
    slot, rows = place
    if keep is None:
        sums.append(jnp.zeros_like(sums[0]))
        leaving[slot, rows, :] = grad_stream.astype(BF16)
    else:
        kept = jnp.where(keep, grad_stream, 0.0)
        sums.append(row_sum(grad_stream - kept))
        leaving[slot, rows, :] = kept.astype(BF16)
    sums = jnp.concatenate(sums + [jnp.zeros((3, sums[0].shape[1]), F32)], 0)
    if start:
        sums_ref[micro] = sums
    else:
        sums_ref[micro] += sums


def pipeline(enter, cot, wide, second, mods, gain, keep, bias_column, bias_row, out_bias, cosine, sine):
    micros, half, features = enter.shape
    length = 2 * half
    width = features // 2
    hidden = wide.shape[0]
    anywhere = pl.BlockSpec(memory_space=pl.ANY)
    inside = pl.BlockSpec(memory_space=pltpu.VMEM)
    seqs = micros // 2
    dma = pltpu.SemaphoreType.DMA
    rows = (micros, half, features)
    return pl.pallas_call(
        pipeline_kernel,
        in_specs=[anywhere] * 4 + [inside] * 8,
        out_specs=[anywhere] * 7 + [inside] * 2,
        out_shape=(
            shape((seqs, length, features), BF16),
            shape((seqs, length, features), BF16),
            shape((micros, half, hidden), BF16),
            shape((micros, half, hidden), BF16),
            shape(rows, BF16),
            shape((micros, half, hidden), BF16),
            shape((micros, half, hidden), BF16),
            shape((micros, 8, features), F32),
            shape((8, hidden), F32),
        ),
        scratch_shapes=[
            pltpu.VMEM((hidden, features), BF16),
            pltpu.VMEM(rows, BF16),
            pltpu.VMEM(rows, BF16),
            pltpu.VMEM(rows, BF16),
            pltpu.VMEM(rows, BF16),
            pltpu.VMEM((micros, half, width), BF16),
            pltpu.VMEM((2, half, hidden), BF16),
            pltpu.VMEM((half, hidden), BF16),
            pltpu.VMEM(rows, BF16),
            pltpu.VMEM((2, half, features), BF16),
            pltpu.VMEM((half, width), BF16),
            pltpu.VMEM((half, width), BF16),
            pltpu.VMEM((half, features), BF16),
            pltpu.VMEM((half, features), F32),
            pltpu.VMEM((micros, 8, length), F32),
            pltpu.VMEM((3, width, 128), F32),
            dma((1 + hidden // half,)),
            dma((2, CHUNKS)),
            dma((micros, CHUNKS)),
            dma((micros, CHUNKS)),
            dma((4,)),
            dma((4, micros)),
            dma((2,)),
            dma((2, seqs)),
            dma((3,)),
            dma((1 + micros,)),
        ],
        compiler_params=params(collective_id=0, has_side_effects=True),
        name="pipeline",
    )(enter, cot, wide, second, mods, gain, keep, bias_column, bias_row, out_bias, cosine, sine)


SMALL_ROWS = 24


def gradient_kernel(
    kept_first, kept_second, kept_rows, back_first, back_second, sums_ref, bias_ref, mod_weight_ref,
    summed_first, summed_second, small_ref,
    wide_a, wide_b, deep_a, deep_b, total_a, total_b, give, got, scatter_send, scatter_got, entry,
    load_sem, pair_send, pair_recv, step_send, step_recv, gather_send, gather_recv, core_send, core_recv,
    small_send, small_recv,
):
    section = lax.axis_index("section")
    dp_index = lax.axis_index("dp")
    dp_count = small_ref.shape[0]
    core = lax.rem(dp_index, 2)
    partner = dp_index + 1 - 2 * core
    attends = lax.rem(section, 2) == 0
    feeds = lax.rem(section, 2) == 1
    micros, half, hidden = back_first.shape
    features = kept_rows.shape[2]
    width = features // 2
    length = 2 * half
    mid = hidden // 2
    columns = features // 2
    small_bits = dp_count.bit_length() - 1
    bits = small_bits - 1

    def bit_of(place):
        return lax.rem(dp_index // (1 << place), 2)

    def across(place):
        return dp_index + (1 - 2 * bit_of(place)) * (1 << place)

    barrier = pltpu.get_barrier_semaphore()
    for place in range(small_bits):
        pl.semaphore_signal(barrier, inc=1, device_id=(across(place), section), device_id_type=MESH)

    def small_entry():
        rows = [sums_ref[m, k : k + 1, :] for m in range(micros) for k in range(3)]
        gain = sum(sums_ref[m, 3:4, :] for m in range(micros))
        embed = sum(sums_ref[m, 4:5, :] for m in range(micros))
        rows.append(gain)
        rows += [bias_ref[0:1, k * features : (k + 1) * features] for k in range(hidden // features)]
        rows.append(bias_ref[1:2, :features])
        condition = []
        for m in range(micros):
            total = None
            for k in range(3):
                term = lax.dot_general(
                    jnp.broadcast_to(sums_ref[m, k : k + 1, :], (8, features)),
                    mod_weight_ref[:, k * features : (k + 1) * features],
                    (((1,), (1,)), ((), ())), precision=HIGH, preferred_element_type=F32,
                )
                total = term if total is None else total + term
            condition.append(total[0:1])
        condition.append(jnp.zeros((1, features - micros * mod_weight_ref.shape[0]), F32))
        rows.append(jnp.concatenate(condition, 1))
        rows.append(embed)
        rows.append(jnp.zeros((SMALL_ROWS - len(rows), features), F32))
        entry[...] = jnp.concatenate(rows, 0)
        small_ref[pl.ds(dp_index, 1)] = entry[...][None]

    def small_copy(step):
        size = 1 << step
        start = (dp_index // size) * size
        block = small_ref.at[pl.ds(start, size)]
        return pltpu.make_async_remote_copy(
            block, block, small_send.at[step], small_recv.at[step],
            device_id=(across(step), section), device_id_type=MESH,
        )

    def small_wait(step):
        size = 1 << step
        start = (dp_index // size) * size + (1 - 2 * bit_of(step)) * size
        block = small_ref.at[pl.ds(start, size)]
        pltpu.make_async_remote_copy(
            block, block, small_send.at[step], small_recv.at[step],
            device_id=(across(step), section), device_id_type=MESH,
        ).wait_recv()
        small_copy(step).wait_send()

    def loads(pairs, first_sem):
        return [
            pltpu.make_async_copy(source, target, load_sem.at[first_sem + i])
            for i, (source, target) in enumerate(pairs)
        ]

    def spans(m):
        return slice(m * half, (m + 1) * half)

    def heads_rows(source, target, first_sem):
        return loads(
            [(source.at[m, :, pl.ds(0, 2 * features)], target.at[spans(m), :]) for m in range(micros)], first_sem
        )

    def heads_columns(block, target, first_sem):
        pairs = []
        for m in range(micros):
            for side in range(2):
                at = side * half
                if block < 3:
                    source = back_first.at[m, pl.ds(0, width), pl.ds(block * length + at, half)]
                    pairs.append((source, target.at[pl.ds(side * width, width), spans(m)]))
                    continue
                for pair in range(3):
                    rows = width // 3
                    source = kept_first.at[m, pl.ds(width, rows), pl.ds(pair * length + at, half)]
                    pairs.append((source, target.at[pl.ds(side * width + pair * rows, rows), spans(m)]))
        return loads(pairs, first_sem)

    def half_columns(source, which, target, first_sem):
        return loads(
            [(source.at[m, :, pl.ds(which * mid, mid)], target.at[spans(m), :]) for m in range(micros)], first_sem
        )

    totals = (total_a, total_b)
    outputs = (summed_first, summed_second)

    def place_order(part):
        order = list(range(1, bits + 1))
        return order if part == 0 else order[::-1]

    def window(part, steps):
        size = mid
        start = 0
        for place in place_order(part)[:steps]:
            size = size // 2
            start = start + bit_of(place) * size
        return start, size

    def lanes(part):
        return pl.ds(part * columns, columns)

    def step_copy(payload, part, step):
        place = place_order(part)[step]
        size = mid >> (step + 1)
        return pltpu.make_async_remote_copy(
            scatter_send.at[payload, part, pl.ds(mid - (mid >> step), size)],
            scatter_got.at[payload, part, pl.ds(mid - (mid >> step), size)],
            step_send.at[payload, part, step], step_recv.at[payload, part, step],
            device_id=(across(place), section), device_id_type=MESH,
        )

    def scatter_start(payload, part, step):
        place = place_order(part)[step]
        start, _ = window(part, step)
        size = mid >> (step + 1)
        away = pl.multiple_of(start + (1 - bit_of(place)) * size, 16)
        scatter_send[payload, part, pl.ds(mid - (mid >> step), size), :] = totals[payload][
            pl.ds(away, size), part * columns : (part + 1) * columns
        ].astype(BF16)
        step_copy(payload, part, step).start()

    def scatter_finish(payload, part, step):
        step_copy(payload, part, step).wait()
        start, size = window(part, step + 1)
        rows = pl.ds(pl.multiple_of(start, 16), size)
        cut = slice(part * columns, (part + 1) * columns)
        value = totals[payload][rows, cut] + scatter_got[payload, part, pl.ds(mid - (mid >> step), size), :].astype(F32)
        if step < bits - 1:
            totals[payload][rows, cut] = value
        else:
            outputs[payload][core, rows, cut] = value.astype(BF16)

    def gather_copy(payload, part, step, theirs):
        place = place_order(part)[step]
        start, size = window(part, step + 1)
        if theirs:
            start = start + (1 - 2 * bit_of(place)) * size
        block = outputs[payload].at[core, pl.ds(pl.multiple_of(start, 16), size), lanes(part)]
        return pltpu.make_async_remote_copy(
            block, block, gather_send.at[payload, part, step], gather_recv.at[payload, part, step],
            device_id=(across(place), section), device_id_type=MESH,
        )

    def core_copy(payload, part, step, other):
        if step == bits:
            start, size = window(part, bits)
        else:
            place = place_order(part)[step]
            start, size = window(part, step + 1)
            start = start + (1 - 2 * bit_of(place)) * size
        side = 1 - core if other else core
        block = outputs[payload].at[side, pl.ds(pl.multiple_of(start, 16), size), lanes(part)]
        return pltpu.make_async_remote_copy(
            block, block, core_send.at[payload, part, step], core_recv.at[payload, part, step],
            device_id=(partner, section), device_id_type=MESH,
        )

    def tick(payload, number):
        for part in range(2):
            if number <= bits:
                if number > 0:
                    scatter_finish(payload, part, number - 1)
                if number < bits:
                    scatter_start(payload, part, number)
                else:
                    core_copy(payload, part, bits, False).start()
                    gather_copy(payload, part, bits - 1, False).start()
            else:
                step = 2 * bits - number
                gather_copy(payload, part, step, True).wait_recv()
                core_copy(payload, part, step, False).start()
                if step > 0:
                    gather_copy(payload, part, step - 1, False).start()

    last_tick = 2 * bits

    def wind_up(payload):
        for part in range(2):
            for step in range(bits):
                gather_copy(payload, part, step, False).wait_send()
            for step in range(bits + 1):
                core_copy(payload, part, step, False).wait_send()
                core_copy(payload, part, step, True).wait_recv()

    @pl.when(attends)
    def _():
        rows = heads_rows(kept_second, wide_a, 0)
        grads = heads_rows(back_second, wide_b, micros)
        buffers = (deep_a, deep_b)
        per = 2 * micros
        blocks = [
            heads_columns(block, buffers[block % 2], 2 * micros + (block % 2) * 3 * per) for block in range(4)
        ]
        for copy in rows + blocks[0] + blocks[1]:
            copy.start()
        small_entry()
        for copy in rows:
            copy.wait()
        for block in range(4):
            for copy in blocks[block]:
                copy.wait()
            source = wide_a if block < 3 else wide_b
            if block == 2:
                for copy in grads:
                    copy.start()
            if block == 3:
                for copy in grads:
                    copy.wait()
            deep = buffers[block % 2]
            total_a[block * width : (block + 1) * width, :] = dot_nn(
                deep[:width, :], source[:, :features]
            ) + dot_nn(deep[width:, :], source[:, features:])
            if block + 2 < 4:
                for copy in blocks[block + 2]:
                    copy.start()

    def transposed_rows(source, first_sem, staged, target):
        copies = loads(
            [(source.at[m, :, pl.ds(0, features)], staged.at[m // 2, pl.ds((m % 2) * half, half)]) for m in range(micros)],
            first_sem,
        )

        def turn():
            for m in range(micros):
                copies[m].wait()
                target[:, m * half : (m + 1) * half] = staged[m // 2, (m % 2) * half : (m % 2 + 1) * half, :].T

        return copies, turn

    def pair_copy(payload):
        return pltpu.make_async_remote_copy(
            give, got.at[payload], pair_send.at[payload], pair_recv.at[payload],
            device_id=(partner, section), device_id_type=MESH,
        )

    pieces = mid // features

    def other_half(deep, wide, payload):
        for piece in range(pieces):
            give[piece * features : (piece + 1) * features, :] = dot_nn(
                deep[...], wide[:, piece * features : (piece + 1) * features]
            ).astype(BF16)

    def own_half(deep, wide, payload):
        for piece in range(pieces):
            totals[payload][piece * features : (piece + 1) * features, :] = dot_nn(
                deep[...], wide[:, piece * features : (piece + 1) * features]
            )

    def add_pair(payload):
        pair_copy(payload).wait()
        totals[payload][...] += got[payload].astype(F32)

    @pl.when(feeds)
    def _():
        far = 1 - core
        first_rows, first_turn = transposed_rows(kept_rows, 0, summed_first, deep_a)
        second_rows = transposed_rows(back_second, micros, summed_second, deep_b)[0]
        first_far = half_columns(back_first, far, wide_a, 2 * micros)
        first_near = half_columns(back_first, core, wide_b, 3 * micros)
        for copy in first_rows + first_far + first_near + second_rows:
            copy.start()
        small_entry()
        first_turn()
        for copy in first_far:
            copy.wait()
        other_half(deep_a, wide_a, 0)

    pl.semaphore_wait(barrier, small_bits)
    small_copy(0).start()

    @pl.when(feeds)
    def _():
        far = 1 - core
        first_near = half_columns(back_first, core, wide_b, 3 * micros)
        second_far = half_columns(kept_second, far, wide_a, 4 * micros)
        second_near = half_columns(kept_second, core, wide_b, 5 * micros)
        second_turn = transposed_rows(back_second, micros, summed_second, deep_b)[1]
        pair_copy(0).start()
        for copy in second_far:
            copy.start()
        for copy in first_near:
            copy.wait()
        own_half(deep_a, wide_b, 0)
        for copy in second_near:
            copy.start()
        second_turn()
        add_pair(0)

    tick(0, 0)

    @pl.when(feeds)
    def _():
        far = 1 - core
        second_far = half_columns(kept_second, far, wide_a, 4 * micros)
        second_near = half_columns(kept_second, core, wide_b, 5 * micros)
        for copy in second_far:
            copy.wait()
        other_half(deep_b, wide_a, 1)
        pair_copy(1).start()
        for copy in second_near:
            copy.wait()
        own_half(deep_b, wide_b, 1)
        add_pair(1)

    for number in range(last_tick + 2):
        if number + 1 <= last_tick:
            tick(0, number + 1)
        if number <= last_tick:

            @pl.when(feeds)
            def _():
                tick(1, number)

        if number < small_bits:
            small_wait(number)
            if number + 1 < small_bits:
                small_copy(number + 1).start()
    for number in range(last_tick + 2, small_bits):
        small_wait(number)
        if number + 1 < small_bits:
            small_copy(number + 1).start()
    wind_up(0)

    @pl.when(feeds)
    def _():
        wind_up(1)


def summed_gradients(kept_first, kept_second, kept_rows, back_first, back_second, sums, bias, mod_weight, dp_count):
    micros, half, hidden = back_first.shape
    features = kept_rows.shape[2]
    mid = hidden // 2
    small_bits = dp_count.bit_length() - 1
    bits = small_bits - 1
    anywhere = pl.BlockSpec(memory_space=pl.ANY)
    inside = pl.BlockSpec(memory_space=pltpu.VMEM)
    dma = pltpu.SemaphoreType.DMA
    tokens = micros * half
    return pl.pallas_call(
        gradient_kernel,
        in_specs=[anywhere] * 5 + [inside] * 3,
        out_specs=[inside] * 3,
        out_shape=(
            shape((2, mid, features), BF16),
            shape((2, mid, features), BF16),
            shape((dp_count, SMALL_ROWS, features), F32),
        ),
        scratch_shapes=[
            pltpu.VMEM((tokens, mid), BF16),
            pltpu.VMEM((tokens, mid), BF16),
            pltpu.VMEM((features, tokens), BF16),
            pltpu.VMEM((features, tokens), BF16),
            pltpu.VMEM((mid, features), F32),
            pltpu.VMEM((mid, features), F32),
            pltpu.VMEM((mid, features), BF16),
            pltpu.VMEM((2, mid, features), BF16),
            pltpu.VMEM((2, 2, mid - (mid >> bits), features // 2), BF16),
            pltpu.VMEM((2, 2, mid - (mid >> bits), features // 2), BF16),
            pltpu.VMEM((SMALL_ROWS, features), F32),
            dma((14 * micros,)),
            dma((2,)),
            dma((2,)),
            dma((2, 2, bits)),
            dma((2, 2, bits)),
            dma((2, 2, bits)),
            dma((2, 2, bits)),
            dma((2, 2, bits + 1)),
            dma((2, 2, bits + 1)),
            dma((small_bits,)),
            dma((small_bits,)),
        ],
        compiler_params=pltpu.CompilerParams(vmem_limit_bytes=62 << 20, collective_id=1, has_side_effects=True),
        name="summed_gradients",
    )(kept_first, kept_second, kept_rows, back_first, back_second, sums, bias, mod_weight)


def place_kernel(first_ref, second_ref, small_ref, conditions_ref, grad_in, grad_out, mod_weight_grad, rows_ref):
    step = pl.program_id(0)
    attends = lax.rem(lax.axis_index("section"), 2) == 0
    features = grad_in.shape[0]
    width = features // 2

    for index in range(8):
        block, side = index // 2, index % 2

        @pl.when(attends & (step == index))
        def _():
            if block < 3:
                grad_in[...] = first_ref[side, block * width : (block + 1) * width, :].astype(F32).T
            else:
                for half in range(2):
                    grad_in[half * width : (half + 1) * width, :] = first_ref[
                        half, 3 * width :, side * width : (side + 1) * width
                    ].astype(F32)
            grad_out[...] = jnp.zeros_like(grad_out)

        @pl.when(jnp.logical_not(attends) & (step == index))
        def _():
            owner, piece, cut = index // 4, (index % 4) // 2, index % 2
            rows = slice(piece * features, (piece + 1) * features)
            lanes = slice(cut * width, (cut + 1) * width)
            grad_in[...] = first_ref[owner, rows, lanes].astype(F32)
            grad_out[...] = second_ref[owner, rows, lanes].astype(F32).T

    @pl.when(step == 0)
    def _():
        count = small_ref.shape[0]
        pairs = [small_ref[2 * i] + small_ref[2 * i + 1] for i in range(count // 2)]
        rows_ref[...] = sum(pairs[1:], pairs[0])
        micros = conditions_ref.shape[0] // (count // 2)
        for k in range(3):
            rows = jnp.concatenate([pair[3 * m + k : 3 * m + k + 1] for pair in pairs for m in range(micros)], 0)
            mod_weight_grad[:, k * features : (k + 1) * features] = lax.dot_general(
                conditions_ref[...], rows, (((0,), (0,)), ((), ())), precision=HIGH, preferred_element_type=F32
            )


def place_gradients(first, second, small, conditions, hidden):
    features = first.shape[2]
    width = features // 2
    cond = conditions.shape[1]
    whole = lambda dims: pl.BlockSpec(dims, lambda i: (0,) * len(dims))
    return pl.pallas_call(
        place_kernel,
        grid=(hidden // width,),
        in_specs=[whole(first.shape), whole(second.shape), whole(small.shape), whole(conditions.shape)],
        out_specs=[
            pl.BlockSpec((features, width), lambda i: (0, i)),
            pl.BlockSpec((width, features), lambda i: (i, 0)),
            whole((cond, 3 * features)),
            whole((SMALL_ROWS, features)),
        ],
        out_shape=(
            shape((features, hidden), F32),
            shape((hidden, features), F32),
            shape((cond, 3 * features), F32),
            shape((SMALL_ROWS, features), F32),
        ),
        compiler_params=params(),
        name="place_gradients",
    )(first, second, small, conditions)


def rope_tables(length, core):
    half = length // 2
    place = lax.broadcasted_iota(jnp.int32, (HALF, length), 1)
    position = jnp.where(place < half, place + core * half, place - core * half).astype(F32)
    column = lax.broadcasted_iota(F32, (HALF, length), 0)
    angles = position * jnp.exp(column * (-2.0 * math.log(10000.0) / HEAD))
    return jnp.cos(angles), jnp.sin(angles)


def shards(
    tokens, span_start, span_length, time_step, time_table, mask_embed, mod_weight, mod_bias,
    norm_gain, in_weight, in_bias, out_weight, out_bias, cotangent,
):
    section = lax.axis_index("section")
    sections = lax.axis_size("section")
    dp_index = lax.axis_index("dp")
    dp_count = lax.axis_size("dp")
    core = dp_index % 2
    seqs, length, features = tokens.shape
    half = length // 2
    micro_count = 2 * seqs
    hidden = in_weight.shape[2]
    width = features // 2
    first = in_weight[0]
    second = out_weight[0]
    gain = norm_gain
    is_first = section == 0

    def flat(dp, sec):
        return dp * sections + sec

    def swap_cores(value, active):
        return lax.ppermute(
            value, AXES, [(flat(d, s), flat(d ^ 1, s)) for d in range(dp_count) for s in active]
        )

    every = list(range(sections))

    def by_owner(mine, theirs, count):
        out = []
        for i in range(count):
            out.append(jnp.where(core == 0, mine[i], theirs[i]))
            out.append(jnp.where(core == 0, theirs[i], mine[i]))
        return out

    position = lax.broadcasted_iota(jnp.int32, (seqs, length), 1)
    in_span = (position >= span_start[:, None]) & (position < (span_start + span_length)[:, None])
    start_rows = jnp.where(in_span[:, :, None], mask_embed[None, None, :], tokens)
    span_rows = in_span.astype(F32)

    def halves(array, axis):
        own = lax.dynamic_slice_in_dim(array, core * half, half, axis)
        other = lax.dynamic_slice_in_dim(array, (1 - core) * half, half, axis)
        return own, other

    step_onehot = (
        time_step[:, None] == lax.broadcasted_iota(jnp.int32, (seqs, time_table.shape[0]), 1)
    ).astype(F32)
    embedded = jnp.dot(step_onehot, time_table, precision=HIGH)
    conditions = jax.nn.silu(embedded)
    modulations = jnp.dot(conditions, mod_weight[0], precision=HIGH) + mod_bias[0]
    modulations = modulations.reshape(seqs, 3, features)
    span_own, span_other = halves(span_rows, 1)
    token_own, token_other = halves(start_rows, 1)
    cot_own, cot_other = halves(cotangent, 1)
    mods = by_owner(modulations, swap_cores(modulations, every), seqs)
    spans = by_owner(span_own, swap_cores(span_other, [0]), seqs)
    enter_rows = by_owner(
        token_own, [swap_cores(token_other[i], [0]) for i in range(seqs)], seqs
    )
    cot_rows = by_owner(cot_own, swap_cores(cot_other, [sections - 1]), seqs)

    cosine, sine = rope_tables(length, core)

    def head_columns(block, which):
        begin = block * features + which * width
        return lax.dynamic_slice_in_dim(first, begin, width, 1)

    weight_heads = jnp.concatenate([head_columns(block, core) for block in range(3)], 1).T
    bias_heads = jnp.concatenate(
        [lax.dynamic_slice_in_dim(in_bias[0], block * features + core * width, width, 0) for block in range(3)]
    )
    bias_heads = jnp.broadcast_to(bias_heads[:, None], (3 * width, 128))
    out_matrix = first[:, 3 * features :]
    out_own = lax.dynamic_slice_in_dim(out_matrix, core * width, width, 0)
    out_other = lax.dynamic_slice_in_dim(out_matrix, (1 - core) * width, width, 0)
    out_pair = jnp.concatenate([out_own, out_other], 0)
    out_row = in_bias[:, 3 * features :]

    keep = jnp.where(is_first, 1.0 - jnp.stack(spans), 1.0)[:, :, None]
    mods_rows = jnp.concatenate(
        [jnp.stack(mods), jnp.zeros((micro_count, 5, features), F32)], 1
    ).reshape(micro_count * 8, features)
    wide = lax.cond(
        section % 2 == 0,
        lambda: jnp.concatenate(
            [weight_heads, out_pair, jnp.zeros((hidden - 3 * width - 2 * width, features), BF16)], 0
        ),
        lambda: first.T,
    )
    states, stream, kept_first, kept_second, kept_rows, back_first, back_second, sums, bias = pipeline(
        jnp.stack(enter_rows), jnp.stack(cot_rows), wide, second, mods_rows, gain, keep, bias_heads, in_bias,
        out_bias, cosine, sine,
    )
    states = states[None]
    stream = stream[None]

    steps_all = lax.all_gather(time_step, "dp").reshape(dp_count // 2, 2, seqs).transpose(0, 2, 1).reshape(-1)
    onehot_all = (
        steps_all[:, None] == lax.broadcasted_iota(jnp.int32, (steps_all.shape[0], time_table.shape[0]), 1)
    ).astype(F32)
    embedded_all = jnp.dot(onehot_all, time_table, precision=HIGH)
    conditions_all, silu_pull = jax.vjp(jax.nn.silu, embedded_all)

    summed_first, summed_second, small = summed_gradients(
        kept_first, kept_second, kept_rows, back_first, back_second, sums, bias, mod_weight[0], dp_count
    )
    base = 3 * micro_count
    blocks = hidden // features
    cross = small[:, base + blocks + 2 : base + blocks + 4].reshape(dp_count // 2, 2, 2, features).sum(1)
    turns = [
        lax.ppermute(cross, "section", [(s, (s + turn) % sections) for s in every]) for turn in range(1, sections)
    ]
    grad_in, grad_out, grad_mod_weight, rows = place_gradients(
        summed_first, summed_second, small, conditions_all, hidden
    )
    grad_mod_bias = jnp.sum(rows[: 3 * micro_count].reshape(micro_count, 3 * features), 0)
    grad_gain = rows[base]
    grad_bias_first = rows[base + 1 : base + 1 + blocks].reshape(hidden)
    grad_bias_second = rows[base + 1 + blocks]
    cross = sum(turns, cross)
    cond = time_table.shape[1]
    grad_condition = cross[:, 0, : micro_count * cond].reshape(-1, cond)
    embed_total = jnp.sum(cross[:, 1], 0)
    grad_embedded = silu_pull(grad_condition)[0]
    table_total = lax.dot_general(
        onehot_all, grad_embedded, (((0,), (0,)), ((), ())), precision=HIGH, preferred_element_type=F32
    )
    return (
        states,
        stream,
        table_total,
        embed_total,
        grad_mod_weight[None],
        grad_mod_bias[None],
        grad_gain[None],
        grad_in[None],
        grad_bias_first[None],
        grad_out[None],
        grad_bias_second[None],
    )


def solution(mesh):
    placed = (
        P("dp", None, None),
        P("dp"),
        P("dp"),
        P("dp"),
        P(),
        P(),
        P("section", None, None),
        P("section", None),
        P("section", None),
        P("section", None, None),
        P("section", None),
        P("section", None, None),
        P("section", None),
        P("dp", None, None),
    )
    return jax.shard_map(
        shards,
        mesh=mesh,
        in_specs=placed,
        out_specs=(
            P("section", "dp", None, None),
            P("section", "dp", None, None),
            P(),
            P(),
            P("section", None, None),
            P("section", None),
            P("section", None),
            P("section", None, None),
            P("section", None),
            P("section", None, None),
            P("section", None),
        ),
        check_vma=False,
    )
```

```python
import math

import jax
import jax.numpy as jnp
import numpy as np
from jax import lax
from jax.experimental import pallas as pl
from jax.experimental.pallas import tpu as pltpu
from jax.sharding import PartitionSpec as P

HEAD = 64
HALF = HEAD // 2
EPS = 1e-06
HIGH = lax.Precision.HIGHEST
F32 = jnp.float32
BF16 = jnp.bfloat16
SCALE = HEAD ** (-0.5)
EXP2_SCALE = SCALE * math.log2(math.e)
GELU_C = math.sqrt(2.0 / math.pi)
VMEM_LIMIT = 56 << 20


def dot_nn(left, right):
    return jnp.dot(left, right, preferred_element_type=F32)


def dot_nt(left, right):
    return lax.dot_general(left, right, (((1,), (1,)), ((), ())), preferred_element_type=F32)


def params(**more):
    return pltpu.CompilerParams(vmem_limit_bytes=VMEM_LIMIT, **more)


def shape(dims, dtype):
    return jax.ShapeDtypeStruct(dims, dtype)


def normalize(rows):
    average = jnp.mean(rows, -1, keepdims=True)
    centered = rows - average
    inverse_std = lax.rsqrt(jnp.mean(centered * centered, -1, keepdims=True) + EPS)
    return centered * inverse_std, inverse_std


MESH = pl.DeviceIdType.MESH
PARTS = 2
CUTS = ((0, 1), (1, 1), (2, 1), (3, 1))


def pipeline_kernel(
    tokens_ref, cot_ref, first_ref, second_ref, start_ref, length_ref, step_ref, table_ref, embed_ref,
    mod_weight_ref, mod_bias_ref, gain_ref, bias_row_ref, out_bias_ref, cos_ref, sin_ref,
    states_ref, stream_ref, kept_first, kept_second, kept_rows, back_first, back_second, sums_ref, bias_ref,
    weights, streams, pool, upstreams, mixed_got, first_buf, second_buf, branches, leaving,
    mixed_own, mixed_send, grad_send, grad_own, lse_ref, bias_columns, mods_ref,
    load_sem, pass_send, pass_recv, back_recv, swap_send, swap_recv, place_send, place_recv, store_sem, fetch_sem,
    local_sem, give_send, give_recv, mod_send, mod_recv, mixed_give, mixed_take, grad_give, grad_take,
):
    section = lax.axis_index("section")
    sections = lax.axis_size("section")
    dp_index = lax.axis_index("dp")
    core = lax.rem(dp_index, 2)
    partner = dp_index + 1 - 2 * core
    micros, half, features = streams.shape
    width = mixed_own.shape[1]
    heads = width // HEAD
    length = 2 * half
    part_rows = half // PARTS
    cuts = [slice(begin * half // 4, (begin + count) * half // 4) for begin, count in CUTS]
    attends = lax.rem(section, 2) == 0
    feeds = lax.rem(section, 2) == 1
    is_first = section == 0
    is_last = section == sections - 1
    hidden = second_ref.shape[0]
    blocks = hidden // features
    seqs = micros // 2
    cond = table_ref.shape[1]
    feed_step = half
    feed_parts = hidden // feed_step
    near = pl.ds(core * half, half)
    far = pl.ds((1 - core) * half, half)

    barrier = pltpu.get_barrier_semaphore()
    pl.semaphore_signal(barrier, inc=1, device_id=(partner, section), device_id_type=MESH)

    @pl.when(section > 0)
    def _():
        pl.semaphore_signal(barrier, inc=1, device_id=(dp_index, section - 1), device_id_type=MESH)

    @pl.when(section < sections - 1)
    def _():
        pl.semaphore_signal(barrier, inc=1, device_id=(dp_index, section + 1), device_id_type=MESH)

    def head_loads():
        copies = []
        for block in range(3):
            lanes = pl.ds(pl.multiple_of(block * features + core * width, 128), width)
            target = pl.ds(block * width, width)
            copies.append((first_ref.at[pl.ds(0, half), lanes], first_buf.at[0, :, target]))
            copies.append(
                (first_ref.at[pl.ds(half, features - half), lanes], first_buf.at[1, pl.ds(0, features - half), target])
            )
        for side in range(2):
            rows = pl.ds(pl.multiple_of((core if side == 0 else 1 - core) * width, 16), width)
            copies.append(
                (first_ref.at[rows, pl.ds(3 * features, features)], weights.at[pl.ds((3 + side) * width, width)])
            )
        return [pltpu.make_async_copy(*copy, load_sem.at[i]) for i, copy in enumerate(copies)]

    def pool_at(slot):
        return pool.at[pl.ds(pl.multiple_of(slot * half, 16), half)]

    def others_at(micro):
        return pool_at(micro)

    def up_others_at(micro):
        return pool_at(micros + micro)

    def feed_loads():
        copies = [
            (first_ref.at[:, pl.ds(block * features, features)], weights.at[pl.ds(block * features, features)])
            for block in range(blocks)
        ]
        copies += [
            (second_ref.at[pl.ds(part * feed_step, feed_step)], pool_at(part)) for part in range(feed_parts)
        ]
        return [pltpu.make_async_copy(*copy, load_sem.at[i]) for i, copy in enumerate(copies)]

    def token_copies(i):
        micro = 2 * i + core
        return [
            pltpu.make_async_copy(tokens_ref.at[i, near], streams.at[micro], local_sem.at[i, 0]),
            pltpu.make_async_copy(tokens_ref.at[i, far], others_at(micro), local_sem.at[i, 1]),
        ]

    def token_gives(i):
        micro = 2 * i + core
        return [
            pltpu.make_async_remote_copy(
                tokens_ref.at[i, rows], target, give_send.at[i, k], give_recv.at[i, k],
                device_id=(partner, section), device_id_type=MESH,
            )
            for k, (rows, target) in enumerate(((far, streams.at[micro]), (near, others_at(micro))))
        ]

    def cot_copy(i):
        return pltpu.make_async_copy(cot_ref.at[i, near], upstreams.at[2 * i + core], local_sem.at[i, 0])

    def cot_give(i):
        return pltpu.make_async_remote_copy(
            cot_ref.at[i, far], upstreams.at[2 * i + core], give_send.at[i, 0], give_recv.at[i, 0],
            device_id=(partner, section), device_id_type=MESH,
        )

    def mod_give(i):
        block = mods_ref.at[2 * i + core]
        return pltpu.make_async_remote_copy(
            block, block, mod_send.at[i], mod_recv.at[i], device_id=(partner, section), device_id_type=MESH
        )

    @pl.when(is_first)
    def _():
        for i in range(seqs):
            for copy in token_copies(i):
                copy.start()

    @pl.when(attends)
    def _():
        for copy in head_loads():
            copy.start()

    @pl.when(feeds)
    def _():
        for copy in feed_loads():
            copy.start()

    @pl.when(is_last)
    def _():
        for i in range(seqs):
            cot_copy(i).start()

    bias_ref[...] = jnp.zeros_like(bias_ref)
    bias_columns[...] = jnp.zeros_like(bias_columns)
    looked_up = [table_ref[pl.ds(step_ref[i], 1), :] for i in range(seqs)]
    embedded = jnp.concatenate(looked_up + [jnp.zeros((8 - seqs, cond), F32)], 0)
    condition = embedded * (1.0 / (1.0 + jnp.exp(-embedded)))
    modulations = mod_bias_ref[...] + lax.dot_general(
        condition, mod_weight_ref[...], (((1,), (0,)), ((), ())), precision=HIGH, preferred_element_type=F32
    )
    for i in range(seqs):
        bias_ref[2:3, i * cond : (i + 1) * cond] = looked_up[i]
        bias_ref[2:3, (seqs + i) * cond : (seqs + i + 1) * cond] = jnp.broadcast_to(
            step_ref[i].astype(F32), (1, cond)
        )
        begin = jnp.broadcast_to(start_ref[i].astype(F32), (1, features))
        end = jnp.broadcast_to((start_ref[i] + length_ref[i]).astype(F32), (1, features))
        mods_ref[2 * i + core] = jnp.concatenate(
            [modulations[i : i + 1, k * features : (k + 1) * features] for k in range(3)]
            + [begin, end, jnp.zeros((3, features), F32)],
            0,
        )

    pl.semaphore_wait(
        barrier, 1 + jnp.where(section > 0, 1, 0) + jnp.where(section < sections - 1, 1, 0)
    )
    for i in range(seqs):
        mod_give(i).start()

        if i == 0:

            @pl.when(is_first)
            def _():
                for copy in token_gives(i):
                    copy.start()

        @pl.when(is_last)
        def _():
            cot_give(i).start()

    @pl.when(attends)
    def _():
        for copy in head_loads():
            copy.wait()
        for block in range(3):
            lanes = slice(block * width, (block + 1) * width)
            weights[lanes, :half] = first_buf[0, :, lanes].T
            weights[lanes, half:] = first_buf[1, : features - half, lanes].T
            at = pl.multiple_of(block * features + core * width, 128)
            bias = jnp.broadcast_to(bias_row_ref[:, pl.ds(at, width)], (8, width)).T
            bias_columns[block, :, 8:16] = bias

    @pl.when(feeds)
    def _():
        for copy in feed_loads():
            copy.wait()

    def rows_of(part):
        return slice(part * part_rows, (part + 1) * part_rows)

    def schedule(step):
        turns = jnp.where(is_last, 1, 0)
        forward = jnp.where(is_last, 1 - lax.rem(step, 2), jnp.where(step < micros, 1, 0))
        micro = jnp.where(is_last, step // 2, lax.rem(step, micros))
        del turns
        return forward == 1, micro

    def pass_on(step, part, micro, forward):
        slot = lax.rem(step, 2)
        rows = pl.ds(cuts[part].start, cuts[part].stop - cuts[part].start)
        source = leaving.at[slot, rows]
        if forward:
            return pltpu.make_async_remote_copy(
                source, streams.at[micro, rows],
                pass_send.at[slot, part], pass_recv.at[micro, part],
                device_id=(dp_index, section + 1), device_id_type=MESH,
            )
        return pltpu.make_async_remote_copy(
            source, upstreams.at[micro, rows],
            pass_send.at[slot, part], back_recv.at[micro, part],
            device_id=(dp_index, section - 1), device_id_type=MESH,
        )

    def place_target(target, micro):
        return target.at[micro // 2, pl.ds(core * half, half)]

    def place_local(step, micro, target):
        slot = lax.rem(step, 2)
        return pltpu.make_async_copy(leaving.at[slot], place_target(target, micro), place_send.at[slot])

    def place_remote(step, micro, target, index):
        slot = lax.rem(step, 2)
        return pltpu.make_async_remote_copy(
            leaving.at[slot], place_target(target, micro), place_send.at[slot],
            place_recv.at[index, micro // 2], device_id=(partner, section), device_id_type=MESH,
        )

    def send_part(step, part, micro, forward):
        reaches = section < sections - 1 if forward else section > 0

        @pl.when(reaches)
        def _():
            pass_on(step, part, micro, forward).start()

    def place_result(step, micro, forward):
        target, index = (states_ref, 0) if forward else (stream_ref, 1)
        mine = lax.rem(micro, 2) == core

        @pl.when(mine)
        def _():
            place_local(step, micro, target).start()

        @pl.when(jnp.logical_not(mine))
        def _():
            place_remote(step, micro, target, index).start()

    def leaving_free(step):
        was_forward, micro = schedule(step)
        mine = lax.rem(micro, 2) == core
        for forward, cond in ((True, was_forward), (False, jnp.logical_not(was_forward))):
            reaches = section < sections - 1 if forward else section > 0
            target, index = (states_ref, 0) if forward else (stream_ref, 1)

            @pl.when(cond & reaches)
            def _():
                for part in range(len(cuts)):
                    pass_on(step, part, micro, forward).wait_send()

            @pl.when(cond & mine)
            def _():
                place_local(step, micro, target).wait()

            @pl.when(cond & jnp.logical_not(mine))
            def _():
                place_remote(step, micro, target, index).wait_send()

    def swap(kind, part, source, target, micro):
        rows = pl.ds(cuts[part].start, cuts[part].stop - cuts[part].start)
        return pltpu.make_async_remote_copy(
            source.at[rows], target.at[rows], swap_send.at[kind, part], swap_recv.at[kind, part, micro],
            device_id=(partner, section), device_id_type=MESH,
        )

    def give_mixed(pair, micro):
        lanes = pl.ds(pl.multiple_of(pair * 2 * HEAD, 2 * HEAD), 2 * HEAD)
        return pltpu.make_async_remote_copy(
            mixed_send.at[:, lanes], mixed_got.at[micro, :, lanes],
            mixed_give.at[pair], mixed_take.at[pair, micro],
            device_id=(partner, section), device_id_type=MESH,
        )

    def give_grad(part, micro):
        rows = pl.ds(part * part_rows, part_rows)
        return pltpu.make_async_remote_copy(
            grad_send.at[rows], others_at(micro).at[rows], grad_give.at[part], grad_take.at[part, micro],
            device_id=(partner, section), device_id_type=MESH,
        )

    def store_first(slot, target, micro):
        return pltpu.make_async_copy(first_buf.at[slot], target.at[micro], store_sem.at[slot])

    def store_second(target, micro):
        lanes = pl.ds(0, 2 * features)
        return pltpu.make_async_copy(second_buf.at[:, lanes], target.at[micro, :, lanes], store_sem.at[2])

    def store_active(micro):
        return pltpu.make_async_copy(second_buf, kept_second.at[micro], store_sem.at[2])

    def store_grad_branch(micro):
        return pltpu.make_async_copy(
            grad_send, back_second.at[micro, :, pl.ds(0, features)], store_sem.at[3]
        )

    def rows_kept(micro):
        return pool_at(feed_parts + lax.rem(micro, 2))

    def store_rows(micro):
        return pltpu.make_async_copy(
            rows_kept(micro), kept_rows.at[micro], store_sem.at[4 + lax.rem(micro, 2)]
        )

    def first_slot_free(slot, when):
        @pl.when(when)
        def _():
            store_first(slot, kept_first, 0).wait()

    def arrive(micro, part, forward):
        if not forward and part == 0:
            mine = lax.rem(micro, 2) == core

            @pl.when(is_last & mine)
            def _():
                cot_copy(micro // 2).wait()

            @pl.when(is_last & jnp.logical_not(mine))
            def _():
                cot_give(micro // 2).wait_recv()

        @pl.when(jnp.logical_not(is_first if forward else is_last))
        def _():
            pass_on(0, part, micro, forward).wait_recv()

    def arrive_mod(micro):
        @pl.when(lax.rem(micro, 2) != core)
        def _():
            mod_give(micro // 2).wait_recv()

    def in_span(micro, begin, count):
        bounds = mods_ref[micro, 3:5, 0:1]
        position = (lax.broadcasted_iota(jnp.int32, (count, 1), 0) + begin).astype(F32)
        return (position >= bounds[0:1]) & (position < bounds[1:2])

    def arrive_tokens(micro):
        mine = lax.rem(micro, 2) == core

        @pl.when(mine)
        def _():
            for copy in token_copies(micro // 2):
                copy.wait()

        @pl.when(jnp.logical_not(mine))
        def _():
            for copy in token_gives(micro // 2):
                copy.wait_recv()

        for target, side in ((streams.at[micro], core), (others_at(micro), 1 - core)):
            for part in range(PARTS):
                rows = rows_of(part)
                span = in_span(micro, side * half + part * part_rows, part_rows)
                target[rows, :] = jnp.where(span, embed_ref[...], target[rows, :])

    def attention_forward(step, micro):
        arrive_mod(micro)
        mod = mods_ref[micro]
        gain = gain_ref[...]
        slot = lax.rem(micro, 2)
        later = jnp.logical_not(is_first)

        @pl.when(is_first)
        def _():
            arrive_tokens(micro)

            @pl.when(step == 0)
            def _():
                for i in range(1, seqs):
                    for copy in token_gives(i):
                        copy.start()

        @pl.when(later)
        def _():
            for part in range(len(cuts)):
                arrive(micro, part, True)
                swap(0, part, streams.at[micro], others_at(micro), micro).start()

        first_slot_free(slot, step >= 2)

        @pl.when(step > 0)
        def _():
            store_second(kept_second, micro).wait()

        def project(source, part):
            standard, _ = normalize(source[rows_of(part % PARTS), :].astype(F32))
            rows = (standard * gain * (1.0 + mod[1:2]) + mod[0:1]).astype(BF16)
            place = (part // PARTS) * features
            second_buf[rows_of(part % PARTS), place : place + features] = rows
            projected = dot_nt(weights[: 3 * width, :], rows)
            side = core if part < PARTS else 1 - core
            columns = pl.ds(pl.multiple_of(side * half + (part % PARTS) * part_rows, 128), part_rows)
            cosine = cos_ref[:, columns]
            sine = sin_ref[:, columns]
            for block in range(3):
                lanes = slice(block * length + part * part_rows, block * length + (part + 1) * part_rows)
                biased = projected[block * width : (block + 1) * width] + bias_columns[block, :, 8:9]
                if block == 2:
                    first_buf[slot, :width, lanes] = biased.astype(BF16)
                    continue
                for head in range(heads):
                    base = head * HEAD
                    front = biased[base : base + HALF]
                    back = biased[base + HALF : base + HEAD]
                    at = head * HEAD
                    first_buf[slot, at : at + HALF, lanes] = (front * cosine - back * sine).astype(BF16)
                    first_buf[slot, at + HALF : at + HEAD, lanes] = (back * cosine + front * sine).astype(BF16)

        for part in range(PARTS):
            project(streams.at[micro], part)

        @pl.when(later)
        def _():
            for part in range(len(cuts)):
                swap(0, part, streams.at[micro], others_at(micro), micro).wait_recv()

        for part in range(PARTS, 2 * PARTS):
            project(others_at(micro), part)

        def scores_of(head):
            base = pl.multiple_of(head * HEAD, HEAD)
            key_rows = first_buf[slot, pl.ds(base, HEAD), length : 2 * length].T
            return dot_nn(key_rows, first_buf[slot, pl.ds(base, HEAD), :length])

        def finish(head, within, scores):
            base = pl.multiple_of(head * HEAD, HEAD)
            top = jnp.max(scores, 0, keepdims=True) * EXP2_SCALE
            spread = jnp.exp2(scores * EXP2_SCALE - top)
            total = jnp.sum(spread, 0, keepdims=True)
            mixed = dot_nn(first_buf[slot, pl.ds(base, HEAD), 2 * length :], spread.astype(BF16))
            lse_ref[micro, pl.ds(head, 1), :] = top + jnp.log2(total)
            return (mixed * (1.0 / total)).astype(BF16)

        def head_pair(pair, carried):
            scores = scores_of(2 * pair), scores_of(2 * pair + 1)
            mixed = jnp.concatenate([finish(2 * pair + i, i, scores[i]) for i in range(2)], 0)
            at = pl.multiple_of(pair * length, length)
            first_buf[slot, width:, pl.ds(at, length)] = mixed
            turned = mixed.T
            lanes = pl.multiple_of(pair * 2 * HEAD, 2 * HEAD)
            mixed_own[:, pl.ds(lanes, 2 * HEAD)] = turned[:half]
            mixed_send[:, pl.ds(lanes, 2 * HEAD)] = turned[half:]
            give_mixed(pair, micro).start()
            return carried

        lax.fori_loop(0, heads // 2, head_pair, 0)
        store_first(slot, kept_first, micro).start()
        store_second(kept_second, micro).start()

        @pl.when(step >= 2)
        def _():
            leaving_free(step - 2)

        for pair in range(heads // 2):
            give_mixed(pair, micro).wait_recv()
        for part, rows in enumerate(cuts):
            mixed = jnp.concatenate([mixed_own[rows, :], mixed_got[micro, rows, :]], 1)
            branch = dot_nn(mixed, weights[3 * width : 5 * width, :]) + bias_row_ref[:, 3 * features :]
            branches[micro, rows, :] = branch.astype(BF16)
            result = streams[micro, rows, :].astype(F32) + mod[2:3] * branch
            leaving[lax.rem(step, 2), rows, :] = result.astype(BF16)
            send_part(step, part, micro, True)
        place_result(step, micro, True)
        for pair in range(heads // 2):
            give_mixed(pair, micro).wait_send()

        @pl.when(later)
        def _():
            for part in range(len(cuts)):
                swap(0, part, streams.at[micro], others_at(micro), micro).wait_send()

    pieces = [(block, lane) for block in range(blocks) for lane in range(0, features, part_rows)]

    def feed_forward(step, micro):
        arrive_mod(micro)
        mod = mods_ref[micro]
        gain = gain_ref[...]

        slot = jnp.where(is_last, 0, lax.rem(micro, 2))
        first_slot_free(slot, jnp.logical_not(is_last) & (micro >= 2))

        @pl.when(micro >= 1)
        def _():
            store_active(micro).wait()

        @pl.when(micro >= 2)
        def _():
            store_rows(micro).wait()

        @pl.when(step >= 2)
        def _():
            leaving_free(step - 2)

        entering_rows = rows_kept(micro)
        for part, rows in enumerate(cuts):
            arrive(micro, part, True)
            standard, _ = normalize(streams[micro, rows, :].astype(F32))
            entering = (standard * gain * (1.0 + mod[1:2]) + mod[0:1]).astype(BF16)
            entering_rows[rows, :] = entering
            for piece, (block, lane) in enumerate(pieces):
                lanes = slice(piece * part_rows, (piece + 1) * part_rows)
                value = (
                    dot_nn(entering, weights[block * features : (block + 1) * features, lane : lane + part_rows])
                    + bias_row_ref[:, lanes]
                )
                square = value * value
                bend = jnp.tanh(GELU_C * value * (1.0 + 0.044715 * square))
                raised = 0.5 + 0.5 * bend
                second_buf[rows, lanes] = (value * raised).astype(BF16)
                first_buf[slot, rows, lanes] = (
                    raised + (0.5 * GELU_C) * value * (1.0 - bend * bend) * (1.0 + (3 * 0.044715) * square)
                ).astype(BF16)
            branch = dot_nn(second_buf[rows, :], pool[:hidden, :]) + out_bias_ref[...]
            branches[micro, rows, :] = branch.astype(BF16)
            result = streams[micro, rows, :].astype(F32) + mod[2:3] * branch
            leaving[lax.rem(step, 2), rows, :] = result.astype(BF16)
            send_part(step, part, micro, True)
        place_result(step, micro, True)
        store_active(micro).start()
        store_rows(micro).start()

        @pl.when(jnp.logical_not(is_last))
        def _():
            store_first(slot, kept_first, micro).start()

    def fetch_kept(micro):
        return pltpu.make_async_copy(kept_first.at[micro], first_buf.at[0], fetch_sem.at[0])

    def attention_backward(step, micro):
        mod = mods_ref[micro]
        gain = gain_ref[...]
        store_second(kept_second, micro).wait()
        first_slot_free(1, step >= micros)

        @pl.when(step == micros)
        def _():
            store_first(0, kept_first, 0).wait()
            fetch_kept(micro).start()

        def exchange(part):
            return swap(1, part, upstreams.at[micro], up_others_at(micro), micro)

        for part in range(len(cuts)):
            arrive(micro, part, False)
            exchange(part).start()
        grad_mixed_at = 2 * features

        def into_heads(source, part):
            grad_branch = (mod[2:3] * source[rows_of(part % PARTS), :].astype(F32)).astype(BF16)
            place = (part // PARTS) * features
            second_buf[rows_of(part % PARTS), place : place + features] = grad_branch
            if part < PARTS:
                bias_ref[0:1, 3 * features :] += jnp.sum(grad_branch.astype(F32), 0, keepdims=True)
            lanes = slice(grad_mixed_at + part * part_rows, grad_mixed_at + (part + 1) * part_rows)
            second_buf[:width, lanes] = dot_nt(weights[3 * width : 4 * width, :], grad_branch).astype(BF16)

        for part in range(PARTS):
            into_heads(upstreams.at[micro], part)
        for part in range(len(cuts)):
            exchange(part).wait_recv()
        for part in range(PARTS, 2 * PARTS):
            into_heads(up_others_at(micro), part)
        fetch_kept(micro).wait()
        near_lanes = pl.ds(pl.multiple_of(core * half, 128), half)
        far_lanes = pl.ds(pl.multiple_of((1 - core) * half, 128), half)
        cosine = jnp.concatenate([cos_ref[:, near_lanes], cos_ref[:, far_lanes]], 1)
        sine = jnp.concatenate([sin_ref[:, near_lanes], sin_ref[:, far_lanes]], 1)

        def turn_back(base, block, gradient):
            front = gradient[:HALF] * SCALE
            back = gradient[HALF:] * SCALE
            turned = jnp.concatenate([front * cosine + back * sine, back * cosine - front * sine], 0)
            put_back(base, block, turned.astype(BF16))

        def put_back(base, block, gradient):
            first_buf[1, pl.ds(base, HEAD), block * length : (block + 1) * length] = gradient
            bias_columns[block, pl.ds(base, HEAD), 0:1] += jnp.sum(gradient.astype(F32), 1, keepdims=True)

        def one_head(head, mixed):
            base = pl.multiple_of(head * HEAD, HEAD)
            query = first_buf[0, pl.ds(base, HEAD), :length]
            key = first_buf[0, pl.ds(base, HEAD), length : 2 * length]
            value = first_buf[0, pl.ds(base, HEAD), 2 * length :]
            grad_mixed = second_buf[pl.ds(base, HEAD), grad_mixed_at : grad_mixed_at + length]
            delta = jnp.sum(grad_mixed.astype(F32) * mixed.astype(F32), 0, keepdims=True)
            scores = dot_nn(key.T, query)
            spread = jnp.exp2(scores * EXP2_SCALE - lse_ref[micro, pl.ds(head, 1), :])
            grad_spread = dot_nn(value.T, grad_mixed)
            grad_scores = (spread * (grad_spread - delta)).astype(BF16)
            grad_value = dot_nn(spread.astype(BF16), grad_mixed.T)
            grad_key = dot_nn(grad_scores, query.T)
            grad_query = dot_nn(key, grad_scores)
            turn_back(base, 0, grad_query)
            turn_back(base, 1, grad_key.T)
            put_back(base, 2, grad_value.T.astype(BF16))

        def head_pair(pair, carried):
            at = pl.multiple_of(pair * length, length)
            mixed = first_buf[0, width:, pl.ds(at, length)]
            one_head(2 * pair, mixed[:HEAD])
            one_head(2 * pair + 1, mixed[HEAD:])
            return carried

        lax.fori_loop(0, heads // 2, head_pair, 0)

        @pl.when(step + 1 < 2 * micros)
        def _():
            fetch_kept(micro + 1).start()

        def grad_rows_of(part):
            begin = part * part_rows
            heads_of = [
                first_buf[1, :width, block * length + begin : block * length + begin + part_rows] for block in range(3)
            ]
            return dot_nn(jnp.concatenate(heads_of, 0).T, weights[: 3 * width, :])

        for part in range(PARTS):
            grad_send[rows_of(part), :] = grad_rows_of(PARTS + part).astype(BF16)
            give_grad(part, micro).start()
        store_first(1, back_first, micro).start()
        store_second(back_second, micro).start()
        for part in range(PARTS):
            grad_own[rows_of(part), :] = grad_rows_of(part)
        leaving_free(step - 2)
        given = others_at(micro)
        for part, rows in enumerate(cuts):
            if rows.start % part_rows == 0:
                give_grad(rows.start // part_rows, micro).wait_recv()
            finish_back(
                grad_own[rows, :] + given[rows, :].astype(F32),
                streams[micro, rows, :].astype(F32),
                upstreams[micro, rows, :].astype(F32),
                branches[micro, rows, :].astype(F32),
                mod, gain,
                jnp.logical_not(in_span(micro, core * half + rows.start, rows.stop - rows.start) & is_first),
                leaving, (lax.rem(step, 2), rows), sums_ref, micro, part == 0,
            )
            send_part(step, part, micro, False)
        place_result(step, micro, False)
        for part in range(len(cuts)):
            exchange(part).wait_send()
        for part in range(PARTS):
            give_grad(part, micro).wait_send()

    def feed_backward(step, micro):
        mod = mods_ref[micro]
        gain = gain_ref[...]
        inner = jnp.logical_not(is_last)

        @pl.when(inner & (step == micros))
        def _():
            store_first(0, kept_first, 0).wait()
            store_first(1, kept_first, 0).wait()
            fetch_kept(micro).start()

        @pl.when(micro >= 1)
        def _():
            store_first(1, back_first, 0).wait()
            store_grad_branch(micro).wait()

        @pl.when(step >= 2)
        def _():
            leaving_free(step - 2)

        @pl.when(inner)
        def _():
            fetch_kept(micro).wait()

        for part, rows in enumerate(cuts):
            arrive(micro, part, False)
            upstream = upstreams[micro, rows, :].astype(F32)
            grad_branch = (mod[2:3] * upstream).astype(BF16)
            grad_send[rows, :] = grad_branch
            bias_ref[1:2, :features] += jnp.sum(grad_branch.astype(F32), 0, keepdims=True)
            for piece in range(len(pieces)):
                lanes = slice(piece * part_rows, (piece + 1) * part_rows)
                grad_active = dot_nt(grad_branch, pool[lanes, :])
                grad_hidden = (grad_active * first_buf[0, rows, lanes].astype(F32)).astype(BF16)
                first_buf[1, rows, lanes] = grad_hidden
                bias_ref[0:1, lanes] += jnp.sum(grad_hidden.astype(F32), 0, keepdims=True)
            total = None
            for block in range(blocks):
                lanes = slice(block * features, (block + 1) * features)
                term = dot_nt(first_buf[1, rows, lanes], weights[lanes, :])
                total = term if total is None else total + term
            finish_back(
                total,
                streams[micro, rows, :].astype(F32),
                upstream,
                branches[micro, rows, :].astype(F32),
                mod, gain, None,
                leaving, (lax.rem(step, 2), rows), sums_ref, micro, part == 0,
            )
            send_part(step, part, micro, False)
        place_result(step, micro, False)
        store_first(1, back_first, micro).start()
        store_grad_branch(micro).start()

        @pl.when(inner & (step + 1 < 2 * micros))
        def _():
            fetch_kept(micro + 1).start()

    def one_step(step, carried):
        forward, micro = schedule(step)
        backward = jnp.logical_not(forward)

        @pl.when(attends & forward)
        def _():
            attention_forward(step, micro)

        @pl.when(attends & backward)
        def _():
            attention_backward(step, micro)

        @pl.when(feeds & forward)
        def _():
            feed_forward(step, micro)

        @pl.when(feeds & backward)
        def _():
            feed_backward(step, micro)

        return carried

    lax.fori_loop(0, 2 * micros, one_step, 0)

    @pl.when(attends)
    def _():
        for block in range(3):
            at = pl.multiple_of(block * features + core * width, 128)
            bias_ref[0:1, pl.ds(at, width)] = bias_columns[block].T[0:1]

    store_first(1, back_first, 0).wait()

    @pl.when(attends)
    def _():
        store_second(back_second, 0).wait()

    @pl.when(feeds)
    def _():
        store_active(0).wait()
        store_grad_branch(0).wait()
        store_rows(0).wait()
        store_rows(1).wait()

    leaving_free(2 * micros - 2)
    leaving_free(2 * micros - 1)
    for i in range(seqs):
        mod_give(i).wait_send()

        @pl.when(is_first)
        def _():
            for copy in token_gives(i):
                copy.wait_send()

        @pl.when(is_last)
        def _():
            cot_give(i).wait_send()

    for index, target in enumerate((states_ref, stream_ref)):
        for slot in range(micros // 2):
            pltpu.make_async_remote_copy(
                leaving.at[0], target.at[slot, pl.ds((1 - core) * half, half)], place_send.at[0],
                place_recv.at[index, slot], device_id=(partner, section), device_id_type=MESH,
            ).wait_recv()


def finish_back(
    grad_rows, stream, upstream, branch, mod, gain, keep, leaving, place, sums_ref, micro, start,
):
    standard, inverse_std = normalize(stream)
    scaling = mod[1:2, :]
    grad_normed = grad_rows * (1.0 + scaling)
    grad_hat = grad_normed * gain
    grad_stream = upstream + inverse_std * (
        grad_hat
        - jnp.mean(grad_hat, -1, keepdims=True)
        - standard * jnp.mean(grad_hat * standard, -1, keepdims=True)
    )
    row_sum = lambda value: jnp.sum(value, 0, keepdims=True)
    with_standard = row_sum(grad_rows * standard)
    sums = [
        row_sum(grad_rows),
        with_standard * gain,
        row_sum(upstream * branch),
        with_standard * (1.0 + scaling),
    ]
    slot, rows = place
    if keep is None:
        sums.append(jnp.zeros_like(sums[0]))
        leaving[slot, rows, :] = grad_stream.astype(BF16)
    else:
        kept = jnp.where(keep, grad_stream, 0.0)
        sums.append(row_sum(grad_stream - kept))
        leaving[slot, rows, :] = kept.astype(BF16)
    sums = jnp.concatenate(sums + [jnp.zeros((3, sums[0].shape[1]), F32)], 0)
    if start:
        sums_ref[micro] = sums
    else:
        sums_ref[micro] += sums


def pipeline(
    tokens, cot, first, second, span_start, span_length, time_step, table, embed, mod_weight, mod_bias, gain,
    bias_row, out_bias, cosine, sine,
):
    seqs, length, features = tokens.shape
    micros = 2 * seqs
    half = length // 2
    width = features // 2
    hidden = second.shape[0]
    anywhere = pl.BlockSpec(memory_space=pl.ANY)
    inside = pl.BlockSpec(memory_space=pltpu.VMEM)
    scalars = pl.BlockSpec(memory_space=pltpu.SMEM)
    dma = pltpu.SemaphoreType.DMA
    rows = (micros, half, features)
    return pl.pallas_call(
        pipeline_kernel,
        in_specs=[anywhere] * 4 + [scalars] * 3 + [inside] * 9,
        out_specs=[anywhere] * 7 + [inside] * 2,
        out_shape=(
            shape((seqs, length, features), BF16),
            shape((seqs, length, features), BF16),
            shape((micros, half, hidden), BF16),
            shape((micros, half, hidden), BF16),
            shape(rows, BF16),
            shape((micros, half, hidden), BF16),
            shape((micros, half, hidden), BF16),
            shape((micros, 8, features), F32),
            shape((8, hidden), F32),
        ),
        scratch_shapes=[
            pltpu.VMEM((hidden, features), BF16),
            pltpu.VMEM(rows, BF16),
            pltpu.VMEM((2 * micros * half, features), BF16),
            pltpu.VMEM(rows, BF16),
            pltpu.VMEM((micros, half, width), BF16),
            pltpu.VMEM((2, half, hidden), BF16),
            pltpu.VMEM((half, hidden), BF16),
            pltpu.VMEM(rows, BF16),
            pltpu.VMEM((2, half, features), BF16),
            pltpu.VMEM((half, width), BF16),
            pltpu.VMEM((half, width), BF16),
            pltpu.VMEM((half, features), BF16),
            pltpu.VMEM((half, features), F32),
            pltpu.VMEM((micros, 8, length), F32),
            pltpu.VMEM((3, width, 128), F32),
            pltpu.VMEM((micros, 8, features), F32),
            dma((hidden // features + hidden // half,)),
            dma((2, len(CUTS))),
            dma((micros, len(CUTS))),
            dma((micros, len(CUTS))),
            dma((2, len(CUTS))),
            dma((2, len(CUTS), micros)),
            dma((2,)),
            dma((2, seqs)),
            dma((6,)),
            dma((1,)),
            dma((seqs, 2)),
            dma((seqs, 2)),
            dma((seqs, 2)),
            dma((seqs,)),
            dma((seqs,)),
            dma((width // (2 * HEAD),)),
            dma((width // (2 * HEAD), micros)),
            dma((PARTS,)),
            dma((PARTS, micros)),
        ],
        compiler_params=params(collective_id=0, has_side_effects=True),
        name="pipeline",
    )(
        tokens, cot, first, second, span_start, span_length, time_step, table, embed, mod_weight, mod_bias, gain,
        bias_row, out_bias, cosine, sine,
    )


SMALL_ROWS = 24


def gradient_kernel(
    kept_first, kept_second, kept_rows, back_first, back_second, sums_ref, bias_ref, mod_weight_ref,
    summed_first, summed_second, small_ref,
    wide_a, wide_b, deep_a, deep_b, total_a, total_b, give, got, scatter_send, scatter_got, entry,
    load_sem, pair_send, pair_recv, step_send, step_recv, gather_send, gather_recv, core_send, core_recv,
    small_send, small_recv,
):
    section = lax.axis_index("section")
    dp_index = lax.axis_index("dp")
    dp_count = small_ref.shape[0]
    core = lax.rem(dp_index, 2)
    partner = dp_index + 1 - 2 * core
    attends = lax.rem(section, 2) == 0
    feeds = lax.rem(section, 2) == 1
    micros, half, hidden = back_first.shape
    features = kept_rows.shape[2]
    width = features // 2
    length = 2 * half
    mid = hidden // 2
    columns = features // 2
    small_bits = dp_count.bit_length() - 1
    bits = small_bits - 1

    def bit_of(place):
        return lax.rem(dp_index // (1 << place), 2)

    def across(place):
        return dp_index + (1 - 2 * bit_of(place)) * (1 << place)

    barrier = pltpu.get_barrier_semaphore()
    for place in range(small_bits):
        pl.semaphore_signal(barrier, inc=1, device_id=(across(place), section), device_id_type=MESH)

    def small_entry():
        rows = [sums_ref[m, k : k + 1, :] for m in range(micros) for k in range(3)]
        gain = sum(sums_ref[m, 3:4, :] for m in range(micros))
        embed = sum(sums_ref[m, 4:5, :] for m in range(micros))
        rows.append(gain)
        rows += [bias_ref[0:1, k * features : (k + 1) * features] for k in range(hidden // features)]
        rows.append(bias_ref[1:2, :features])
        condition = []
        for m in range(micros):
            total = None
            for k in range(3):
                term = lax.dot_general(
                    jnp.broadcast_to(sums_ref[m, k : k + 1, :], (8, features)),
                    mod_weight_ref[:, k * features : (k + 1) * features],
                    (((1,), (1,)), ((), ())), precision=HIGH, preferred_element_type=F32,
                )
                total = term if total is None else total + term
            condition.append(total[0:1])
        condition.append(jnp.zeros((1, features - micros * mod_weight_ref.shape[0]), F32))
        rows.append(jnp.concatenate(condition, 1))
        rows.append(embed)
        rows.append(bias_ref[2:3, :features])
        rows.append(jnp.zeros((SMALL_ROWS - len(rows), features), F32))
        entry[...] = jnp.concatenate(rows, 0)
        small_ref[pl.ds(dp_index, 1)] = entry[...][None]

    def small_copy(step):
        size = 1 << step
        start = (dp_index // size) * size
        block = small_ref.at[pl.ds(start, size)]
        return pltpu.make_async_remote_copy(
            block, block, small_send.at[step], small_recv.at[step],
            device_id=(across(step), section), device_id_type=MESH,
        )

    def small_wait(step):
        size = 1 << step
        start = (dp_index // size) * size + (1 - 2 * bit_of(step)) * size
        block = small_ref.at[pl.ds(start, size)]
        pltpu.make_async_remote_copy(
            block, block, small_send.at[step], small_recv.at[step],
            device_id=(across(step), section), device_id_type=MESH,
        ).wait_recv()
        small_copy(step).wait_send()

    def loads(pairs, first_sem):
        return [
            pltpu.make_async_copy(source, target, load_sem.at[first_sem + i])
            for i, (source, target) in enumerate(pairs)
        ]

    def spans(m):
        return slice(m * half, (m + 1) * half)

    def heads_rows(source, target, first_sem):
        return loads(
            [(source.at[m, :, pl.ds(0, 2 * features)], target.at[spans(m), :]) for m in range(micros)], first_sem
        )

    def heads_columns(block, target, first_sem):
        pairs = []
        for m in range(micros):
            for side in range(2):
                at = side * half
                if block < 3:
                    source = back_first.at[m, pl.ds(0, width), pl.ds(block * length + at, half)]
                    pairs.append((source, target.at[pl.ds(side * width, width), spans(m)]))
                    continue
                for pair in range(3):
                    rows = width // 3
                    source = kept_first.at[m, pl.ds(width, rows), pl.ds(pair * length + at, half)]
                    pairs.append((source, target.at[pl.ds(side * width + pair * rows, rows), spans(m)]))
        return loads(pairs, first_sem)

    def half_columns(source, which, target, first_sem):
        return loads(
            [(source.at[m, :, pl.ds(which * mid, mid)], target.at[spans(m), :]) for m in range(micros)], first_sem
        )

    totals = (total_a, total_b)
    outputs = (summed_first, summed_second)

    def place_order(part):
        order = list(range(1, bits + 1))
        return order if part == 0 else order[::-1]

    def window(part, steps):
        size = mid
        start = 0
        for place in place_order(part)[:steps]:
            size = size // 2
            start = start + bit_of(place) * size
        return start, size

    def lanes(part):
        return pl.ds(part * columns, columns)

    def step_copy(payload, part, step):
        place = place_order(part)[step]
        size = mid >> (step + 1)
        return pltpu.make_async_remote_copy(
            scatter_send.at[payload, part, pl.ds(mid - (mid >> step), size)],
            scatter_got.at[payload, part, pl.ds(mid - (mid >> step), size)],
            step_send.at[payload, part, step], step_recv.at[payload, part, step],
            device_id=(across(place), section), device_id_type=MESH,
        )

    def scatter_start(payload, part, step):
        place = place_order(part)[step]
        start, _ = window(part, step)
        size = mid >> (step + 1)
        away = pl.multiple_of(start + (1 - bit_of(place)) * size, 16)
        scatter_send[payload, part, pl.ds(mid - (mid >> step), size), :] = totals[payload][
            pl.ds(away, size), part * columns : (part + 1) * columns
        ].astype(BF16)
        step_copy(payload, part, step).start()

    def scatter_finish(payload, part, step):
        step_copy(payload, part, step).wait()
        start, size = window(part, step + 1)
        rows = pl.ds(pl.multiple_of(start, 16), size)
        cut = slice(part * columns, (part + 1) * columns)
        value = totals[payload][rows, cut] + scatter_got[payload, part, pl.ds(mid - (mid >> step), size), :].astype(F32)
        if step < bits - 1:
            totals[payload][rows, cut] = value
        else:
            outputs[payload][core, rows, cut] = value.astype(BF16)

    def gather_copy(payload, part, step, theirs):
        place = place_order(part)[step]
        start, size = window(part, step + 1)
        if theirs:
            start = start + (1 - 2 * bit_of(place)) * size
        block = outputs[payload].at[core, pl.ds(pl.multiple_of(start, 16), size), lanes(part)]
        return pltpu.make_async_remote_copy(
            block, block, gather_send.at[payload, part, step], gather_recv.at[payload, part, step],
            device_id=(across(place), section), device_id_type=MESH,
        )

    def core_copy(payload, part, step, other):
        if step == bits:
            start, size = window(part, bits)
        else:
            place = place_order(part)[step]
            start, size = window(part, step + 1)
            start = start + (1 - 2 * bit_of(place)) * size
        side = 1 - core if other else core
        block = outputs[payload].at[side, pl.ds(pl.multiple_of(start, 16), size), lanes(part)]
        return pltpu.make_async_remote_copy(
            block, block, core_send.at[payload, part, step], core_recv.at[payload, part, step],
            device_id=(partner, section), device_id_type=MESH,
        )

    def tick(payload, number):
        for part in range(2):
            if number <= bits:
                if number > 0:
                    scatter_finish(payload, part, number - 1)
                if number < bits:
                    scatter_start(payload, part, number)
                else:
                    core_copy(payload, part, bits, False).start()
                    gather_copy(payload, part, bits - 1, False).start()
            else:
                step = 2 * bits - number
                gather_copy(payload, part, step, True).wait_recv()
                core_copy(payload, part, step, False).start()
                if step > 0:
                    gather_copy(payload, part, step - 1, False).start()

    last_tick = 2 * bits

    def wind_up(payload):
        for part in range(2):
            for step in range(bits):
                gather_copy(payload, part, step, False).wait_send()
            for step in range(bits + 1):
                core_copy(payload, part, step, False).wait_send()
                core_copy(payload, part, step, True).wait_recv()

    @pl.when(attends)
    def _():
        rows = heads_rows(kept_second, wide_a, 0)
        grads = heads_rows(back_second, wide_b, micros)
        buffers = (deep_a, deep_b)
        per = 2 * micros
        blocks = [
            heads_columns(block, buffers[block % 2], 2 * micros + (block % 2) * 3 * per) for block in range(4)
        ]
        for copy in rows + blocks[0] + blocks[1]:
            copy.start()
        small_entry()
        for copy in rows:
            copy.wait()
        for block in range(4):
            for copy in blocks[block]:
                copy.wait()
            source = wide_a if block < 3 else wide_b
            if block == 2:
                for copy in grads:
                    copy.start()
            if block == 3:
                for copy in grads:
                    copy.wait()
            deep = buffers[block % 2]
            total_a[block * width : (block + 1) * width, :] = dot_nn(
                deep[:width, :], source[:, :features]
            ) + dot_nn(deep[width:, :], source[:, features:])
            if block + 2 < 4:
                for copy in blocks[block + 2]:
                    copy.start()

    def transposed_rows(source, first_sem, staged, target):
        copies = loads(
            [(source.at[m, :, pl.ds(0, features)], staged.at[m // 2, pl.ds((m % 2) * half, half)]) for m in range(micros)],
            first_sem,
        )

        def turn():
            for m in range(micros):
                copies[m].wait()
                target[:, m * half : (m + 1) * half] = staged[m // 2, (m % 2) * half : (m % 2 + 1) * half, :].T

        return copies, turn

    def pair_copy(payload):
        return pltpu.make_async_remote_copy(
            give, got.at[payload], pair_send.at[payload], pair_recv.at[payload],
            device_id=(partner, section), device_id_type=MESH,
        )

    pieces = mid // features

    def other_half(deep, wide, payload):
        for piece in range(pieces):
            give[piece * features : (piece + 1) * features, :] = dot_nn(
                deep[...], wide[:, piece * features : (piece + 1) * features]
            ).astype(BF16)

    def own_half(deep, wide, payload):
        for piece in range(pieces):
            totals[payload][piece * features : (piece + 1) * features, :] = dot_nn(
                deep[...], wide[:, piece * features : (piece + 1) * features]
            )

    def add_pair(payload):
        pair_copy(payload).wait()
        totals[payload][...] += got[payload].astype(F32)

    @pl.when(feeds)
    def _():
        far = 1 - core
        first_rows, first_turn = transposed_rows(kept_rows, 0, summed_first, deep_a)
        second_rows = transposed_rows(back_second, micros, summed_second, deep_b)[0]
        first_far = half_columns(back_first, far, wide_a, 2 * micros)
        first_near = half_columns(back_first, core, wide_b, 3 * micros)
        for copy in first_rows + first_far + first_near + second_rows:
            copy.start()
        small_entry()
        first_turn()
        for copy in first_far:
            copy.wait()
        other_half(deep_a, wide_a, 0)

    pl.semaphore_wait(barrier, small_bits)
    small_copy(0).start()

    @pl.when(feeds)
    def _():
        far = 1 - core
        first_near = half_columns(back_first, core, wide_b, 3 * micros)
        second_far = half_columns(kept_second, far, wide_a, 4 * micros)
        second_near = half_columns(kept_second, core, wide_b, 5 * micros)
        second_turn = transposed_rows(back_second, micros, summed_second, deep_b)[1]
        pair_copy(0).start()
        for copy in second_far:
            copy.start()
        for copy in first_near:
            copy.wait()
        own_half(deep_a, wide_b, 0)
        for copy in second_near:
            copy.start()
        second_turn()
        add_pair(0)

    tick(0, 0)

    @pl.when(feeds)
    def _():
        far = 1 - core
        second_far = half_columns(kept_second, far, wide_a, 4 * micros)
        second_near = half_columns(kept_second, core, wide_b, 5 * micros)
        for copy in second_far:
            copy.wait()
        other_half(deep_b, wide_a, 1)
        pair_copy(1).start()
        for copy in second_near:
            copy.wait()
        own_half(deep_b, wide_b, 1)
        add_pair(1)

    for number in range(last_tick + 2):
        if number + 1 <= last_tick:
            tick(0, number + 1)
        if number <= last_tick:

            @pl.when(feeds)
            def _():
                tick(1, number)

        if number < small_bits:
            small_wait(number)
            if number + 1 < small_bits:
                small_copy(number + 1).start()
    for number in range(last_tick + 2, small_bits):
        small_wait(number)
        if number + 1 < small_bits:
            small_copy(number + 1).start()
    wind_up(0)

    @pl.when(feeds)
    def _():
        wind_up(1)


def summed_gradients(kept_first, kept_second, kept_rows, back_first, back_second, sums, bias, mod_weight, dp_count):
    micros, half, hidden = back_first.shape
    features = kept_rows.shape[2]
    mid = hidden // 2
    small_bits = dp_count.bit_length() - 1
    bits = small_bits - 1
    anywhere = pl.BlockSpec(memory_space=pl.ANY)
    inside = pl.BlockSpec(memory_space=pltpu.VMEM)
    dma = pltpu.SemaphoreType.DMA
    tokens = micros * half
    return pl.pallas_call(
        gradient_kernel,
        in_specs=[anywhere] * 5 + [inside] * 3,
        out_specs=[inside] * 3,
        out_shape=(
            shape((2, mid, features), BF16),
            shape((2, mid, features), BF16),
            shape((dp_count, SMALL_ROWS, features), F32),
        ),
        scratch_shapes=[
            pltpu.VMEM((tokens, mid), BF16),
            pltpu.VMEM((tokens, mid), BF16),
            pltpu.VMEM((features, tokens), BF16),
            pltpu.VMEM((features, tokens), BF16),
            pltpu.VMEM((mid, features), F32),
            pltpu.VMEM((mid, features), F32),
            pltpu.VMEM((mid, features), BF16),
            pltpu.VMEM((2, mid, features), BF16),
            pltpu.VMEM((2, 2, mid - (mid >> bits), features // 2), BF16),
            pltpu.VMEM((2, 2, mid - (mid >> bits), features // 2), BF16),
            pltpu.VMEM((SMALL_ROWS, features), F32),
            dma((14 * micros,)),
            dma((2,)),
            dma((2,)),
            dma((2, 2, bits)),
            dma((2, 2, bits)),
            dma((2, 2, bits)),
            dma((2, 2, bits)),
            dma((2, 2, bits + 1)),
            dma((2, 2, bits + 1)),
            dma((small_bits,)),
            dma((small_bits,)),
        ],
        compiler_params=pltpu.CompilerParams(vmem_limit_bytes=62 << 20, collective_id=1, has_side_effects=True),
        name="summed_gradients",
    )(kept_first, kept_second, kept_rows, back_first, back_second, sums, bias, mod_weight)


def place_kernel(first_ref, second_ref, small_ref, grad_in, grad_out, mod_weight_grad, rows_ref):
    step = pl.program_id(0)
    attends = lax.rem(lax.axis_index("section"), 2) == 0
    features = grad_in.shape[0]
    width = features // 2

    for index in range(8):
        block, side = index // 2, index % 2

        @pl.when(attends & (step == index))
        def _():
            if block < 3:
                grad_in[...] = first_ref[side, block * width : (block + 1) * width, :].astype(F32).T
            else:
                for half in range(2):
                    grad_in[half * width : (half + 1) * width, :] = first_ref[
                        half, 3 * width :, side * width : (side + 1) * width
                    ].astype(F32)
            grad_out[...] = jnp.zeros_like(grad_out)

        @pl.when(jnp.logical_not(attends) & (step == index))
        def _():
            owner, piece, cut = index // 4, (index % 4) // 2, index % 2
            rows = slice(piece * features, (piece + 1) * features)
            lanes = slice(cut * width, (cut + 1) * width)
            grad_in[...] = first_ref[owner, rows, lanes].astype(F32)
            grad_out[...] = second_ref[owner, rows, lanes].astype(F32).T

    @pl.when(step == 0)
    def _():
        count = small_ref.shape[0]
        cond = mod_weight_grad.shape[0]
        pairs = [small_ref[2 * i] + small_ref[2 * i + 1] for i in range(count // 2)]
        rows_ref[...] = sum(pairs[1:], pairs[0])
        embedded = jnp.concatenate(embedded_of(small_ref, cond, 0), 0)
        conditions = embedded * (1.0 / (1.0 + jnp.exp(-embedded)))
        for k in range(3):
            rows = jnp.concatenate([pair[3 * m + k : 3 * m + k + 1] for pair in pairs for m in range(MICROS)], 0)
            mod_weight_grad[:, k * features : (k + 1) * features] = lax.dot_general(
                conditions, rows, (((0,), (0,)), ((), ())), precision=HIGH, preferred_element_type=F32
            )


MICROS = 4


def embedded_of(small_ref, cond, group):
    seqs = MICROS // 2
    return [
        small_ref[2 * chip + core, SMALL_ROWS - 4 : SMALL_ROWS - 3, (group * seqs + i) * cond : (group * seqs + i + 1) * cond]
        for chip in range(small_ref.shape[0] // 2)
        for i in range(seqs)
        for core in range(2)
    ]


def place_gradients(first, second, small, cond, hidden):
    features = first.shape[2]
    width = features // 2
    whole = lambda dims: pl.BlockSpec(dims, lambda i: (0,) * len(dims))
    return pl.pallas_call(
        place_kernel,
        grid=(hidden // width,),
        in_specs=[whole(first.shape), whole(second.shape), whole(small.shape)],
        out_specs=[
            pl.BlockSpec((features, width), lambda i: (0, i)),
            pl.BlockSpec((width, features), lambda i: (i, 0)),
            whole((cond, 3 * features)),
            whole((SMALL_ROWS, features)),
        ],
        out_shape=(
            shape((features, hidden), F32),
            shape((hidden, features), F32),
            shape((cond, 3 * features), F32),
            shape((SMALL_ROWS, features), F32),
        ),
        compiler_params=params(),
        name="place_gradients",
    )(first, second, small)


def table_kernel(small_ref, own_ref, one_ref, two_ref, three_ref, table_grad, embed_grad):
    steps, cond = table_grad.shape
    across = own_ref[...] + one_ref[...] + two_ref[...] + three_ref[...]
    count = across.shape[0]
    embed_grad[...] = sum((across[i, 1:2] for i in range(1, count)), across[0, 1:2])
    embedded = jnp.concatenate(embedded_of(small_ref, cond, 0), 0)
    chosen = jnp.concatenate(embedded_of(small_ref, cond, 1), 0)[:, 0:1]
    gradients = []
    for chip in range(count // 2):
        row = across[2 * chip, 0:1] + across[2 * chip + 1, 0:1]
        gradients += [row[:, m * cond : (m + 1) * cond] for m in range(MICROS)]
    squash = 1.0 / (1.0 + jnp.exp(-embedded))
    gradient = jnp.concatenate(gradients, 0) * (squash * (1.0 + embedded * (1.0 - squash)))
    places = lax.broadcasted_iota(jnp.int32, (chosen.shape[0], steps), 1).astype(F32)
    onehot = jnp.where(places == chosen, 1.0, 0.0)
    table_grad[...] = lax.dot_general(
        onehot, gradient, (((0,), (0,)), ((), ())), precision=HIGH, preferred_element_type=F32
    )


def table_gradients(small, across, steps, cond):
    return pl.pallas_call(
        table_kernel,
        out_shape=(shape((steps, cond), F32), shape((1, small.shape[2]), F32)),
        compiler_params=params(),
        name="table_gradients",
    )(small, *across)


def rope_tables(length):
    position = np.arange(length, dtype=np.float32)[None, :]
    column = np.arange(HALF, dtype=np.float32)[:, None]
    angles = position * np.exp(column * np.float32(-2.0 * math.log(10000.0) / HEAD))
    return jnp.asarray(np.cos(angles)), jnp.asarray(np.sin(angles))


def shards(
    tokens, span_start, span_length, time_step, time_table, mask_embed, mod_weight, mod_bias,
    norm_gain, in_weight, in_bias, out_weight, out_bias, cotangent,
):
    sections = lax.axis_size("section")
    dp_count = lax.axis_size("dp")
    seqs, length, features = tokens.shape
    micros = 2 * seqs
    hidden = in_weight.shape[2]
    steps, cond = time_table.shape
    cosine, sine = rope_tables(length)
    states, stream, kept_first, kept_second, kept_rows, back_first, back_second, sums, bias = pipeline(
        tokens, cotangent, in_weight[0], out_weight[0], span_start, span_length, time_step, time_table,
        mask_embed[None], mod_weight[0], mod_bias, norm_gain, in_bias, out_bias, cosine, sine,
    )
    summed_first, summed_second, small = summed_gradients(
        kept_first, kept_second, kept_rows, back_first, back_second, sums, bias, mod_weight[0], dp_count
    )
    base = 3 * micros
    blocks = hidden // features
    across = small[:, base + blocks + 2 : base + blocks + 4]
    turns = [
        lax.ppermute(across, "section", [(s, (s + turn) % sections) for s in range(sections)])
        for turn in range(1, sections)
    ]
    grad_in, grad_out, grad_mod_weight, rows = place_gradients(summed_first, summed_second, small, cond, hidden)
    table_total, embed_total = table_gradients(small, [across] + turns, steps, cond)
    grad_mod_bias = jnp.sum(rows[:base].reshape(micros, 3 * features), 0)
    return (
        states[None],
        stream[None],
        table_total,
        embed_total[0],
        grad_mod_weight[None],
        grad_mod_bias[None],
        rows[base][None],
        grad_in[None],
        rows[base + 1 : base + 1 + blocks].reshape(1, hidden),
        grad_out[None],
        rows[base + 1 + blocks][None],
    )


def solution(mesh):
    placed = (
        P("dp", None, None),
        P("dp"),
        P("dp"),
        P("dp"),
        P(),
        P(),
        P("section", None, None),
        P("section", None),
        P("section", None),
        P("section", None, None),
        P("section", None),
        P("section", None, None),
        P("section", None),
        P("dp", None, None),
    )
    return jax.shard_map(
        shards,
        mesh=mesh,
        in_specs=placed,
        out_specs=(
            P("section", "dp", None, None),
            P("section", "dp", None, None),
            P(),
            P(),
            P("section", None, None),
            P("section", None),
            P("section", None),
            P("section", None, None),
            P("section", None),
            P("section", None, None),
            P("section", None),
        ),
        check_vma=False,
    )
```

```python
import math

import jax
import jax.numpy as jnp
import numpy as np
from jax import lax
from jax.experimental import pallas as pl
from jax.experimental.pallas import tpu as pltpu
from jax.sharding import PartitionSpec as P

HEAD = 64
HALF = HEAD // 2
EPS = 1e-06
HIGH = lax.Precision.HIGHEST
F32 = jnp.float32
BF16 = jnp.bfloat16
SCALE = HEAD ** (-0.5)
EXP2_SCALE = SCALE * math.log2(math.e)
GELU_C = math.sqrt(2.0 / math.pi)
VMEM_LIMIT = 56 << 20


def dot_nn(left, right):
    return jnp.dot(left, right, preferred_element_type=F32)


def dot_nt(left, right):
    return lax.dot_general(left, right, (((1,), (1,)), ((), ())), preferred_element_type=F32)


def params(**more):
    return pltpu.CompilerParams(vmem_limit_bytes=VMEM_LIMIT, **more)


def shape(dims, dtype):
    return jax.ShapeDtypeStruct(dims, dtype)


def normalize(rows):
    average = jnp.mean(rows, -1, keepdims=True)
    centered = rows - average
    inverse_std = lax.rsqrt(jnp.mean(centered * centered, -1, keepdims=True) + EPS)
    return centered * inverse_std, inverse_std


MESH = pl.DeviceIdType.MESH
PARTS = 2
CUTS = 4


def pipeline_kernel(
    tokens_ref, cot_ref, first_ref, second_ref, start_ref, length_ref, step_ref, table_ref, embed_ref,
    mod_weight_ref, mod_bias_ref, gain_ref, bias_row_ref, out_bias_ref, cos_ref, sin_ref,
    states_ref, stream_ref, kept_first, kept_second, kept_rows, back_first, back_second, kept_spread, sums_ref, bias_ref,
    weights, streams, pool, upstreams, mixed_got, first_buf, second_buf, branches, leaving,
    mixed_own, mixed_send, grad_send, grad_own, spreads, bias_columns, mods_ref,
    load_sem, pass_send, pass_recv, back_recv, swap_send, swap_recv, place_send, place_recv, store_sem, fetch_sem,
    local_sem, give_send, give_recv, mod_send, mod_recv, mixed_give, mixed_take, grad_give, grad_take, spread_sem,
):
    section = lax.axis_index("section")
    sections = lax.axis_size("section")
    dp_index = lax.axis_index("dp")
    core = lax.rem(dp_index, 2)
    partner = dp_index + 1 - 2 * core
    micros, half, features = streams.shape
    width = mixed_own.shape[1]
    heads = width // HEAD
    length = 2 * half
    part_rows = half // PARTS
    cut_rows = half // CUTS
    attends = lax.rem(section, 2) == 0
    feeds = lax.rem(section, 2) == 1
    is_first = section == 0
    is_last = section == sections - 1
    hidden = second_ref.shape[0]
    blocks = hidden // features
    seqs = micros // 2
    cond = table_ref.shape[1]
    feed_step = half
    feed_parts = hidden // feed_step
    near = pl.ds(core * half, half)
    far = pl.ds((1 - core) * half, half)

    barrier = pltpu.get_barrier_semaphore()
    pl.semaphore_signal(barrier, inc=1, device_id=(partner, section), device_id_type=MESH)

    @pl.when(section > 0)
    def _():
        pl.semaphore_signal(barrier, inc=1, device_id=(dp_index, section - 1), device_id_type=MESH)

    @pl.when(section < sections - 1)
    def _():
        pl.semaphore_signal(barrier, inc=1, device_id=(dp_index, section + 1), device_id_type=MESH)

    def head_loads():
        copies = []
        for block in range(3):
            lanes = pl.ds(pl.multiple_of(block * features + core * width, 128), width)
            target = pl.ds(block * width, width)
            copies.append((first_ref.at[pl.ds(0, half), lanes], first_buf.at[0, :, target]))
            copies.append(
                (first_ref.at[pl.ds(half, features - half), lanes], first_buf.at[1, pl.ds(0, features - half), target])
            )
        for side in range(2):
            rows = pl.ds(pl.multiple_of((core if side == 0 else 1 - core) * width, 16), width)
            copies.append(
                (first_ref.at[rows, pl.ds(3 * features, features)], weights.at[pl.ds((3 + side) * width, width)])
            )
        return [pltpu.make_async_copy(*copy, load_sem.at[i]) for i, copy in enumerate(copies)]

    def pool_at(slot):
        return pool.at[pl.ds(pl.multiple_of(slot * half, 16), half)]

    def others_at(micro):
        return pool_at(micro)

    def up_others_at(micro):
        return pool_at(micros + micro)

    def feed_loads():
        copies = [
            (first_ref.at[:, pl.ds(block * features, features)], weights.at[pl.ds(block * features, features)])
            for block in range(blocks)
        ]
        copies += [
            (second_ref.at[pl.ds(part * feed_step, feed_step)], pool_at(part)) for part in range(feed_parts)
        ]
        return [pltpu.make_async_copy(*copy, load_sem.at[i]) for i, copy in enumerate(copies)]

    def token_copies(i):
        micro = 2 * i + core
        return [
            pltpu.make_async_copy(tokens_ref.at[i, near], streams.at[micro], local_sem.at[i, 0]),
            pltpu.make_async_copy(tokens_ref.at[i, far], others_at(micro), local_sem.at[i, 1]),
        ]

    def token_gives(i):
        micro = 2 * i + core
        return [
            pltpu.make_async_remote_copy(
                tokens_ref.at[i, rows], target, give_send.at[i, k], give_recv.at[i, k],
                device_id=(partner, section), device_id_type=MESH,
            )
            for k, (rows, target) in enumerate(((far, streams.at[micro]), (near, others_at(micro))))
        ]

    def cot_copy(i):
        return pltpu.make_async_copy(cot_ref.at[i, near], upstreams.at[2 * i + core], local_sem.at[i, 0])

    def cot_give(i):
        return pltpu.make_async_remote_copy(
            cot_ref.at[i, far], upstreams.at[2 * i + core], give_send.at[i, 0], give_recv.at[i, 0],
            device_id=(partner, section), device_id_type=MESH,
        )

    def mod_give(i):
        block = mods_ref.at[2 * i + core]
        return pltpu.make_async_remote_copy(
            block, block, mod_send.at[i], mod_recv.at[i], device_id=(partner, section), device_id_type=MESH
        )

    @pl.when(is_first)
    def _():
        for i in range(seqs):
            for copy in token_copies(i):
                copy.start()

    @pl.when(attends)
    def _():
        for copy in head_loads():
            copy.start()

    @pl.when(feeds)
    def _():
        for copy in feed_loads():
            copy.start()

    @pl.when(is_last)
    def _():
        for i in range(seqs):
            cot_copy(i).start()

    bias_ref[...] = jnp.zeros_like(bias_ref)
    bias_columns[...] = jnp.zeros_like(bias_columns)
    looked_up = [table_ref[pl.ds(step_ref[i], 1), :] for i in range(seqs)]
    embedded = jnp.concatenate(looked_up + [jnp.zeros((8 - seqs, cond), F32)], 0)
    condition = embedded * (1.0 / (1.0 + jnp.exp(-embedded)))
    modulations = mod_bias_ref[...] + lax.dot_general(
        condition, mod_weight_ref[...], (((1,), (0,)), ((), ())), precision=HIGH, preferred_element_type=F32
    )
    for i in range(seqs):
        chosen = jnp.broadcast_to(step_ref[i].astype(F32), (1, cond))
        for side in range(2):
            row = slice(2 + side, 3 + side)
            bias_ref[row, i * cond : (i + 1) * cond] = jnp.where(core == side, looked_up[i], 0.0)
            bias_ref[row, (seqs + i) * cond : (seqs + i + 1) * cond] = jnp.where(core == side, chosen, 0.0)
        begin = jnp.broadcast_to(start_ref[i].astype(F32), (1, features))
        end = jnp.broadcast_to((start_ref[i] + length_ref[i]).astype(F32), (1, features))
        mods_ref[2 * i + core] = jnp.concatenate(
            [modulations[i : i + 1, k * features : (k + 1) * features] for k in range(3)]
            + [begin, end, jnp.zeros((3, features), F32)],
            0,
        )

    pl.semaphore_wait(
        barrier, 1 + jnp.where(section > 0, 1, 0) + jnp.where(section < sections - 1, 1, 0)
    )
    for i in range(seqs):
        mod_give(i).start()

        if i == 0:

            @pl.when(is_first)
            def _():
                for copy in token_gives(i):
                    copy.start()

        @pl.when(is_last)
        def _():
            cot_give(i).start()

    @pl.when(attends)
    def _():
        for copy in head_loads():
            copy.wait()
        for block in range(3):
            lanes = slice(block * width, (block + 1) * width)
            weights[lanes, :half] = first_buf[0, :, lanes].T
            weights[lanes, half:] = first_buf[1, : features - half, lanes].T
            at = pl.multiple_of(block * features + core * width, 128)
            bias = jnp.broadcast_to(bias_row_ref[:, pl.ds(at, width)], (8, width)).T
            bias_columns[block, :, 8:16] = bias

    @pl.when(feeds)
    def _():
        for copy in feed_loads():
            copy.wait()

    def cut_at(part):
        return pl.ds(pl.multiple_of(part * cut_rows, 16), cut_rows)

    def each_cut(body):
        def one(part, carried):
            body(part, cut_at(part))
            return carried

        lax.fori_loop(0, CUTS, one, 0)

    def rows_of(part):
        return slice(part * part_rows, (part + 1) * part_rows)

    def schedule(step):
        turns = jnp.where(is_last, 1, 0)
        forward = jnp.where(is_last, 1 - lax.rem(step, 2), jnp.where(step < micros, 1, 0))
        micro = jnp.where(is_last, step // 2, lax.rem(step, micros))
        del turns
        return forward == 1, micro

    def pass_on(step, part, micro, forward):
        slot = lax.rem(step, 2)
        rows = cut_at(part)
        source = leaving.at[slot, rows]
        if forward:
            return pltpu.make_async_remote_copy(
                source, streams.at[micro, rows],
                pass_send.at[slot, part], pass_recv.at[micro, part],
                device_id=(dp_index, section + 1), device_id_type=MESH,
            )
        return pltpu.make_async_remote_copy(
            source, upstreams.at[micro, rows],
            pass_send.at[slot, part], back_recv.at[micro, part],
            device_id=(dp_index, section - 1), device_id_type=MESH,
        )

    def place_target(target, micro):
        return target.at[micro // 2, pl.ds(core * half, half)]

    def place_local(step, micro, target):
        slot = lax.rem(step, 2)
        return pltpu.make_async_copy(leaving.at[slot], place_target(target, micro), place_send.at[slot])

    def place_remote(step, micro, target, index):
        slot = lax.rem(step, 2)
        return pltpu.make_async_remote_copy(
            leaving.at[slot], place_target(target, micro), place_send.at[slot],
            place_recv.at[index, micro // 2], device_id=(partner, section), device_id_type=MESH,
        )

    def send_part(step, part, micro, forward):
        reaches = section < sections - 1 if forward else section > 0

        @pl.when(reaches)
        def _():
            pass_on(step, part, micro, forward).start()

    def place_result(step, micro, forward):
        target, index = (states_ref, 0) if forward else (stream_ref, 1)
        mine = lax.rem(micro, 2) == core

        @pl.when(mine)
        def _():
            place_local(step, micro, target).start()

        @pl.when(jnp.logical_not(mine))
        def _():
            place_remote(step, micro, target, index).start()

    def leaving_free(step):
        was_forward, micro = schedule(step)
        mine = lax.rem(micro, 2) == core
        for forward, cond in ((True, was_forward), (False, jnp.logical_not(was_forward))):
            reaches = section < sections - 1 if forward else section > 0
            target, index = (states_ref, 0) if forward else (stream_ref, 1)

            @pl.when(cond & reaches)
            def _():
                for part in range(CUTS):
                    pass_on(step, part, micro, forward).wait_send()

            @pl.when(cond & mine)
            def _():
                place_local(step, micro, target).wait()

            @pl.when(cond & jnp.logical_not(mine))
            def _():
                place_remote(step, micro, target, index).wait_send()

    def swap(kind, part, source, target, micro):
        rows = cut_at(part)
        return pltpu.make_async_remote_copy(
            source.at[rows], target.at[rows], swap_send.at[kind, part], swap_recv.at[kind, part, micro],
            device_id=(partner, section), device_id_type=MESH,
        )

    def give_mixed(pair, micro):
        lanes = pl.ds(pl.multiple_of(pair * 2 * HEAD, 2 * HEAD), 2 * HEAD)
        return pltpu.make_async_remote_copy(
            mixed_send.at[:, lanes], mixed_got.at[micro, :, lanes],
            mixed_give.at[pair], mixed_take.at[pair, micro],
            device_id=(partner, section), device_id_type=MESH,
        )

    def give_grad(part, micro):
        rows = pl.ds(part * part_rows, part_rows)
        return pltpu.make_async_remote_copy(
            grad_send.at[rows], others_at(micro).at[rows], grad_give.at[part], grad_take.at[part, micro],
            device_id=(partner, section), device_id_type=MESH,
        )

    def store_first(slot, target, micro):
        return pltpu.make_async_copy(first_buf.at[slot], target.at[micro], store_sem.at[slot])

    def store_second(target, micro):
        lanes = pl.ds(0, 2 * features)
        return pltpu.make_async_copy(second_buf.at[:, lanes], target.at[micro, :, lanes], store_sem.at[2])

    def store_active(micro):
        return pltpu.make_async_copy(second_buf, kept_second.at[micro], store_sem.at[2])

    def store_grad_branch(micro):
        return pltpu.make_async_copy(
            grad_send, back_second.at[micro, :, pl.ds(0, features)], store_sem.at[3]
        )

    def rows_kept(micro):
        return pool_at(feed_parts + lax.rem(micro, 2))

    def store_rows(micro):
        return pltpu.make_async_copy(
            rows_kept(micro), kept_rows.at[micro], store_sem.at[4 + lax.rem(micro, 2)]
        )

    pairs = heads // 2

    def spread_slot(pair, micro):
        return lax.rem(micro * pairs + pair, 2)

    def spread_store(pair, micro):
        slot = spread_slot(pair, micro)
        return pltpu.make_async_copy(
            spreads.at[slot], kept_spread.at[micro, pl.ds(2 * pair, 2)], spread_sem.at[slot]
        )

    def spread_fetch(pair, micro):
        slot = spread_slot(pair, micro)
        return pltpu.make_async_copy(
            kept_spread.at[micro, pl.ds(2 * pair, 2)], spreads.at[slot], spread_sem.at[slot]
        )

    def first_slot_free(slot, when):
        @pl.when(when)
        def _():
            store_first(slot, kept_first, 0).wait()

    def arrive(micro, part, forward):
        @pl.when(jnp.logical_not(is_first if forward else is_last))
        def _():
            pass_on(0, part, micro, forward).wait_recv()

    def arrive_cot(micro):
        mine = lax.rem(micro, 2) == core

        @pl.when(is_last & mine)
        def _():
            cot_copy(micro // 2).wait()

        @pl.when(is_last & jnp.logical_not(mine))
        def _():
            cot_give(micro // 2).wait_recv()

    def arrive_mod(micro):
        @pl.when(lax.rem(micro, 2) != core)
        def _():
            mod_give(micro // 2).wait_recv()

    def in_span(micro, begin, count):
        bounds = mods_ref[micro, 3:5, 0:1]
        position = (lax.broadcasted_iota(jnp.int32, (count, 1), 0) + begin).astype(F32)
        return (position >= bounds[0:1]) & (position < bounds[1:2])

    def arrive_tokens(micro, k):
        mine = lax.rem(micro, 2) == core

        @pl.when(mine)
        def _():
            token_copies(micro // 2)[k].wait()

        @pl.when(jnp.logical_not(mine))
        def _():
            token_gives(micro // 2)[k].wait_recv()

        target, side = (streams.at[micro], core) if k == 0 else (others_at(micro), 1 - core)
        for part in range(PARTS):
            rows = rows_of(part)
            span = in_span(micro, side * half + part * part_rows, part_rows)
            target[rows, :] = jnp.where(span, embed_ref[...], target[rows, :])

    def exchange(part, micro):
        return swap(1, part, upstreams.at[micro], up_others_at(micro), micro)

    def exchange_start(micro):
        for part in range(CUTS):
            arrive(micro, part, False)
            exchange(part, micro).start()

    def attention_forward(step, micro):
        arrive_mod(micro)
        mod = mods_ref[micro]
        gain = gain_ref[...]
        slot = lax.rem(micro, 2)
        later = jnp.logical_not(is_first)

        @pl.when(is_first)
        def _():
            arrive_tokens(micro, 0)

        @pl.when(later)
        def _():
            for part in range(CUTS):
                arrive(micro, part, True)
                swap(0, part, streams.at[micro], others_at(micro), micro).start()

        first_slot_free(slot, step >= 2)

        @pl.when(step > 0)
        def _():
            store_second(kept_second, micro).wait()

        def project(source, part):
            standard, _ = normalize(source[rows_of(part % PARTS), :].astype(F32))
            rows = (standard * gain * (1.0 + mod[1:2]) + mod[0:1]).astype(BF16)
            place = (part // PARTS) * features
            second_buf[rows_of(part % PARTS), place : place + features] = rows
            projected = dot_nt(weights[: 3 * width, :], rows)
            side = core if part < PARTS else 1 - core
            columns = pl.ds(pl.multiple_of(side * half + (part % PARTS) * part_rows, 128), part_rows)
            cosine = cos_ref[:, columns]
            sine = sin_ref[:, columns]
            for block in range(3):
                lanes = slice(block * length + part * part_rows, block * length + (part + 1) * part_rows)
                biased = projected[block * width : (block + 1) * width] + bias_columns[block, :, 8:9]
                if block == 2:
                    first_buf[slot, :width, lanes] = biased.astype(BF16)
                    continue
                for head in range(heads):
                    base = head * HEAD
                    front = biased[base : base + HALF]
                    back = biased[base + HALF : base + HEAD]
                    at = head * HEAD
                    first_buf[slot, at : at + HALF, lanes] = (front * cosine - back * sine).astype(BF16)
                    first_buf[slot, at + HALF : at + HEAD, lanes] = (back * cosine + front * sine).astype(BF16)

        for part in range(PARTS):
            project(streams.at[micro], part)

        @pl.when(is_first)
        def _():
            arrive_tokens(micro, 1)

            @pl.when(step == 0)
            def _():
                for i in range(1, seqs):
                    for copy in token_gives(i):
                        copy.start()

        @pl.when(later)
        def _():
            for part in range(CUTS):
                swap(0, part, streams.at[micro], others_at(micro), micro).wait_recv()

        for part in range(PARTS, 2 * PARTS):
            project(others_at(micro), part)

        def scores_of(head):
            base = pl.multiple_of(head * HEAD, HEAD)
            key_rows = first_buf[slot, pl.ds(base, HEAD), length : 2 * length].T
            return dot_nn(key_rows, first_buf[slot, pl.ds(base, HEAD), :length])

        def finish(head, within, scores, kept):
            base = pl.multiple_of(head * HEAD, HEAD)
            top = jnp.max(scores, 0, keepdims=True) * EXP2_SCALE
            spread = jnp.exp2(scores * EXP2_SCALE - top)
            spread = (spread * (1.0 / jnp.sum(spread, 0, keepdims=True))).astype(BF16)
            spreads[kept, within] = spread
            return dot_nn(first_buf[slot, pl.ds(base, HEAD), 2 * length :], spread).astype(BF16)

        def head_pair(pair, carried):
            kept = spread_slot(pair, micro)

            @pl.when(micro * pairs + pair >= 2)
            def _():
                spread_store(pair, micro).wait()

            scores = scores_of(2 * pair), scores_of(2 * pair + 1)
            mixed = jnp.concatenate([finish(2 * pair + i, i, scores[i], kept) for i in range(2)], 0)
            spread_store(pair, micro).start()
            at = pl.multiple_of(pair * length, length)
            first_buf[slot, width:, pl.ds(at, length)] = mixed
            turned = mixed.T
            lanes = pl.multiple_of(pair * 2 * HEAD, 2 * HEAD)
            mixed_own[:, pl.ds(lanes, 2 * HEAD)] = turned[:half]
            mixed_send[:, pl.ds(lanes, 2 * HEAD)] = turned[half:]
            give_mixed(pair, micro).start()
            return carried

        lax.fori_loop(0, heads // 2, head_pair, 0)
        store_first(slot, kept_first, micro).start()
        store_second(kept_second, micro).start()

        @pl.when(later & (step == micros - 1))
        def _():
            exchange_start(0)

        @pl.when(step >= 2)
        def _():
            leaving_free(step - 2)

        for pair in range(heads // 2):
            give_mixed(pair, micro).wait_recv()
        def out_cut(part, rows):
            mixed = jnp.concatenate([mixed_own[rows, :], mixed_got[micro, rows, :]], 1)
            branch = dot_nn(mixed, weights[3 * width : 5 * width, :]) + bias_row_ref[:, 3 * features :]
            branches[micro, rows, :] = branch.astype(BF16)
            result = streams[micro, rows, :].astype(F32) + mod[2:3] * branch
            leaving[lax.rem(step, 2), rows, :] = result.astype(BF16)
            send_part(step, part, micro, True)

        each_cut(out_cut)
        place_result(step, micro, True)
        for pair in range(heads // 2):
            give_mixed(pair, micro).wait_send()

        @pl.when(later)
        def _():
            for part in range(CUTS):
                swap(0, part, streams.at[micro], others_at(micro), micro).wait_send()

    pieces = [(block, lane) for block in range(blocks) for lane in range(0, features, part_rows)]

    def feed_forward(step, micro):
        arrive_mod(micro)
        mod = mods_ref[micro]
        gain = gain_ref[...]

        slot = jnp.where(is_last, 0, lax.rem(micro, 2))
        first_slot_free(slot, jnp.logical_not(is_last) & (micro >= 2))

        @pl.when(micro >= 1)
        def _():
            store_active(micro).wait()

        @pl.when(micro >= 2)
        def _():
            store_rows(micro).wait()

        @pl.when(step >= 2)
        def _():
            leaving_free(step - 2)

        entering_rows = rows_kept(micro)
        def feed_cut(part, rows):
            arrive(micro, part, True)
            standard, _ = normalize(streams[micro, rows, :].astype(F32))
            entering = (standard * gain * (1.0 + mod[1:2]) + mod[0:1]).astype(BF16)
            entering_rows[rows, :] = entering
            for piece, (block, lane) in enumerate(pieces):
                lanes = slice(piece * part_rows, (piece + 1) * part_rows)
                value = (
                    dot_nn(entering, weights[block * features : (block + 1) * features, lane : lane + part_rows])
                    + bias_row_ref[:, lanes]
                )
                square = value * value
                bend = jnp.tanh(GELU_C * value * (1.0 + 0.044715 * square))
                raised = 0.5 + 0.5 * bend
                second_buf[rows, lanes] = (value * raised).astype(BF16)
                first_buf[slot, rows, lanes] = (
                    raised + (0.5 * GELU_C) * value * (1.0 - bend * bend) * (1.0 + (3 * 0.044715) * square)
                ).astype(BF16)
            branch = dot_nn(second_buf[rows, :], pool[:hidden, :]) + out_bias_ref[...]
            branches[micro, rows, :] = branch.astype(BF16)
            result = streams[micro, rows, :].astype(F32) + mod[2:3] * branch
            leaving[lax.rem(step, 2), rows, :] = result.astype(BF16)
            send_part(step, part, micro, True)

        each_cut(feed_cut)
        place_result(step, micro, True)
        store_active(micro).start()
        store_rows(micro).start()

        @pl.when(jnp.logical_not(is_last))
        def _():
            store_first(slot, kept_first, micro).start()

    def fetch_kept(micro):
        return pltpu.make_async_copy(kept_first.at[micro], first_buf.at[0], fetch_sem.at[0])

    def attention_backward(step, micro):
        mod = mods_ref[micro]
        store_second(kept_second, micro).wait()
        first_slot_free(1, step >= micros)

        @pl.when(step == micros)
        def _():
            store_first(0, kept_first, 0).wait()
            fetch_kept(micro).start()
            for pair in range(pairs - 2, pairs):
                spread_store(pair, micros - 1).wait()
            spread_fetch(0, 0).start()

        @pl.when(is_first)
        def _():
            exchange_start(micro)

        grad_mixed_at = 2 * features

        def into_heads(source, part):
            grad_branch = (mod[2:3] * source[rows_of(part % PARTS), :].astype(F32)).astype(BF16)
            place = (part // PARTS) * features
            second_buf[rows_of(part % PARTS), place : place + features] = grad_branch
            if part < PARTS:
                bias_ref[0:1, 3 * features :] += jnp.sum(grad_branch.astype(F32), 0, keepdims=True)
            lanes = slice(grad_mixed_at + part * part_rows, grad_mixed_at + (part + 1) * part_rows)
            second_buf[:width, lanes] = dot_nt(weights[3 * width : 4 * width, :], grad_branch).astype(BF16)

        for part in range(PARTS):
            into_heads(upstreams.at[micro], part)

        @pl.when(step > micros)
        def _():
            finish_attention(step - 1, micro - 1)

        for part in range(CUTS):
            exchange(part, micro).wait_recv()
        for part in range(PARTS, 2 * PARTS):
            into_heads(up_others_at(micro), part)
        fetch_kept(micro).wait()
        near_lanes = pl.ds(pl.multiple_of(core * half, 128), half)
        far_lanes = pl.ds(pl.multiple_of((1 - core) * half, 128), half)
        cosine = jnp.concatenate([cos_ref[:, near_lanes], cos_ref[:, far_lanes]], 1)
        sine = jnp.concatenate([sin_ref[:, near_lanes], sin_ref[:, far_lanes]], 1)

        def turn_back(base, block, gradient):
            front = gradient[:HALF] * SCALE
            back = gradient[HALF:] * SCALE
            turned = jnp.concatenate([front * cosine + back * sine, back * cosine - front * sine], 0)
            put_back(base, block, turned.astype(BF16))

        def put_back(base, block, gradient):
            first_buf[1, pl.ds(base, HEAD), block * length : (block + 1) * length] = gradient
            bias_columns[block, pl.ds(base, HEAD), 0:1] += jnp.sum(gradient.astype(F32), 1, keepdims=True)

        def one_head(head, within, mixed, kept):
            base = pl.multiple_of(head * HEAD, HEAD)
            query = first_buf[0, pl.ds(base, HEAD), :length]
            key = first_buf[0, pl.ds(base, HEAD), length : 2 * length]
            spread = spreads[kept, within]
            value = first_buf[0, pl.ds(base, HEAD), 2 * length :]
            grad_mixed = second_buf[pl.ds(base, HEAD), grad_mixed_at : grad_mixed_at + length]
            delta = jnp.sum(grad_mixed.astype(F32) * mixed.astype(F32), 0, keepdims=True)
            grad_spread = dot_nn(value.T, grad_mixed)
            grad_scores = (spread.astype(F32) * (grad_spread - delta)).astype(BF16)
            grad_value = dot_nn(spread, grad_mixed.T)
            grad_key = dot_nn(grad_scores, query.T)
            grad_query = dot_nn(key, grad_scores)
            turn_back(base, 0, grad_query)
            turn_back(base, 1, grad_key.T)
            put_back(base, 2, grad_value.T.astype(BF16))

        def head_pair(pair, carried):
            at = pl.multiple_of(pair * length, length)
            mixed = first_buf[0, width:, pl.ds(at, length)]
            spread_fetch(pair, micro).wait()
            ends = pair == pairs - 1

            @pl.when(jnp.logical_not(ends & (micro == micros - 1)))
            def _():
                spread_fetch(jnp.where(ends, 0, pair + 1), jnp.where(ends, micro + 1, micro)).start()

            kept = spread_slot(pair, micro)
            one_head(2 * pair, 0, mixed[:HEAD], kept)
            one_head(2 * pair + 1, 1, mixed[HEAD:], kept)
            return carried

        lax.fori_loop(0, heads // 2, head_pair, 0)

        for part in range(CUTS):
            exchange(part, micro).wait_send()

        @pl.when(step + 1 < 2 * micros)
        def _():
            fetch_kept(micro + 1).start()

            @pl.when(jnp.logical_not(is_first))
            def _():
                exchange_start(micro + 1)

        def grad_rows_of(part):
            begin = part * part_rows
            heads_of = [
                first_buf[1, :width, block * length + begin : block * length + begin + part_rows] for block in range(3)
            ]
            return dot_nn(jnp.concatenate(heads_of, 0).T, weights[: 3 * width, :])

        for part in range(PARTS):
            grad_send[rows_of(part), :] = grad_rows_of(PARTS + part).astype(BF16)
            give_grad(part, micro).start()
        store_first(1, back_first, micro).start()
        store_second(back_second, micro).start()
        for part in range(PARTS):
            grad_own[rows_of(part), :] = grad_rows_of(part)

    def finish_attention(step, micro):
        mod = mods_ref[micro]
        gain = gain_ref[...]
        leaving_free(step - 2)
        given = others_at(micro)
        sums_ref[micro] = jnp.zeros((8, features), F32)

        def finish_cut(part, rows):
            @pl.when(lax.rem(part, CUTS // PARTS) == 0)
            def _():
                give_grad(part // (CUTS // PARTS), micro).wait_recv()

            finish_back(
                grad_own[rows, :] + given[rows, :].astype(F32),
                streams[micro, rows, :].astype(F32),
                upstreams[micro, rows, :].astype(F32),
                branches[micro, rows, :].astype(F32),
                mod, gain,
                jnp.logical_not(in_span(micro, core * half + part * cut_rows, cut_rows) & is_first),
                leaving, (lax.rem(step, 2), rows), sums_ref, micro,
            )
            send_part(step, part, micro, False)

        each_cut(finish_cut)
        place_result(step, micro, False)
        for part in range(PARTS):
            give_grad(part, micro).wait_send()

    def feed_backward(step, micro):
        mod = mods_ref[micro]
        gain = gain_ref[...]
        inner = jnp.logical_not(is_last)

        @pl.when(inner & (step == micros))
        def _():
            store_first(0, kept_first, 0).wait()
            store_first(1, kept_first, 0).wait()
            fetch_kept(micro).start()

        @pl.when(micro >= 1)
        def _():
            store_first(1, back_first, 0).wait()
            store_grad_branch(micro).wait()

        @pl.when(step >= 2)
        def _():
            leaving_free(step - 2)

        @pl.when(inner)
        def _():
            fetch_kept(micro).wait()

        arrive_cot(micro)
        sums_ref[micro] = jnp.zeros((8, features), F32)

        def feed_cut(part, rows):
            arrive(micro, part, False)
            upstream = upstreams[micro, rows, :].astype(F32)
            grad_branch = (mod[2:3] * upstream).astype(BF16)
            grad_send[rows, :] = grad_branch
            bias_ref[1:2, :features] += jnp.sum(grad_branch.astype(F32), 0, keepdims=True)
            for piece in range(len(pieces)):
                lanes = slice(piece * part_rows, (piece + 1) * part_rows)
                grad_active = dot_nt(grad_branch, pool[lanes, :])
                grad_hidden = (grad_active * first_buf[0, rows, lanes].astype(F32)).astype(BF16)
                first_buf[1, rows, lanes] = grad_hidden
                bias_ref[0:1, lanes] += jnp.sum(grad_hidden.astype(F32), 0, keepdims=True)
            total = None
            for block in range(blocks):
                lanes = slice(block * features, (block + 1) * features)
                term = dot_nt(first_buf[1, rows, lanes], weights[lanes, :])
                total = term if total is None else total + term
            finish_back(
                total,
                streams[micro, rows, :].astype(F32),
                upstream,
                branches[micro, rows, :].astype(F32),
                mod, gain, None,
                leaving, (lax.rem(step, 2), rows), sums_ref, micro,
            )
            send_part(step, part, micro, False)

        each_cut(feed_cut)
        place_result(step, micro, False)
        store_first(1, back_first, micro).start()
        store_grad_branch(micro).start()

        @pl.when(inner & (step + 1 < 2 * micros))
        def _():
            fetch_kept(micro + 1).start()

    def one_step(step, carried):
        forward, micro = schedule(step)
        backward = jnp.logical_not(forward)

        @pl.when(attends & forward)
        def _():
            attention_forward(step, micro)

        @pl.when(attends & backward)
        def _():
            attention_backward(step, micro)

        @pl.when(feeds & forward)
        def _():
            feed_forward(step, micro)

        @pl.when(feeds & backward)
        def _():
            feed_backward(step, micro)

        return carried

    lax.fori_loop(0, 2 * micros, one_step, 0)

    @pl.when(attends)
    def _():
        finish_attention(2 * micros - 1, micros - 1)
        for block in range(3):
            at = pl.multiple_of(block * features + core * width, 128)
            bias_ref[0:1, pl.ds(at, width)] = bias_columns[block].T[0:1]

    store_first(1, back_first, 0).wait()

    @pl.when(attends)
    def _():
        store_second(back_second, 0).wait()

    @pl.when(feeds)
    def _():
        store_active(0).wait()
        store_grad_branch(0).wait()
        store_rows(0).wait()
        store_rows(1).wait()

    leaving_free(2 * micros - 2)
    leaving_free(2 * micros - 1)
    for i in range(seqs):
        mod_give(i).wait_send()

        @pl.when(is_first)
        def _():
            for copy in token_gives(i):
                copy.wait_send()

        @pl.when(is_last)
        def _():
            cot_give(i).wait_send()

    for index, target in enumerate((states_ref, stream_ref)):
        for slot in range(micros // 2):
            pltpu.make_async_remote_copy(
                leaving.at[0], target.at[slot, pl.ds((1 - core) * half, half)], place_send.at[0],
                place_recv.at[index, slot], device_id=(partner, section), device_id_type=MESH,
            ).wait_recv()


def finish_back(
    grad_rows, stream, upstream, branch, mod, gain, keep, leaving, place, sums_ref, micro,
):
    standard, inverse_std = normalize(stream)
    scaling = mod[1:2, :]
    grad_normed = grad_rows * (1.0 + scaling)
    grad_hat = grad_normed * gain
    grad_stream = upstream + inverse_std * (
        grad_hat
        - jnp.mean(grad_hat, -1, keepdims=True)
        - standard * jnp.mean(grad_hat * standard, -1, keepdims=True)
    )
    row_sum = lambda value: jnp.sum(value, 0, keepdims=True)
    with_standard = row_sum(grad_rows * standard)
    sums = [
        row_sum(grad_rows),
        with_standard * gain,
        row_sum(upstream * branch),
        with_standard * (1.0 + scaling),
    ]
    slot, rows = place
    if keep is None:
        sums.append(jnp.zeros_like(sums[0]))
        leaving[slot, rows, :] = grad_stream.astype(BF16)
    else:
        kept = jnp.where(keep, grad_stream, 0.0)
        sums.append(row_sum(grad_stream - kept))
        leaving[slot, rows, :] = kept.astype(BF16)
    sums = jnp.concatenate(sums + [jnp.zeros((3, sums[0].shape[1]), F32)], 0)
    sums_ref[micro] += sums


def pipeline(
    tokens, cot, first, second, span_start, span_length, time_step, table, embed, mod_weight, mod_bias, gain,
    bias_row, out_bias, cosine, sine,
):
    seqs, length, features = tokens.shape
    micros = 2 * seqs
    half = length // 2
    width = features // 2
    hidden = second.shape[0]
    anywhere = pl.BlockSpec(memory_space=pl.ANY)
    inside = pl.BlockSpec(memory_space=pltpu.VMEM)
    scalars = pl.BlockSpec(memory_space=pltpu.SMEM)
    dma = pltpu.SemaphoreType.DMA
    rows = (micros, half, features)
    return pl.pallas_call(
        pipeline_kernel,
        in_specs=[anywhere] * 4 + [scalars] * 3 + [inside] * 9,
        out_specs=[anywhere] * 8 + [inside] * 2,
        out_shape=(
            shape((seqs, length, features), BF16),
            shape((seqs, length, features), BF16),
            shape((micros, half, hidden), BF16),
            shape((micros, half, hidden), BF16),
            shape(rows, BF16),
            shape((micros, half, hidden), BF16),
            shape((micros, half, hidden), BF16),
            shape((micros, width // HEAD, length, length), BF16),
            shape((micros, 8, features), F32),
            shape((8, hidden), F32),
        ),
        scratch_shapes=[
            pltpu.VMEM((hidden, features), BF16),
            pltpu.VMEM(rows, BF16),
            pltpu.VMEM((2 * micros * half, features), BF16),
            pltpu.VMEM(rows, BF16),
            pltpu.VMEM((micros, half, width), BF16),
            pltpu.VMEM((2, half, hidden), BF16),
            pltpu.VMEM((half, hidden), BF16),
            pltpu.VMEM(rows, BF16),
            pltpu.VMEM((2, half, features), BF16),
            pltpu.VMEM((half, width), BF16),
            pltpu.VMEM((half, width), BF16),
            pltpu.VMEM((half, features), BF16),
            pltpu.VMEM((half, features), F32),
            pltpu.VMEM((2, 2, length, length), BF16),
            pltpu.VMEM((3, width, 128), F32),
            pltpu.VMEM((micros, 8, features), F32),
            dma((hidden // features + hidden // half,)),
            dma((2, CUTS)),
            dma((micros, CUTS)),
            dma((micros, CUTS)),
            dma((2, CUTS)),
            dma((2, CUTS, micros)),
            dma((2,)),
            dma((2, seqs)),
            dma((6,)),
            dma((1,)),
            dma((seqs, 2)),
            dma((seqs, 2)),
            dma((seqs, 2)),
            dma((seqs,)),
            dma((seqs,)),
            dma((width // (2 * HEAD),)),
            dma((width // (2 * HEAD), micros)),
            dma((PARTS,)),
            dma((PARTS, micros)),
            dma((2,)),
        ],
        compiler_params=pltpu.CompilerParams(vmem_limit_bytes=60 << 20, collective_id=0, has_side_effects=True),
        name="pipeline",
    )(
        tokens, cot, first, second, span_start, span_length, time_step, table, embed, mod_weight, mod_bias, gain,
        bias_row, out_bias, cosine, sine,
    )


SMALL_ROWS = 24


def gradient_kernel(
    kept_first, kept_second, kept_rows, back_first, back_second, sums_ref, bias_ref, mod_weight_ref,
    summed_first, summed_second, small_ref, across_ref,
    wide_a, wide_b, deep_a, deep_b, total_a, total_b, give, got, scatter_send, scatter_got, summed, entry,
    load_sem, pair_send, pair_recv, step_send, step_recv, gather_send, gather_recv, core_send, core_recv,
    small_send, small_recv, store_sem, share_sem,
):
    section = lax.axis_index("section")
    dp_index = lax.axis_index("dp")
    chips = small_ref.shape[0]
    core = lax.rem(dp_index, 2)
    partner = dp_index + 1 - 2 * core
    attends = lax.rem(section, 2) == 0
    feeds = lax.rem(section, 2) == 1
    micros, half, hidden = back_first.shape
    features = kept_rows.shape[2]
    width = features // 2
    length = 2 * half
    mid = hidden // 2
    bits = chips.bit_length() - 1
    small_bits = bits + 1
    cuts = part_cuts(mid, features, bits)

    def bit_of(place):
        return lax.rem(dp_index // (1 << place), 2)

    def across(place):
        return dp_index + (1 - 2 * bit_of(place)) * (1 << place)

    barrier = pltpu.get_barrier_semaphore()
    for place in range(small_bits):
        pl.semaphore_signal(barrier, inc=1, device_id=(across(place), section), device_id_type=MESH)

    def small_entry():
        rows = [sums_ref[m, k : k + 1, :] for m in range(micros) for k in range(3)]
        gain = sum(sums_ref[m, 3:4, :] for m in range(micros))
        embed = sum(sums_ref[m, 4:5, :] for m in range(micros))
        rows.append(gain)
        rows += [bias_ref[0:1, k * features : (k + 1) * features] for k in range(hidden // features)]
        rows.append(bias_ref[1:2, :features])
        condition = []
        for m in range(micros):
            total = None
            for k in range(3):
                term = lax.dot_general(
                    jnp.broadcast_to(sums_ref[m, k : k + 1, :], (8, features)),
                    mod_weight_ref[:, k * features : (k + 1) * features],
                    (((1,), (1,)), ((), ())), precision=HIGH, preferred_element_type=F32,
                )
                total = term if total is None else total + term
            condition.append(total[0:1])
        condition.append(jnp.zeros((1, features - micros * mod_weight_ref.shape[0]), F32))
        rows.append(jnp.concatenate(condition, 1))
        rows.append(embed)
        rows += [bias_ref[2:3, :features], bias_ref[3:4, :features]]
        rows.append(jnp.zeros((SMALL_ROWS - len(rows), features), F32))
        entry[0] = jnp.concatenate(rows, 0)

    def small_block(step, theirs):
        size = 1 << (step - 1)
        chip = dp_index // 2
        start = (chip // size) * size
        if theirs:
            start = start + (1 - 2 * bit_of(step)) * size
        return small_ref.at[pl.ds(start, size)]

    def small_copy(step, theirs=False):
        source, target = entry.at[0], entry.at[1]
        if step > 0:
            source = target = small_block(step, theirs)
        return pltpu.make_async_remote_copy(
            source, target, small_send.at[step], small_recv.at[step],
            device_id=(across(step), section), device_id_type=MESH,
        )

    def small_wait(step):
        small_copy(step, True).wait_recv()
        small_copy(step).wait_send()
        if step == 0:
            small_ref[pl.ds(dp_index // 2, 1)] = (entry[0] + entry[1])[None]

    def small_step(number):
        if 1 <= number <= small_bits:
            small_wait(number - 1)
            if number < small_bits:
                small_copy(number).start()

    def loads(pairs, first_sem):
        return [
            pltpu.make_async_copy(source, target, load_sem.at[first_sem + i])
            for i, (source, target) in enumerate(pairs)
        ]

    def spans(m):
        return slice(m * half, (m + 1) * half)

    def heads_rows(source, target, first_sem):
        return loads(
            [(source.at[m, :, pl.ds(0, 2 * features)], target.at[spans(m), :]) for m in range(micros)], first_sem
        )

    def heads_columns(block, target, first_sem):
        pairs = []
        for m in range(micros):
            for side in range(2):
                at = side * half
                if block < 3:
                    source = back_first.at[m, pl.ds(0, width), pl.ds(block * length + at, half)]
                    pairs.append((source, target.at[pl.ds(side * width, width), spans(m)]))
                    continue
                for pair in range(3):
                    rows = width // 3
                    source = kept_first.at[m, pl.ds(width, rows), pl.ds(pair * length + at, half)]
                    pairs.append((source, target.at[pl.ds(side * width + pair * rows, rows), spans(m)]))
        return loads(pairs, first_sem)

    def half_columns(source, which, target, first_sem):
        return loads(
            [(source.at[m, :, pl.ds(which * mid, mid)], target.at[spans(m), :]) for m in range(micros)], first_sem
        )

    totals = (total_a, total_b)

    def place_order(part):
        order = list(range(1, bits + 1))
        return order if part == 0 else order[::-1]

    def window(part, steps):
        start, size, _, _ = cuts[part]
        for place in place_order(part)[:steps]:
            size = size // 2
            start = start + bit_of(place) * size
        return start, size

    def lanes(part, piece):
        _, _, column, count = cuts[part]
        return slice(column + piece * count // PIECES, column + (piece + 1) * count // PIECES)

    def buffer_at(part, piece, step):
        _, rows, _, count = cuts[part]
        begin = rows - (rows >> step)
        return slice(begin, begin + (rows >> (step + 1))), slice(piece * count // PIECES, (piece + 1) * count // PIECES)

    def step_copy(payload, part, piece, step):
        rows, cut = buffer_at(part, piece, step)
        return pltpu.make_async_remote_copy(
            scatter_send.at[payload, part, rows, cut], scatter_got.at[payload, part, rows, cut],
            step_send.at[payload, part, piece, step], step_recv.at[payload, part, piece, step],
            device_id=(across(place_order(part)[step]), section), device_id_type=MESH,
        )

    def scatter_start(payload, part, piece, step):
        start, size = window(part, step)
        size = size // 2
        away = pl.multiple_of(start + (1 - bit_of(place_order(part)[step])) * size, 16)
        rows, cut = buffer_at(part, piece, step)
        scatter_send[payload, part, rows, cut] = totals[payload][pl.ds(away, size), lanes(part, piece)].astype(BF16)
        step_copy(payload, part, piece, step).start()

    def scatter_finish(payload, part, piece, step):
        step_copy(payload, part, piece, step).wait()
        start, size = window(part, step + 1)
        rows = pl.ds(pl.multiple_of(start, 16), size)
        cut = lanes(part, piece)
        got_rows, got_cut = buffer_at(part, piece, step)
        value = totals[payload][rows, cut] + scatter_got[payload, part, got_rows, got_cut].astype(F32)
        if step < bits - 1:
            totals[payload][rows, cut] = value
        else:
            summed[payload, core, rows, cut] = value.astype(BF16)

    def gather_copy(payload, part, piece, step, theirs):
        place = place_order(part)[step]
        start, size = window(part, step + 1)
        if theirs:
            start = start + (1 - 2 * bit_of(place)) * size
        block = summed.at[payload, core, pl.ds(pl.multiple_of(start, 16), size), lanes(part, piece)]
        return pltpu.make_async_remote_copy(
            block, block, gather_send.at[payload, part, piece, step], gather_recv.at[payload, part, piece, step],
            device_id=(across(place), section), device_id_type=MESH,
        )

    def core_copy(payload, part, piece, step, other):
        if step == bits:
            start, size = window(part, bits)
        else:
            start, size = window(part, step + 1)
            start = start + (1 - 2 * bit_of(place_order(part)[step])) * size
        side = 1 - core if other else core
        block = summed.at[payload, side, pl.ds(pl.multiple_of(start, 16), size), lanes(part, piece)]
        return pltpu.make_async_remote_copy(
            block, block, core_send.at[payload, part, piece, step], core_recv.at[payload, part, piece, step],
            device_id=(partner, section), device_id_type=MESH,
        )

    def stage(payload, part, number):
        for piece in range(PIECES):
            if number <= bits:
                if number > 0:
                    scatter_finish(payload, part, piece, number - 1)
                if number < bits:
                    scatter_start(payload, part, piece, number)
                else:
                    gather_copy(payload, part, piece, bits - 1, False).start()
                    core_copy(payload, part, piece, bits, False).start()
            else:
                step = 2 * bits - number
                gather_copy(payload, part, piece, step, True).wait_recv()
                if step > 0:
                    gather_copy(payload, part, piece, step - 1, False).start()
                core_copy(payload, part, piece, step, False).start()

    last_stage = 2 * bits

    def store(payload, part):
        start, rows, column, count = cuts[part]
        target = (summed_first, summed_second)[payload]
        place = (slice(None), pl.ds(start, rows), pl.ds(column, count))
        return pltpu.make_async_copy(
            summed.at[(payload,) + place], target.at[place], store_sem.at[payload, part]
        )

    def wind_up(payload, part):
        for piece in range(PIECES):
            for step in range(bits):
                gather_copy(payload, part, piece, step, False).wait_send()
            for step in range(bits + 1):
                core_copy(payload, part, piece, step, False).wait_send()
                core_copy(payload, part, piece, step, True).wait_recv()
        store(payload, part).start()

    by_rows = cuts[1][0] > 0

    def after_half(payload, half_number):
        if by_rows:
            stage(payload, half_number, 0)
        elif half_number == 1:
            stage(payload, 0, 0)
            stage(payload, 1, 0)

    buffers = (deep_a, deep_b)

    def head_loads():
        per = 2 * micros
        return (
            heads_rows(kept_second, wide_a, 0),
            heads_rows(back_second, wide_b, micros),
            [heads_columns(block, buffers[block % 2], 2 * micros + (block % 2) * 3 * per) for block in range(4)],
        )

    @pl.when(attends)
    def _():
        rows, _, blocks = head_loads()
        for copy in rows + blocks[0] + blocks[1]:
            copy.start()

    def transposed_rows(source, first_sem, staged):
        return loads(
            [
                (source.at[m, :, pl.ds(0, features)], staged.at[m // 2, pl.ds((m % 2) * half, half)])
                for m in range(micros)
            ],
            first_sem,
        )

    def turn(copies, staged, target):
        for m in range(micros):
            copies[m].wait()
            target[:, m * half : (m + 1) * half] = staged[m // 2, (m % 2) * half : (m % 2 + 1) * half, :].T

    def feed_loads():
        near, far = core, 1 - core
        return (
            transposed_rows(kept_rows, 0, summed.at[0]),
            transposed_rows(back_second, micros, summed.at[1]),
            half_columns(back_first, far, wide_a, 2 * micros),
            half_columns(back_first, near, wide_b, 3 * micros),
            half_columns(kept_second, far, wide_a, 4 * micros),
            half_columns(kept_second, near, wide_b, 5 * micros),
        )

    @pl.when(feeds)
    def _():
        first_rows, second_rows, first_far, first_near, _, _ = feed_loads()
        for copy in first_rows + first_far + first_near + second_rows:
            copy.start()

    def head_products(block, loaded):
        rows, grads, blocks = loaded
        if block == 0:
            for copy in rows:
                copy.wait()
        for copy in blocks[block]:
            copy.wait()
        source = wide_a if block < 3 else wide_b
        if block == 1:
            for copy in grads:
                copy.start()
        if block == 3:
            for copy in grads:
                copy.wait()
        deep = buffers[block % 2]
        total_a[block * width : (block + 1) * width, :] = dot_nn(
            deep[:width, :], source[:, :features]
        ) + dot_nn(deep[width:, :], source[:, features:])
        if block + 2 < 4:
            for copy in blocks[block + 2]:
                copy.start()

    def other_product(deep, wide, piece):
        rows = slice(piece * features, (piece + 1) * features)
        give[rows, :] = dot_nn(deep[...], wide[:, rows]).astype(BF16)

    @pl.when(attends)
    def _():
        loaded = head_loads()
        for block in range(2):
            head_products(block, loaded)

    @pl.when(feeds)
    def _():
        first_rows, _, first_far, _, _, _ = feed_loads()
        turn(first_rows, summed.at[0], deep_a)
        for copy in first_far:
            copy.wait()
        other_product(deep_a, wide_a, 0)

    pl.semaphore_wait(barrier, small_bits)

    @pl.when(attends)
    def _():
        loaded = head_loads()
        after_half(0, 0)
        for block in range(2, 4):
            head_products(block, loaded)
        after_half(0, 1)
        small_entry()
        small_copy(0).start()
        for number in range(1, max(last_stage, small_bits) + 1):
            if number <= last_stage:
                stage(0, 0, number)
                stage(0, 1, number)
            small_step(number)
        for part in range(2):
            wind_up(0, part)
        for part in range(2):
            store(0, part).wait()

    def pair_copy(payload, piece):
        rows = pl.ds(piece * features, features)
        return pltpu.make_async_remote_copy(
            give.at[rows], got.at[payload, rows], pair_send.at[payload, piece], pair_recv.at[payload, piece],
            device_id=(partner, section), device_id_type=MESH,
        )

    pieces = mid // features

    def own_product(payload, deep, wide, piece):
        rows = slice(piece * features, (piece + 1) * features)
        totals[payload][rows, :] = dot_nn(deep[...], wide[:, rows])

    def add_pair(payload, piece):
        rows = slice(piece * features, (piece + 1) * features)
        pair_copy(payload, piece).wait()
        totals[payload][rows, :] += got[payload, rows, :].astype(F32)
        after_half(payload, piece)

    @pl.when(feeds)
    def _():
        _, second_rows, _, first_near, second_far, second_near = feed_loads()
        pair_copy(0, 0).start()
        for copy in first_near:
            copy.wait()
        own_product(0, deep_a, wide_b, 0)
        for piece in range(1, pieces):
            other_product(deep_a, wide_a, piece)
            pair_copy(0, piece).start()
        for copy in second_far:
            copy.start()
        add_pair(0, 0)
        for piece in range(1, pieces):
            own_product(0, deep_a, wide_b, piece)
        for copy in second_near:
            copy.start()
        for piece in range(1, pieces):
            add_pair(0, piece)
        small_entry()
        small_copy(0).start()
        turn(second_rows, summed.at[1], deep_b)
        for copy in second_far:
            copy.wait()
        for piece in range(pieces):
            other_product(deep_b, wide_a, piece)
            pair_copy(1, piece).start()
        for copy in second_near:
            copy.wait()
        stage(0, 0, 1)
        own_product(1, deep_b, wide_b, 0)
        add_pair(1, 0)
        stage(0, 1, 1)
        for piece in range(1, pieces):
            own_product(1, deep_b, wide_b, piece)
            add_pair(1, piece)
        for number in range(2, max(last_stage, small_bits) + 2):
            if number <= last_stage:
                stage(0, 0, number)
                stage(0, 1, number)
            if number - 1 <= last_stage:
                stage(1, 0, number - 1)
                stage(1, 1, number - 1)
            small_step(number - 1)
        for payload in range(2):
            for part in range(2):
                wind_up(payload, part)
        for payload in range(2):
            for part in range(2):
                store(payload, part).wait()

    share = pltpu.make_async_copy(small_ref.at[:, pl.ds(SMALL_ROWS - 8, 8)], across_ref, share_sem)
    share.start()
    share.wait()


PIECES = 3


def part_cuts(mid, features, bits):
    if (mid // 2 >> bits) % 16 == 0:
        return [(0, mid // 2, 0, features), (mid // 2, mid // 2, 0, features)]
    return [(0, mid, 0, features // 2), (0, mid, features // 2, features // 2)]


def summed_gradients(kept_first, kept_second, kept_rows, back_first, back_second, sums, bias, mod_weight, dp_count):
    micros, half, hidden = back_first.shape
    features = kept_rows.shape[2]
    mid = hidden // 2
    small_bits = dp_count.bit_length() - 1
    bits = small_bits - 1
    anywhere = pl.BlockSpec(memory_space=pl.ANY)
    inside = pl.BlockSpec(memory_space=pltpu.VMEM)
    dma = pltpu.SemaphoreType.DMA
    tokens = micros * half
    _, rows, _, columns = part_cuts(mid, features, bits)[0]
    return pl.pallas_call(
        gradient_kernel,
        in_specs=[anywhere] * 5 + [inside] * 3,
        out_specs=[anywhere] * 2 + [inside, anywhere],
        out_shape=(
            shape((2, mid, features), BF16),
            shape((2, mid, features), BF16),
            shape((dp_count // 2, SMALL_ROWS, features), F32),
            shape((dp_count // 2, 8, features), F32),
        ),
        scratch_shapes=[
            pltpu.VMEM((tokens, mid), BF16),
            pltpu.VMEM((tokens, mid), BF16),
            pltpu.VMEM((features, tokens), BF16),
            pltpu.VMEM((features, tokens), BF16),
            pltpu.VMEM((mid, features), F32),
            pltpu.VMEM((mid, features), F32),
            pltpu.VMEM((mid, features), BF16),
            pltpu.VMEM((2, mid, features), BF16),
            pltpu.VMEM((2, 2, rows - (rows >> bits), columns), BF16),
            pltpu.VMEM((2, 2, rows - (rows >> bits), columns), BF16),
            pltpu.VMEM((2, 2, mid, features), BF16),
            pltpu.VMEM((2, SMALL_ROWS, features), F32),
            dma((14 * micros,)),
            dma((2, mid // features)),
            dma((2, mid // features)),
            dma((2, 2, PIECES, bits)),
            dma((2, 2, PIECES, bits)),
            dma((2, 2, PIECES, bits)),
            dma((2, 2, PIECES, bits)),
            dma((2, 2, PIECES, bits + 1)),
            dma((2, 2, PIECES, bits + 1)),
            dma((small_bits,)),
            dma((small_bits,)),
            dma((2, 2)),
            dma,
        ],
        compiler_params=pltpu.CompilerParams(vmem_limit_bytes=62 << 20, collective_id=1, has_side_effects=True),
        name="summed_gradients",
    )(kept_first, kept_second, kept_rows, back_first, back_second, sums, bias, mod_weight)


def small_places(small_ref, mod_weight_grad, mod_bias_grad, gain_grad, first_bias_grad, second_bias_grad):
    count = small_ref.shape[0]
    cond = mod_weight_grad.shape[0]
    features = gain_grad.shape[1]
    pairs = [small_ref[i] for i in range(count)]
    total = sum(pairs[1:], pairs[0])
    embedded = jnp.concatenate(embedded_of(small_ref, cond, 0), 0)
    conditions = embedded * (1.0 / (1.0 + jnp.exp(-embedded)))
    for k in range(3):
        rows = jnp.concatenate([pair[3 * m + k : 3 * m + k + 1] for pair in pairs for m in range(MICROS)], 0)
        lanes = slice(k * features, (k + 1) * features)
        mod_weight_grad[:, lanes] = lax.dot_general(
            conditions, rows, (((0,), (0,)), ((), ())), precision=HIGH, preferred_element_type=F32
        )
        mod_bias_grad[:, lanes] = sum((total[3 * m + k : 3 * m + k + 1] for m in range(1, MICROS)), total[k : k + 1])
    base = 3 * MICROS
    gain_grad[...] = total[base : base + 1]
    blocks = first_bias_grad.shape[1] // features
    for block in range(blocks):
        first_bias_grad[:, block * features : (block + 1) * features] = total[base + 1 + block : base + 2 + block]
    second_bias_grad[...] = total[base + 1 + blocks : base + 2 + blocks]


def attention_place_kernel(first_ref, small_ref, grad_in, grad_out, *small_grads):
    step = pl.program_id(0)
    width = grad_in.shape[1]
    for side in range(2):

        @pl.when((step < 6) & (lax.rem(step, 2) == side))
        def _():
            grad_in[...] = first_ref[side].T.astype(F32)

        @pl.when(step == 6 + side)
        def _():
            for half in range(2):
                grad_in[half * width : (half + 1) * width, :] = first_ref[
                    half, :, side * width : (side + 1) * width
                ].astype(F32)

    grad_out[...] = jnp.zeros_like(grad_out)

    @pl.when(step == 0)
    def _():
        small_places(small_ref, *small_grads)


def feed_place_kernel(first_ref, second_ref, small_ref, grad_in, grad_out, *small_grads):
    grad_in[...] = first_ref[0].astype(F32)
    grad_out[...] = second_ref[0].T.astype(F32)

    @pl.when(pl.program_id(0) == 0)
    def _():
        small_places(small_ref, *small_grads)


MICROS = 4


def embedded_of(small_ref, cond, group):
    seqs = MICROS // 2
    return [
        small_ref[
            chip, SMALL_ROWS - 4 + core : SMALL_ROWS - 3 + core, (group * seqs + i) * cond : (group * seqs + i + 1) * cond
        ]
        for chip in range(small_ref.shape[0])
        for i in range(seqs)
        for core in range(2)
    ]


def place_gradients(attends, first, second, small, cond, hidden):
    features = first.shape[2]
    width = features // 2
    whole = lambda dims: pl.BlockSpec(dims, lambda i: (0,) * len(dims))
    small_dims = ((cond, 3 * features), (1, 3 * features), (1, features), (1, hidden), (1, features))
    outputs = dict(
        grid=(hidden // width,),
        out_specs=[
            pl.BlockSpec((features, width), lambda i: (0, i)),
            pl.BlockSpec((width, features), lambda i: (i, 0)),
        ]
        + [whole(dims) for dims in small_dims],
        out_shape=(shape((features, hidden), F32), shape((hidden, features), F32))
        + tuple(shape(dims, F32) for dims in small_dims),
        compiler_params=params(),
    )
    owned = pl.BlockSpec((1, features, width), lambda i: (i // 4, (i % 4) // 2, i % 2))

    def attention_half():
        return tuple(
            pl.pallas_call(
                attention_place_kernel,
                in_specs=[pl.BlockSpec((2, width, features), lambda i: (0, i // 2, 0)), whole(small.shape)],
                name="place_attention",
                **outputs,
            )(first, small)
        )

    def feed_half():
        return tuple(
            pl.pallas_call(
                feed_place_kernel, in_specs=[owned, owned, whole(small.shape)], name="place_feed", **outputs
            )(first, second, small)
        )

    return lax.cond(attends, attention_half, feed_half)


def table_kernel(small_ref, own_ref, one_ref, two_ref, three_ref, table_grad, embed_grad):
    steps, cond = table_grad.shape
    across = sum((ref[:, 2:4, :] for ref in (one_ref, two_ref, three_ref)), own_ref[:, 2:4, :])
    count = across.shape[0]
    embed_grad[...] = sum((across[i, 1] for i in range(1, count)), across[0, 1])
    embedded = jnp.concatenate(embedded_of(small_ref, cond, 0), 0)
    chosen = jnp.concatenate(embedded_of(small_ref, cond, 1), 0)[:, 0:1]
    gradients = []
    for chip in range(count):
        row = across[chip, 0:1]
        gradients += [row[:, m * cond : (m + 1) * cond] for m in range(MICROS)]
    squash = 1.0 / (1.0 + jnp.exp(-embedded))
    gradient = jnp.concatenate(gradients, 0) * (squash * (1.0 + embedded * (1.0 - squash)))
    places = lax.broadcasted_iota(jnp.int32, (chosen.shape[0], steps), 1).astype(F32)
    onehot = jnp.where(places == chosen, 1.0, 0.0)
    table_grad[...] = lax.dot_general(
        onehot, gradient, (((0,), (0,)), ((), ())), precision=HIGH, preferred_element_type=F32
    )


def table_gradients(small, across, steps, cond):
    return pl.pallas_call(
        table_kernel,
        out_shape=(shape((steps, cond), F32), shape((small.shape[2],), F32)),
        compiler_params=params(),
        name="table_gradients",
    )(small, *across)


def rope_tables(length):
    position = np.arange(length, dtype=np.float32)[None, :]
    column = np.arange(HALF, dtype=np.float32)[:, None]
    angles = position * np.exp(column * np.float32(-2.0 * math.log(10000.0) / HEAD))
    return jnp.asarray(np.cos(angles)), jnp.asarray(np.sin(angles))


def shards(
    tokens, span_start, span_length, time_step, time_table, mask_embed, mod_weight, mod_bias,
    norm_gain, in_weight, in_bias, out_weight, out_bias, cotangent,
):
    sections = lax.axis_size("section")
    dp_count = lax.axis_size("dp")
    seqs, length, features = tokens.shape
    hidden = in_weight.shape[2]
    steps, cond = time_table.shape
    cosine, sine = rope_tables(length)
    states, stream, kept_first, kept_second, kept_rows, back_first, back_second, _, sums, bias = pipeline(
        tokens, cotangent, in_weight[0], out_weight[0], span_start, span_length, time_step, time_table,
        mask_embed[None], mod_weight[0], mod_bias, norm_gain, in_bias, out_bias, cosine, sine,
    )
    summed_first, summed_second, small, across = summed_gradients(
        kept_first, kept_second, kept_rows, back_first, back_second, sums, bias, mod_weight[0], dp_count
    )
    turns = [
        lax.ppermute(across, "section", [(s, (s + turn) % sections) for s in range(sections)])
        for turn in range(1, sections)
    ]
    grad_in, grad_out, grad_mod_weight, grad_mod_bias, grad_gain, grad_bias_first, grad_bias_second = place_gradients(
        lax.axis_index("section") % 2 == 0, summed_first, summed_second, small, cond, hidden
    )
    table_total, embed_total = table_gradients(small, [across] + turns, steps, cond)
    return (
        states[None],
        stream[None],
        table_total,
        embed_total,
        grad_mod_weight[None],
        grad_mod_bias,
        grad_gain,
        grad_in[None],
        grad_bias_first,
        grad_out[None],
        grad_bias_second,
    )


def solution(mesh):
    placed = (
        P("dp", None, None),
        P("dp"),
        P("dp"),
        P("dp"),
        P(),
        P(),
        P("section", None, None),
        P("section", None),
        P("section", None),
        P("section", None, None),
        P("section", None),
        P("section", None, None),
        P("section", None),
        P("dp", None, None),
    )
    return jax.shard_map(
        shards,
        mesh=mesh,
        in_specs=placed,
        out_specs=(
            P("section", "dp", None, None),
            P("section", "dp", None, None),
            P(),
            P(),
            P("section", None, None),
            P("section", None),
            P("section", None),
            P("section", None, None),
            P("section", None),
            P("section", None, None),
            P("section", None),
        ),
        check_vma=False,
    )
```

```python
import math

import jax
import jax.numpy as jnp
import numpy as np
from jax import lax
from jax.experimental import pallas as pl
from jax.experimental.pallas import tpu as pltpu
from jax.sharding import PartitionSpec as P

HEAD = 64
HALF = HEAD // 2
EPS = 1e-06
HIGH = lax.Precision.HIGHEST
F32 = jnp.float32
BF16 = jnp.bfloat16
SCALE = HEAD ** (-0.5)
EXP2_SCALE = SCALE * math.log2(math.e)
GELU_C = math.sqrt(2.0 / math.pi)
VMEM_LIMIT = 56 << 20


def dot_nn(left, right):
    return jnp.dot(left, right, preferred_element_type=F32)


def dot_nt(left, right):
    return lax.dot_general(left, right, (((1,), (1,)), ((), ())), preferred_element_type=F32)


def params(**more):
    return pltpu.CompilerParams(vmem_limit_bytes=VMEM_LIMIT, **more)


def shape(dims, dtype):
    return jax.ShapeDtypeStruct(dims, dtype)


def normalize(rows):
    average = jnp.mean(rows, -1, keepdims=True)
    centered = rows - average
    inverse_std = lax.rsqrt(jnp.mean(centered * centered, -1, keepdims=True) + EPS)
    return centered * inverse_std, inverse_std


MESH = pl.DeviceIdType.MESH
PARTS = 2
CUTS = 4


def pipeline_kernel(
    tokens_ref, cot_ref, first_ref, second_ref, start_ref, length_ref, step_ref, table_ref, embed_ref,
    mod_weight_ref, mod_bias_ref, gain_ref, bias_row_ref, out_bias_ref, cos_ref, sin_ref,
    states_ref, stream_ref, kept_first, kept_second, kept_rows, back_first, back_second, kept_spread, sums_ref, bias_ref,
    weights, streams, pool, upstreams, mixed_got, first_buf, second_buf, branches, leaving,
    mixed_own, mixed_send, grad_send, grad_own, spreads, bias_columns, mods_ref,
    load_sem, pass_send, pass_recv, back_recv, swap_send, swap_recv, place_send, place_recv, store_sem, fetch_sem,
    local_sem, give_send, give_recv, mod_send, mod_recv, mixed_give, mixed_take, grad_give, grad_take, spread_sem,
):
    section = lax.axis_index("section")
    sections = lax.axis_size("section")
    dp_index = lax.axis_index("dp")
    core = lax.rem(dp_index, 2)
    partner = dp_index + 1 - 2 * core
    micros, half, features = streams.shape
    width = mixed_own.shape[1]
    heads = width // HEAD
    length = 2 * half
    part_rows = half // PARTS
    cut_rows = half // CUTS
    attends = lax.rem(section, 2) == 0
    feeds = lax.rem(section, 2) == 1
    is_first = section == 0
    is_last = section == sections - 1
    hidden = second_ref.shape[0]
    blocks = hidden // features
    seqs = micros // 2
    cond = table_ref.shape[1]
    feed_step = half
    feed_parts = hidden // feed_step
    near = pl.ds(core * half, half)
    far = pl.ds((1 - core) * half, half)

    barrier = pltpu.get_barrier_semaphore()
    pl.semaphore_signal(barrier, inc=1, device_id=(partner, section), device_id_type=MESH)

    @pl.when(section > 0)
    def _():
        pl.semaphore_signal(barrier, inc=1, device_id=(dp_index, section - 1), device_id_type=MESH)

    @pl.when(section < sections - 1)
    def _():
        pl.semaphore_signal(barrier, inc=1, device_id=(dp_index, section + 1), device_id_type=MESH)

    def head_loads():
        copies = []
        for block in range(3):
            lanes = pl.ds(pl.multiple_of(block * features + core * width, 128), width)
            target = pl.ds(block * width, width)
            copies.append((first_ref.at[pl.ds(0, half), lanes], first_buf.at[0, :, target]))
            copies.append(
                (first_ref.at[pl.ds(half, features - half), lanes], first_buf.at[1, pl.ds(0, features - half), target])
            )
        for side in range(2):
            rows = pl.ds(pl.multiple_of((core if side == 0 else 1 - core) * width, 16), width)
            copies.append(
                (first_ref.at[rows, pl.ds(3 * features, features)], weights.at[pl.ds((3 + side) * width, width)])
            )
        return [pltpu.make_async_copy(*copy, load_sem.at[i]) for i, copy in enumerate(copies)]

    def pool_at(slot):
        return pool.at[pl.ds(pl.multiple_of(slot * half, 16), half)]

    def others_at(micro):
        return pool_at(micro)

    def up_others_at(micro):
        return pool_at(micros + micro)

    def feed_loads():
        copies = [
            (first_ref.at[:, pl.ds(block * features, features)], weights.at[pl.ds(block * features, features)])
            for block in range(blocks)
        ]
        copies += [
            (second_ref.at[pl.ds(part * feed_step, feed_step)], pool_at(part)) for part in range(feed_parts)
        ]
        return [pltpu.make_async_copy(*copy, load_sem.at[i]) for i, copy in enumerate(copies)]

    def token_copies(i):
        micro = 2 * i + core
        return [
            pltpu.make_async_copy(tokens_ref.at[i, near], streams.at[micro], local_sem.at[i, 0]),
            pltpu.make_async_copy(tokens_ref.at[i, far], others_at(micro), local_sem.at[i, 1]),
        ]

    def token_gives(i):
        micro = 2 * i + core
        return [
            pltpu.make_async_remote_copy(
                tokens_ref.at[i, rows], target, give_send.at[i, k], give_recv.at[i, k],
                device_id=(partner, section), device_id_type=MESH,
            )
            for k, (rows, target) in enumerate(((far, streams.at[micro]), (near, others_at(micro))))
        ]

    def cot_copy(i):
        return pltpu.make_async_copy(cot_ref.at[i, near], upstreams.at[2 * i + core], local_sem.at[i, 0])

    def cot_give(i):
        return pltpu.make_async_remote_copy(
            cot_ref.at[i, far], upstreams.at[2 * i + core], give_send.at[i, 0], give_recv.at[i, 0],
            device_id=(partner, section), device_id_type=MESH,
        )

    def mod_give(i):
        block = mods_ref.at[2 * i + core]
        return pltpu.make_async_remote_copy(
            block, block, mod_send.at[i], mod_recv.at[i], device_id=(partner, section), device_id_type=MESH
        )

    @pl.when(is_first)
    def _():
        for i in range(seqs):
            for copy in token_copies(i):
                copy.start()

    @pl.when(attends)
    def _():
        for copy in head_loads():
            copy.start()

    @pl.when(feeds)
    def _():
        for copy in feed_loads():
            copy.start()

    @pl.when(is_last)
    def _():
        for i in range(seqs):
            cot_copy(i).start()

    bias_ref[...] = jnp.zeros_like(bias_ref)
    bias_columns[...] = jnp.zeros_like(bias_columns)
    looked_up = [table_ref[pl.ds(step_ref[i], 1), :] for i in range(seqs)]
    embedded = jnp.concatenate(looked_up + [jnp.zeros((8 - seqs, cond), F32)], 0)
    condition = embedded * (1.0 / (1.0 + jnp.exp(-embedded)))
    modulations = mod_bias_ref[...] + lax.dot_general(
        condition, mod_weight_ref[...], (((1,), (0,)), ((), ())), precision=HIGH, preferred_element_type=F32
    )
    for i in range(seqs):
        chosen = jnp.broadcast_to(step_ref[i].astype(F32), (1, cond))
        for side in range(2):
            row = slice(2 + side, 3 + side)
            bias_ref[row, i * cond : (i + 1) * cond] = jnp.where(core == side, looked_up[i], 0.0)
            bias_ref[row, (seqs + i) * cond : (seqs + i + 1) * cond] = jnp.where(core == side, chosen, 0.0)
        begin = jnp.broadcast_to(start_ref[i].astype(F32), (1, features))
        end = jnp.broadcast_to((start_ref[i] + length_ref[i]).astype(F32), (1, features))
        mods_ref[2 * i + core] = jnp.concatenate(
            [modulations[i : i + 1, k * features : (k + 1) * features] for k in range(3)]
            + [begin, end, jnp.zeros((3, features), F32)],
            0,
        )

    pl.semaphore_wait(
        barrier, 1 + jnp.where(section > 0, 1, 0) + jnp.where(section < sections - 1, 1, 0)
    )
    for i in range(seqs):
        mod_give(i).start()

        if i == 0:

            @pl.when(is_first)
            def _():
                for copy in token_gives(i):
                    copy.start()

        @pl.when(is_last)
        def _():
            cot_give(i).start()

    @pl.when(attends)
    def _():
        for copy in head_loads():
            copy.wait()
        for block in range(3):
            lanes = slice(block * width, (block + 1) * width)
            weights[lanes, :half] = first_buf[0, :, lanes].T
            weights[lanes, half:] = first_buf[1, : features - half, lanes].T
            at = pl.multiple_of(block * features + core * width, 128)
            bias = jnp.broadcast_to(bias_row_ref[:, pl.ds(at, width)], (8, width)).T
            bias_columns[block, :, 8:16] = bias

    @pl.when(feeds)
    def _():
        for copy in feed_loads():
            copy.wait()

    def cut_at(part):
        return pl.ds(pl.multiple_of(part * cut_rows, 16), cut_rows)

    def each_cut(body):
        def one(part, carried):
            body(part, cut_at(part))
            return carried

        lax.fori_loop(0, CUTS, one, 0)

    def rows_of(part):
        return slice(part * part_rows, (part + 1) * part_rows)

    def schedule(step):
        turns = jnp.where(is_last, 1, 0)
        forward = jnp.where(is_last, 1 - lax.rem(step, 2), jnp.where(step < micros, 1, 0))
        micro = jnp.where(is_last, step // 2, lax.rem(step, micros))
        del turns
        return forward == 1, micro

    def pass_on(step, part, micro, forward):
        slot = lax.rem(step, 2)
        rows = cut_at(part)
        source = leaving.at[slot, rows]
        if forward:
            return pltpu.make_async_remote_copy(
                source, streams.at[micro, rows],
                pass_send.at[slot, part], pass_recv.at[micro, part],
                device_id=(dp_index, section + 1), device_id_type=MESH,
            )
        return pltpu.make_async_remote_copy(
            source, upstreams.at[micro, rows],
            pass_send.at[slot, part], back_recv.at[micro, part],
            device_id=(dp_index, section - 1), device_id_type=MESH,
        )

    def place_target(target, micro):
        return target.at[micro // 2, pl.ds(core * half, half)]

    def place_local(step, micro, target):
        slot = lax.rem(step, 2)
        return pltpu.make_async_copy(leaving.at[slot], place_target(target, micro), place_send.at[slot])

    def place_remote(step, micro, target, index):
        slot = lax.rem(step, 2)
        return pltpu.make_async_remote_copy(
            leaving.at[slot], place_target(target, micro), place_send.at[slot],
            place_recv.at[index, micro // 2], device_id=(partner, section), device_id_type=MESH,
        )

    def send_part(step, part, micro, forward):
        reaches = section < sections - 1 if forward else section > 0

        @pl.when(reaches)
        def _():
            pass_on(step, part, micro, forward).start()

    def place_result(step, micro, forward):
        target, index = (states_ref, 0) if forward else (stream_ref, 1)
        mine = lax.rem(micro, 2) == core

        @pl.when(mine)
        def _():
            place_local(step, micro, target).start()

        @pl.when(jnp.logical_not(mine))
        def _():
            place_remote(step, micro, target, index).start()

    def leaving_free(step):
        was_forward, micro = schedule(step)
        mine = lax.rem(micro, 2) == core
        for forward, cond in ((True, was_forward), (False, jnp.logical_not(was_forward))):
            reaches = section < sections - 1 if forward else section > 0
            target, index = (states_ref, 0) if forward else (stream_ref, 1)

            @pl.when(cond & reaches)
            def _():
                for part in range(CUTS):
                    pass_on(step, part, micro, forward).wait_send()

            @pl.when(cond & mine)
            def _():
                place_local(step, micro, target).wait()

            @pl.when(cond & jnp.logical_not(mine))
            def _():
                place_remote(step, micro, target, index).wait_send()

    def swap(kind, part, source, target, micro):
        rows = cut_at(part)
        return pltpu.make_async_remote_copy(
            source.at[rows], target.at[rows], swap_send.at[kind, part], swap_recv.at[kind, part, micro],
            device_id=(partner, section), device_id_type=MESH,
        )

    def give_mixed(pair, micro):
        lanes = pl.ds(pl.multiple_of(pair * 2 * HEAD, 2 * HEAD), 2 * HEAD)
        return pltpu.make_async_remote_copy(
            mixed_send.at[:, lanes], mixed_got.at[micro, :, lanes],
            mixed_give.at[pair], mixed_take.at[pair, micro],
            device_id=(partner, section), device_id_type=MESH,
        )

    def give_grad(part, micro):
        rows = pl.ds(part * part_rows, part_rows)
        return pltpu.make_async_remote_copy(
            grad_send.at[rows], others_at(micro).at[rows], grad_give.at[part], grad_take.at[part, micro],
            device_id=(partner, section), device_id_type=MESH,
        )

    def store_first(slot, target, micro):
        return pltpu.make_async_copy(first_buf.at[slot], target.at[micro], store_sem.at[slot])

    def store_second(target, micro):
        lanes = pl.ds(0, 2 * features)
        return pltpu.make_async_copy(second_buf.at[:, lanes], target.at[micro, :, lanes], store_sem.at[2])

    def store_active(micro):
        return pltpu.make_async_copy(second_buf, kept_second.at[micro], store_sem.at[2])

    def store_grad_branch(micro):
        return pltpu.make_async_copy(
            grad_send, back_second.at[micro, :, pl.ds(0, features)], store_sem.at[3]
        )

    def rows_kept(micro):
        return pool_at(feed_parts + lax.rem(micro, 2))

    def store_rows(micro):
        return pltpu.make_async_copy(
            rows_kept(micro), kept_rows.at[micro], store_sem.at[4 + lax.rem(micro, 2)]
        )

    pairs = heads // 2

    def spread_slot(pair, micro):
        return lax.rem(micro * pairs + pair, 2)

    def spread_store(pair, micro):
        slot = spread_slot(pair, micro)
        return pltpu.make_async_copy(
            spreads.at[slot], kept_spread.at[micro, pl.ds(2 * pair, 2)], spread_sem.at[slot]
        )

    def spread_fetch(pair, micro):
        slot = spread_slot(pair, micro)
        return pltpu.make_async_copy(
            kept_spread.at[micro, pl.ds(2 * pair, 2)], spreads.at[slot], spread_sem.at[slot]
        )

    def first_slot_free(slot, when):
        @pl.when(when)
        def _():
            store_first(slot, kept_first, 0).wait()

    def arrive(micro, part, forward):
        @pl.when(jnp.logical_not(is_first if forward else is_last))
        def _():
            pass_on(0, part, micro, forward).wait_recv()

    def arrive_cot(micro):
        mine = lax.rem(micro, 2) == core

        @pl.when(is_last & mine)
        def _():
            cot_copy(micro // 2).wait()

        @pl.when(is_last & jnp.logical_not(mine))
        def _():
            cot_give(micro // 2).wait_recv()

    def arrive_mod(micro):
        @pl.when(lax.rem(micro, 2) != core)
        def _():
            mod_give(micro // 2).wait_recv()

    def in_span(micro, begin, count):
        bounds = mods_ref[micro, 3:5, 0:1]
        position = (lax.broadcasted_iota(jnp.int32, (count, 1), 0) + begin).astype(F32)
        return (position >= bounds[0:1]) & (position < bounds[1:2])

    def arrive_tokens(micro, k):
        mine = lax.rem(micro, 2) == core

        @pl.when(mine)
        def _():
            token_copies(micro // 2)[k].wait()

        @pl.when(jnp.logical_not(mine))
        def _():
            token_gives(micro // 2)[k].wait_recv()

        target, side = (streams.at[micro], core) if k == 0 else (others_at(micro), 1 - core)
        for part in range(PARTS):
            rows = rows_of(part)
            span = in_span(micro, side * half + part * part_rows, part_rows)
            target[rows, :] = jnp.where(span, embed_ref[...], target[rows, :])

    def exchange(part, micro):
        return swap(1, part, upstreams.at[micro], up_others_at(micro), micro)

    def exchange_start(micro):
        for part in range(CUTS):
            arrive(micro, part, False)
            exchange(part, micro).start()

    def attention_forward(step, micro):
        arrive_mod(micro)
        mod = mods_ref[micro]
        gain = gain_ref[...]
        slot = lax.rem(micro, 2)
        later = jnp.logical_not(is_first)

        @pl.when(is_first)
        def _():
            arrive_tokens(micro, 0)

        @pl.when(later)
        def _():
            for part in range(CUTS):
                arrive(micro, part, True)
                swap(0, part, streams.at[micro], others_at(micro), micro).start()

        first_slot_free(slot, step >= 2)

        @pl.when(step > 0)
        def _():
            store_second(kept_second, micro).wait()

        def project(source, part):
            standard, _ = normalize(source[rows_of(part % PARTS), :].astype(F32))
            rows = (standard * gain * (1.0 + mod[1:2]) + mod[0:1]).astype(BF16)
            place = (part // PARTS) * features
            second_buf[rows_of(part % PARTS), place : place + features] = rows
            projected = dot_nt(weights[: 3 * width, :], rows)
            side = core if part < PARTS else 1 - core
            columns = pl.ds(pl.multiple_of(side * half + (part % PARTS) * part_rows, 128), part_rows)
            cosine = cos_ref[:, columns]
            sine = sin_ref[:, columns]
            for block in range(3):
                lanes = slice(block * length + part * part_rows, block * length + (part + 1) * part_rows)
                biased = projected[block * width : (block + 1) * width] + bias_columns[block, :, 8:9]
                if block == 2:
                    first_buf[slot, :width, lanes] = biased.astype(BF16)
                    continue
                for head in range(heads):
                    base = head * HEAD
                    front = biased[base : base + HALF]
                    back = biased[base + HALF : base + HEAD]
                    at = head * HEAD
                    first_buf[slot, at : at + HALF, lanes] = (front * cosine - back * sine).astype(BF16)
                    first_buf[slot, at + HALF : at + HEAD, lanes] = (back * cosine + front * sine).astype(BF16)

        for part in range(PARTS):
            project(streams.at[micro], part)

        @pl.when(is_first)
        def _():
            arrive_tokens(micro, 1)

            @pl.when(step == 0)
            def _():
                for i in range(1, seqs):
                    for copy in token_gives(i):
                        copy.start()

        @pl.when(later)
        def _():
            for part in range(CUTS):
                swap(0, part, streams.at[micro], others_at(micro), micro).wait_recv()

        for part in range(PARTS, 2 * PARTS):
            project(others_at(micro), part)

        def scores_of(head):
            base = pl.multiple_of(head * HEAD, HEAD)
            key_rows = first_buf[slot, pl.ds(base, HEAD), length : 2 * length].T
            return dot_nn(key_rows, first_buf[slot, pl.ds(base, HEAD), :length])

        def finish(head, within, scores, kept):
            base = pl.multiple_of(head * HEAD, HEAD)
            top = jnp.max(scores, 0, keepdims=True) * EXP2_SCALE
            spread = jnp.exp2(scores * EXP2_SCALE - top)
            spread = (spread * (1.0 / jnp.sum(spread, 0, keepdims=True))).astype(BF16)
            spreads[kept, within] = spread
            return dot_nn(first_buf[slot, pl.ds(base, HEAD), 2 * length :], spread).astype(BF16)

        def head_pair(pair, carried):
            kept = spread_slot(pair, micro)

            @pl.when(micro * pairs + pair >= 2)
            def _():
                spread_store(pair, micro).wait()

            scores = scores_of(2 * pair), scores_of(2 * pair + 1)
            mixed = jnp.concatenate([finish(2 * pair + i, i, scores[i], kept) for i in range(2)], 0)
            spread_store(pair, micro).start()
            at = pl.multiple_of(pair * length, length)
            first_buf[slot, width:, pl.ds(at, length)] = mixed
            turned = mixed.T
            lanes = pl.multiple_of(pair * 2 * HEAD, 2 * HEAD)
            mixed_own[:, pl.ds(lanes, 2 * HEAD)] = turned[:half]
            mixed_send[:, pl.ds(lanes, 2 * HEAD)] = turned[half:]
            give_mixed(pair, micro).start()
            return carried

        lax.fori_loop(0, heads // 2, head_pair, 0)
        store_first(slot, kept_first, micro).start()
        store_second(kept_second, micro).start()

        @pl.when(later & (step == micros - 1))
        def _():
            exchange_start(0)

        @pl.when(step >= 2)
        def _():
            leaving_free(step - 2)

        for pair in range(heads // 2):
            give_mixed(pair, micro).wait_recv()
        def out_cut(part, rows):
            mixed = jnp.concatenate([mixed_own[rows, :], mixed_got[micro, rows, :]], 1)
            branch = dot_nn(mixed, weights[3 * width : 5 * width, :]) + bias_row_ref[:, 3 * features :]
            branches[micro, rows, :] = branch.astype(BF16)
            result = streams[micro, rows, :].astype(F32) + mod[2:3] * branch
            leaving[lax.rem(step, 2), rows, :] = result.astype(BF16)
            send_part(step, part, micro, True)

        each_cut(out_cut)
        place_result(step, micro, True)
        for pair in range(heads // 2):
            give_mixed(pair, micro).wait_send()

        @pl.when(later)
        def _():
            for part in range(CUTS):
                swap(0, part, streams.at[micro], others_at(micro), micro).wait_send()

    pieces = [(block, lane) for block in range(blocks) for lane in range(0, features, part_rows)]

    def feed_forward(step, micro):
        arrive_mod(micro)
        mod = mods_ref[micro]
        gain = gain_ref[...]

        slot = jnp.where(is_last, 0, lax.rem(micro, 2))
        first_slot_free(slot, jnp.logical_not(is_last) & (micro >= 2))

        @pl.when(micro >= 1)
        def _():
            store_active(micro).wait()

        @pl.when(micro >= 2)
        def _():
            store_rows(micro).wait()

        @pl.when(step >= 2)
        def _():
            leaving_free(step - 2)

        entering_rows = rows_kept(micro)
        def feed_cut(part, rows):
            arrive(micro, part, True)
            standard, _ = normalize(streams[micro, rows, :].astype(F32))
            entering = (standard * gain * (1.0 + mod[1:2]) + mod[0:1]).astype(BF16)
            entering_rows[rows, :] = entering
            for piece, (block, lane) in enumerate(pieces):
                lanes = slice(piece * part_rows, (piece + 1) * part_rows)
                value = (
                    dot_nn(entering, weights[block * features : (block + 1) * features, lane : lane + part_rows])
                    + bias_row_ref[:, lanes]
                )
                square = value * value
                bend = jnp.tanh(GELU_C * value * (1.0 + 0.044715 * square))
                raised = 0.5 + 0.5 * bend
                second_buf[rows, lanes] = (value * raised).astype(BF16)
                first_buf[slot, rows, lanes] = (
                    raised + (0.5 * GELU_C) * value * (1.0 - bend * bend) * (1.0 + (3 * 0.044715) * square)
                ).astype(BF16)
            branch = dot_nn(second_buf[rows, :], pool[:hidden, :]) + out_bias_ref[...]
            branches[micro, rows, :] = branch.astype(BF16)
            result = streams[micro, rows, :].astype(F32) + mod[2:3] * branch
            leaving[lax.rem(step, 2), rows, :] = result.astype(BF16)
            send_part(step, part, micro, True)

        each_cut(feed_cut)
        place_result(step, micro, True)
        store_active(micro).start()
        store_rows(micro).start()

        @pl.when(jnp.logical_not(is_last))
        def _():
            store_first(slot, kept_first, micro).start()

    def fetch_kept(micro):
        return pltpu.make_async_copy(kept_first.at[micro], first_buf.at[0], fetch_sem.at[0])

    def attention_backward(step, micro):
        mod = mods_ref[micro]
        store_second(kept_second, micro).wait()
        first_slot_free(1, step >= micros)

        @pl.when(step == micros)
        def _():
            store_first(0, kept_first, 0).wait()
            fetch_kept(micro).start()
            for pair in range(pairs - 2, pairs):
                spread_store(pair, micros - 1).wait()
            spread_fetch(0, 0).start()

        @pl.when(is_first)
        def _():
            exchange_start(micro)

        grad_mixed_at = 2 * features

        def into_heads(source, part):
            grad_branch = (mod[2:3] * source[rows_of(part % PARTS), :].astype(F32)).astype(BF16)
            place = (part // PARTS) * features
            second_buf[rows_of(part % PARTS), place : place + features] = grad_branch
            if part < PARTS:
                bias_ref[0:1, 3 * features :] += jnp.sum(grad_branch.astype(F32), 0, keepdims=True)
            lanes = slice(grad_mixed_at + part * part_rows, grad_mixed_at + (part + 1) * part_rows)
            second_buf[:width, lanes] = dot_nt(weights[3 * width : 4 * width, :], grad_branch).astype(BF16)

        for part in range(PARTS):
            into_heads(upstreams.at[micro], part)

        @pl.when(step > micros)
        def _():
            finish_attention(step - 1, micro - 1)

        for part in range(CUTS):
            exchange(part, micro).wait_recv()
        for part in range(PARTS, 2 * PARTS):
            into_heads(up_others_at(micro), part)
        fetch_kept(micro).wait()
        near_lanes = pl.ds(pl.multiple_of(core * half, 128), half)
        far_lanes = pl.ds(pl.multiple_of((1 - core) * half, 128), half)
        cosine = jnp.concatenate([cos_ref[:, near_lanes], cos_ref[:, far_lanes]], 1)
        sine = jnp.concatenate([sin_ref[:, near_lanes], sin_ref[:, far_lanes]], 1)

        def turn_back(base, block, gradient):
            front = gradient[:HALF] * SCALE
            back = gradient[HALF:] * SCALE
            turned = jnp.concatenate([front * cosine + back * sine, back * cosine - front * sine], 0)
            put_back(base, block, turned.astype(BF16))

        def put_back(base, block, gradient):
            first_buf[1, pl.ds(base, HEAD), block * length : (block + 1) * length] = gradient
            bias_columns[block, pl.ds(base, HEAD), 0:1] += jnp.sum(gradient.astype(F32), 1, keepdims=True)

        def one_head(head, within, mixed, kept):
            base = pl.multiple_of(head * HEAD, HEAD)
            query = first_buf[0, pl.ds(base, HEAD), :length]
            key = first_buf[0, pl.ds(base, HEAD), length : 2 * length]
            spread = spreads[kept, within]
            value = first_buf[0, pl.ds(base, HEAD), 2 * length :]
            grad_mixed = second_buf[pl.ds(base, HEAD), grad_mixed_at : grad_mixed_at + length]
            delta = jnp.sum(grad_mixed.astype(F32) * mixed.astype(F32), 0, keepdims=True)
            grad_spread = dot_nn(value.T, grad_mixed)
            grad_scores = (spread.astype(F32) * (grad_spread - delta)).astype(BF16)
            grad_value = dot_nn(spread, grad_mixed.T)
            grad_key = dot_nn(grad_scores, query.T)
            grad_query = dot_nn(key, grad_scores)
            turn_back(base, 0, grad_query)
            turn_back(base, 1, grad_key.T)
            put_back(base, 2, grad_value.T.astype(BF16))

        def head_pair(pair, carried):
            at = pl.multiple_of(pair * length, length)
            mixed = first_buf[0, width:, pl.ds(at, length)]
            spread_fetch(pair, micro).wait()
            ends = pair == pairs - 1

            @pl.when(jnp.logical_not(ends & (micro == micros - 1)))
            def _():
                spread_fetch(jnp.where(ends, 0, pair + 1), jnp.where(ends, micro + 1, micro)).start()

            kept = spread_slot(pair, micro)
            one_head(2 * pair, 0, mixed[:HEAD], kept)
            one_head(2 * pair + 1, 1, mixed[HEAD:], kept)
            return carried

        lax.fori_loop(0, heads // 2, head_pair, 0)

        for part in range(CUTS):
            exchange(part, micro).wait_send()

        @pl.when(step + 1 < 2 * micros)
        def _():
            fetch_kept(micro + 1).start()

            @pl.when(jnp.logical_not(is_first))
            def _():
                exchange_start(micro + 1)

        def grad_rows_of(part):
            begin = part * part_rows
            heads_of = [
                first_buf[1, :width, block * length + begin : block * length + begin + part_rows] for block in range(3)
            ]
            return dot_nn(jnp.concatenate(heads_of, 0).T, weights[: 3 * width, :])

        for part in range(PARTS):
            grad_send[rows_of(part), :] = grad_rows_of(PARTS + part).astype(BF16)
            give_grad(part, micro).start()
        store_first(1, back_first, micro).start()
        store_second(back_second, micro).start()
        for part in range(PARTS):
            grad_own[rows_of(part), :] = grad_rows_of(part)

    def finish_attention(step, micro):
        mod = mods_ref[micro]
        gain = gain_ref[...]
        leaving_free(step - 2)
        given = others_at(micro)
        sums_ref[micro] = jnp.zeros((8, features), F32)

        def finish_cut(part, rows):
            @pl.when(lax.rem(part, CUTS // PARTS) == 0)
            def _():
                give_grad(part // (CUTS // PARTS), micro).wait_recv()

            finish_back(
                grad_own[rows, :] + given[rows, :].astype(F32),
                streams[micro, rows, :].astype(F32),
                upstreams[micro, rows, :].astype(F32),
                branches[micro, rows, :].astype(F32),
                mod, gain,
                jnp.logical_not(in_span(micro, core * half + part * cut_rows, cut_rows) & is_first),
                leaving, (lax.rem(step, 2), rows), sums_ref, micro,
            )
            send_part(step, part, micro, False)

        each_cut(finish_cut)
        place_result(step, micro, False)
        for part in range(PARTS):
            give_grad(part, micro).wait_send()

    def feed_backward(step, micro):
        mod = mods_ref[micro]
        gain = gain_ref[...]
        inner = jnp.logical_not(is_last)

        @pl.when(inner & (step == micros))
        def _():
            store_first(0, kept_first, 0).wait()
            store_first(1, kept_first, 0).wait()
            fetch_kept(micro).start()

        @pl.when(micro >= 1)
        def _():
            store_first(1, back_first, 0).wait()
            store_grad_branch(micro).wait()

        @pl.when(step >= 2)
        def _():
            leaving_free(step - 2)

        @pl.when(inner)
        def _():
            fetch_kept(micro).wait()

        arrive_cot(micro)
        sums_ref[micro] = jnp.zeros((8, features), F32)

        def feed_cut(part, rows):
            arrive(micro, part, False)
            upstream = upstreams[micro, rows, :].astype(F32)
            grad_branch = (mod[2:3] * upstream).astype(BF16)
            grad_send[rows, :] = grad_branch
            bias_ref[1:2, :features] += jnp.sum(grad_branch.astype(F32), 0, keepdims=True)
            for piece in range(len(pieces)):
                lanes = slice(piece * part_rows, (piece + 1) * part_rows)
                grad_active = dot_nt(grad_branch, pool[lanes, :])
                grad_hidden = (grad_active * first_buf[0, rows, lanes].astype(F32)).astype(BF16)
                first_buf[1, rows, lanes] = grad_hidden
                bias_ref[0:1, lanes] += jnp.sum(grad_hidden.astype(F32), 0, keepdims=True)
            total = None
            for block in range(blocks):
                lanes = slice(block * features, (block + 1) * features)
                term = dot_nt(first_buf[1, rows, lanes], weights[lanes, :])
                total = term if total is None else total + term
            finish_back(
                total,
                streams[micro, rows, :].astype(F32),
                upstream,
                branches[micro, rows, :].astype(F32),
                mod, gain, None,
                leaving, (lax.rem(step, 2), rows), sums_ref, micro,
            )
            send_part(step, part, micro, False)

        each_cut(feed_cut)
        place_result(step, micro, False)
        store_first(1, back_first, micro).start()
        store_grad_branch(micro).start()

        @pl.when(inner & (step + 1 < 2 * micros))
        def _():
            fetch_kept(micro + 1).start()

    def one_step(step, carried):
        forward, micro = schedule(step)
        backward = jnp.logical_not(forward)

        @pl.when(attends & forward)
        def _():
            attention_forward(step, micro)

        @pl.when(attends & backward)
        def _():
            attention_backward(step, micro)

        @pl.when(feeds & forward)
        def _():
            feed_forward(step, micro)

        @pl.when(feeds & backward)
        def _():
            feed_backward(step, micro)

        return carried

    lax.fori_loop(0, 2 * micros, one_step, 0)

    @pl.when(attends)
    def _():
        finish_attention(2 * micros - 1, micros - 1)
        for block in range(3):
            at = pl.multiple_of(block * features + core * width, 128)
            bias_ref[0:1, pl.ds(at, width)] = bias_columns[block].T[0:1]

    store_first(1, back_first, 0).wait()

    @pl.when(attends)
    def _():
        store_second(back_second, 0).wait()

    @pl.when(feeds)
    def _():
        store_active(0).wait()
        store_grad_branch(0).wait()
        store_rows(0).wait()
        store_rows(1).wait()

    leaving_free(2 * micros - 2)
    leaving_free(2 * micros - 1)
    for i in range(seqs):
        mod_give(i).wait_send()

        @pl.when(is_first)
        def _():
            for copy in token_gives(i):
                copy.wait_send()

        @pl.when(is_last)
        def _():
            cot_give(i).wait_send()

    for index, target in enumerate((states_ref, stream_ref)):
        for slot in range(micros // 2):
            pltpu.make_async_remote_copy(
                leaving.at[0], target.at[slot, pl.ds((1 - core) * half, half)], place_send.at[0],
                place_recv.at[index, slot], device_id=(partner, section), device_id_type=MESH,
            ).wait_recv()


def finish_back(
    grad_rows, stream, upstream, branch, mod, gain, keep, leaving, place, sums_ref, micro,
):
    standard, inverse_std = normalize(stream)
    scaling = mod[1:2, :]
    grad_normed = grad_rows * (1.0 + scaling)
    grad_hat = grad_normed * gain
    grad_stream = upstream + inverse_std * (
        grad_hat
        - jnp.mean(grad_hat, -1, keepdims=True)
        - standard * jnp.mean(grad_hat * standard, -1, keepdims=True)
    )
    row_sum = lambda value: jnp.sum(value, 0, keepdims=True)
    with_standard = row_sum(grad_rows * standard)
    sums = [
        row_sum(grad_rows),
        with_standard * gain,
        row_sum(upstream * branch),
        with_standard * (1.0 + scaling),
    ]
    slot, rows = place
    if keep is None:
        sums.append(jnp.zeros_like(sums[0]))
        leaving[slot, rows, :] = grad_stream.astype(BF16)
    else:
        kept = jnp.where(keep, grad_stream, 0.0)
        sums.append(row_sum(grad_stream - kept))
        leaving[slot, rows, :] = kept.astype(BF16)
    sums = jnp.concatenate(sums + [jnp.zeros((3, sums[0].shape[1]), F32)], 0)
    sums_ref[micro] += sums


def pipeline(
    tokens, cot, first, second, span_start, span_length, time_step, table, embed, mod_weight, mod_bias, gain,
    bias_row, out_bias, cosine, sine,
):
    seqs, length, features = tokens.shape
    micros = 2 * seqs
    half = length // 2
    width = features // 2
    hidden = second.shape[0]
    anywhere = pl.BlockSpec(memory_space=pl.ANY)
    inside = pl.BlockSpec(memory_space=pltpu.VMEM)
    scalars = pl.BlockSpec(memory_space=pltpu.SMEM)
    dma = pltpu.SemaphoreType.DMA
    rows = (micros, half, features)
    return pl.pallas_call(
        pipeline_kernel,
        in_specs=[anywhere] * 4 + [scalars] * 3 + [inside] * 9,
        out_specs=[anywhere] * 8 + [inside] * 2,
        out_shape=(
            shape((seqs, length, features), BF16),
            shape((seqs, length, features), BF16),
            shape((micros, half, hidden), BF16),
            shape((micros, half, hidden), BF16),
            shape(rows, BF16),
            shape((micros, half, hidden), BF16),
            shape((micros, half, hidden), BF16),
            shape((micros, width // HEAD, length, length), BF16),
            shape((micros, 8, features), F32),
            shape((8, hidden), F32),
        ),
        scratch_shapes=[
            pltpu.VMEM((hidden, features), BF16),
            pltpu.VMEM(rows, BF16),
            pltpu.VMEM((2 * micros * half, features), BF16),
            pltpu.VMEM(rows, BF16),
            pltpu.VMEM((micros, half, width), BF16),
            pltpu.VMEM((2, half, hidden), BF16),
            pltpu.VMEM((half, hidden), BF16),
            pltpu.VMEM(rows, BF16),
            pltpu.VMEM((2, half, features), BF16),
            pltpu.VMEM((half, width), BF16),
            pltpu.VMEM((half, width), BF16),
            pltpu.VMEM((half, features), BF16),
            pltpu.VMEM((half, features), F32),
            pltpu.VMEM((2, 2, length, length), BF16),
            pltpu.VMEM((3, width, 128), F32),
            pltpu.VMEM((micros, 8, features), F32),
            dma((hidden // features + hidden // half,)),
            dma((2, CUTS)),
            dma((micros, CUTS)),
            dma((micros, CUTS)),
            dma((2, CUTS)),
            dma((2, CUTS, micros)),
            dma((2,)),
            dma((2, seqs)),
            dma((6,)),
            dma((1,)),
            dma((seqs, 2)),
            dma((seqs, 2)),
            dma((seqs, 2)),
            dma((seqs,)),
            dma((seqs,)),
            dma((width // (2 * HEAD),)),
            dma((width // (2 * HEAD), micros)),
            dma((PARTS,)),
            dma((PARTS, micros)),
            dma((2,)),
        ],
        compiler_params=pltpu.CompilerParams(vmem_limit_bytes=60 << 20, collective_id=0, has_side_effects=True),
        name="pipeline",
    )(
        tokens, cot, first, second, span_start, span_length, time_step, table, embed, mod_weight, mod_bias, gain,
        bias_row, out_bias, cosine, sine,
    )


SMALL_ROWS = 24


def gradient_kernel(
    kept_first, kept_second, kept_rows, back_first, back_second, sums_ref, bias_ref, mod_weight_ref,
    summed_first, summed_second, small_ref, across_ref,
    wide_a, wide_b, deep_a, deep_b, total_a, total_b, give, got, scatter_send, scatter_got, summed, entry,
    load_sem, pair_send, pair_recv, step_send, step_recv, gather_send, gather_recv, core_send, core_recv,
    small_send, small_recv, store_sem, share_sem,
):
    section = lax.axis_index("section")
    dp_index = lax.axis_index("dp")
    chips = small_ref.shape[0]
    core = lax.rem(dp_index, 2)
    partner = dp_index + 1 - 2 * core
    attends = lax.rem(section, 2) == 0
    feeds = lax.rem(section, 2) == 1
    micros, half, hidden = back_first.shape
    features = kept_rows.shape[2]
    width = features // 2
    length = 2 * half
    mid = hidden // 2
    bits = chips.bit_length() - 1
    small_bits = bits + 1
    cuts = part_cuts(mid, features, bits)

    def bit_of(place):
        return lax.rem(dp_index // (1 << place), 2)

    def across(place):
        return dp_index + (1 - 2 * bit_of(place)) * (1 << place)

    barrier = pltpu.get_barrier_semaphore()
    for place in range(small_bits):
        pl.semaphore_signal(barrier, inc=1, device_id=(across(place), section), device_id_type=MESH)

    def small_entry():
        rows = [sums_ref[m, k : k + 1, :] for m in range(micros) for k in range(3)]
        gain = sum(sums_ref[m, 3:4, :] for m in range(micros))
        embed = sum(sums_ref[m, 4:5, :] for m in range(micros))
        rows.append(gain)
        rows += [bias_ref[0:1, k * features : (k + 1) * features] for k in range(hidden // features)]
        rows.append(bias_ref[1:2, :features])
        condition = []
        for m in range(micros):
            total = None
            for k in range(3):
                term = lax.dot_general(
                    jnp.broadcast_to(sums_ref[m, k : k + 1, :], (8, features)),
                    mod_weight_ref[:, k * features : (k + 1) * features],
                    (((1,), (1,)), ((), ())), precision=HIGH, preferred_element_type=F32,
                )
                total = term if total is None else total + term
            condition.append(total[0:1])
        condition.append(jnp.zeros((1, features - micros * mod_weight_ref.shape[0]), F32))
        rows.append(jnp.concatenate(condition, 1))
        rows.append(embed)
        rows += [bias_ref[2:3, :features], bias_ref[3:4, :features]]
        rows.append(jnp.zeros((SMALL_ROWS - len(rows), features), F32))
        entry[0] = jnp.concatenate(rows, 0)

    def small_block(step, theirs):
        size = 1 << (step - 1)
        chip = dp_index // 2
        start = (chip // size) * size
        if theirs:
            start = start + (1 - 2 * bit_of(step)) * size
        return small_ref.at[pl.ds(start, size)]

    def small_copy(step, theirs=False):
        source, target = entry.at[0], entry.at[1]
        if step > 0:
            source = target = small_block(step, theirs)
        return pltpu.make_async_remote_copy(
            source, target, small_send.at[step], small_recv.at[step],
            device_id=(across(step), section), device_id_type=MESH,
        )

    def small_wait(step):
        small_copy(step, True).wait_recv()
        small_copy(step).wait_send()
        if step == 0:
            small_ref[pl.ds(dp_index // 2, 1)] = (entry[0] + entry[1])[None]

    def small_step(number):
        if 1 <= number <= small_bits:
            small_wait(number - 1)
            if number < small_bits:
                small_copy(number).start()

    def loads(pairs, first_sem):
        return [
            pltpu.make_async_copy(source, target, load_sem.at[first_sem + i])
            for i, (source, target) in enumerate(pairs)
        ]

    def spans(m):
        return slice(m * half, (m + 1) * half)

    def heads_rows(source, target, first_sem):
        return loads(
            [(source.at[m, :, pl.ds(0, 2 * features)], target.at[spans(m), :]) for m in range(micros)], first_sem
        )

    def heads_columns(block, target, first_sem):
        pairs = []
        for m in range(micros):
            for side in range(2):
                at = side * half
                if block < 3:
                    source = back_first.at[m, pl.ds(0, width), pl.ds(block * length + at, half)]
                    pairs.append((source, target.at[pl.ds(side * width, width), spans(m)]))
                    continue
                for pair in range(3):
                    rows = width // 3
                    source = kept_first.at[m, pl.ds(width, rows), pl.ds(pair * length + at, half)]
                    pairs.append((source, target.at[pl.ds(side * width + pair * rows, rows), spans(m)]))
        return loads(pairs, first_sem)

    def half_columns(source, which, target, first_sem):
        return loads(
            [(source.at[m, :, pl.ds(which * mid, mid)], target.at[spans(m), :]) for m in range(micros)], first_sem
        )

    totals = (total_a, total_b)

    def place_order(part):
        order = list(range(1, bits + 1))
        return order if part == 0 else order[::-1]

    def window(part, steps):
        start, size, _, _ = cuts[part]
        for place in place_order(part)[:steps]:
            size = size // 2
            start = start + bit_of(place) * size
        return start, size

    def lanes(part, piece):
        _, _, column, count = cuts[part]
        return slice(column + piece * count // PIECES, column + (piece + 1) * count // PIECES)

    def buffer_at(part, piece, step):
        _, rows, _, count = cuts[part]
        begin = rows - (rows >> step)
        return slice(begin, begin + (rows >> (step + 1))), slice(piece * count // PIECES, (piece + 1) * count // PIECES)

    def step_copy(payload, part, piece, step):
        rows, cut = buffer_at(part, piece, step)
        return pltpu.make_async_remote_copy(
            scatter_send.at[payload, part, rows, cut], scatter_got.at[payload, part, rows, cut],
            step_send.at[payload, part, piece, step], step_recv.at[payload, part, piece, step],
            device_id=(across(place_order(part)[step]), section), device_id_type=MESH,
        )

    def scatter_start(payload, part, piece, step):
        start, size = window(part, step)
        size = size // 2
        away = pl.multiple_of(start + (1 - bit_of(place_order(part)[step])) * size, 16)
        rows, cut = buffer_at(part, piece, step)
        scatter_send[payload, part, rows, cut] = totals[payload][pl.ds(away, size), lanes(part, piece)].astype(BF16)
        step_copy(payload, part, piece, step).start()

    def scatter_finish(payload, part, piece, step):
        step_copy(payload, part, piece, step).wait()
        start, size = window(part, step + 1)
        rows = pl.ds(pl.multiple_of(start, 16), size)
        cut = lanes(part, piece)
        got_rows, got_cut = buffer_at(part, piece, step)
        value = totals[payload][rows, cut] + scatter_got[payload, part, got_rows, got_cut].astype(F32)
        if step < bits - 1:
            totals[payload][rows, cut] = value
        else:
            summed[payload, core, rows, cut] = value.astype(BF16)

    def gather_copy(payload, part, piece, step, theirs):
        place = place_order(part)[step]
        start, size = window(part, step + 1)
        if theirs:
            start = start + (1 - 2 * bit_of(place)) * size
        block = summed.at[payload, core, pl.ds(pl.multiple_of(start, 16), size), lanes(part, piece)]
        return pltpu.make_async_remote_copy(
            block, block, gather_send.at[payload, part, piece, step], gather_recv.at[payload, part, piece, step],
            device_id=(across(place), section), device_id_type=MESH,
        )

    def core_copy(payload, part, piece, step, other):
        if step == bits:
            start, size = window(part, bits)
        else:
            start, size = window(part, step + 1)
            start = start + (1 - 2 * bit_of(place_order(part)[step])) * size
        side = 1 - core if other else core
        block = summed.at[payload, side, pl.ds(pl.multiple_of(start, 16), size), lanes(part, piece)]
        return pltpu.make_async_remote_copy(
            block, block, core_send.at[payload, part, piece, step], core_recv.at[payload, part, piece, step],
            device_id=(partner, section), device_id_type=MESH,
        )

    def stage(payload, part, number):
        for piece in range(PIECES):
            if number <= bits:
                if number > 0:
                    scatter_finish(payload, part, piece, number - 1)
                if number < bits:
                    scatter_start(payload, part, piece, number)
                else:
                    gather_copy(payload, part, piece, bits - 1, False).start()
                    core_copy(payload, part, piece, bits, False).start()
            else:
                step = 2 * bits - number
                gather_copy(payload, part, piece, step, True).wait_recv()
                if step > 0:
                    gather_copy(payload, part, piece, step - 1, False).start()
                core_copy(payload, part, piece, step, False).start()

    last_stage = 2 * bits

    def store(payload, part):
        start, rows, column, count = cuts[part]
        target = (summed_first, summed_second)[payload]
        place = (slice(None), pl.ds(start, rows), pl.ds(column, count))
        return pltpu.make_async_copy(
            summed.at[(payload,) + place], target.at[place], store_sem.at[payload, part]
        )

    def wind_up(payload, part):
        for piece in range(PIECES):
            for step in range(bits):
                gather_copy(payload, part, piece, step, False).wait_send()
            for step in range(bits + 1):
                core_copy(payload, part, piece, step, False).wait_send()
                core_copy(payload, part, piece, step, True).wait_recv()
        store(payload, part).start()

    by_rows = cuts[1][0] > 0

    def after_half(payload, half_number):
        if by_rows:
            stage(payload, half_number, 0)
        elif half_number == 1:
            stage(payload, 0, 0)
            stage(payload, 1, 0)

    buffers = (deep_a, deep_b)

    def head_loads():
        per = 2 * micros
        return (
            heads_rows(kept_second, wide_a, 0),
            heads_rows(back_second, wide_b, micros),
            [heads_columns(block, buffers[block % 2], 2 * micros + (block % 2) * 3 * per) for block in range(4)],
        )

    @pl.when(attends)
    def _():
        rows, _, blocks = head_loads()
        for copy in rows + blocks[0] + blocks[1]:
            copy.start()

    def transposed_rows(source, first_sem, staged):
        return loads(
            [
                (source.at[m, :, pl.ds(0, features)], staged.at[m // 2, pl.ds((m % 2) * half, half)])
                for m in range(micros)
            ],
            first_sem,
        )

    def turn(copies, staged, target):
        for m in range(micros):
            copies[m].wait()
            target[:, m * half : (m + 1) * half] = staged[m // 2, (m % 2) * half : (m % 2 + 1) * half, :].T

    def feed_loads():
        near, far = core, 1 - core
        return (
            transposed_rows(kept_rows, 0, summed.at[0]),
            transposed_rows(back_second, micros, summed.at[1]),
            half_columns(back_first, far, wide_a, 2 * micros),
            half_columns(back_first, near, wide_b, 3 * micros),
            half_columns(kept_second, far, wide_a, 4 * micros),
            half_columns(kept_second, near, wide_b, 5 * micros),
        )

    @pl.when(feeds)
    def _():
        first_rows, second_rows, first_far, first_near, _, _ = feed_loads()
        for copy in first_rows + first_far + first_near + second_rows:
            copy.start()

    def head_products(block, loaded):
        rows, grads, blocks = loaded
        if block == 0:
            for copy in rows:
                copy.wait()
        for copy in blocks[block]:
            copy.wait()
        source = wide_a if block < 3 else wide_b
        if block == 1:
            for copy in grads:
                copy.start()
        if block == 3:
            for copy in grads:
                copy.wait()
        deep = buffers[block % 2]
        total_a[block * width : (block + 1) * width, :] = dot_nn(
            deep[:width, :], source[:, :features]
        ) + dot_nn(deep[width:, :], source[:, features:])
        if block + 2 < 4:
            for copy in blocks[block + 2]:
                copy.start()

    def other_product(deep, wide, piece):
        rows = slice(piece * features, (piece + 1) * features)
        give[rows, :] = dot_nn(deep[...], wide[:, rows]).astype(BF16)

    small_entry()
    pl.semaphore_wait(barrier, small_bits)
    small_copy(0).start()

    @pl.when(attends)
    def _():
        loaded = head_loads()
        head_products(0, loaded)
        small_step(1)
        head_products(1, loaded)
        small_step(2)
        after_half(0, 0)
        for block in range(2, 4):
            head_products(block, loaded)
        small_step(3)
        after_half(0, 1)
        for number in range(1, last_stage + 1):
            stage(0, 0, number)
            stage(0, 1, number)
        for number in range(4, small_bits + 1):
            small_step(number)
        for part in range(2):
            wind_up(0, part)
        for part in range(2):
            store(0, part).wait()

    def pair_copy(payload, piece):
        rows = pl.ds(piece * features, features)
        return pltpu.make_async_remote_copy(
            give.at[rows], got.at[payload, rows], pair_send.at[payload, piece], pair_recv.at[payload, piece],
            device_id=(partner, section), device_id_type=MESH,
        )

    pieces = mid // features

    def own_product(payload, deep, wide, piece):
        rows = slice(piece * features, (piece + 1) * features)
        totals[payload][rows, :] = dot_nn(deep[...], wide[:, rows])

    def add_pair(payload, piece):
        rows = slice(piece * features, (piece + 1) * features)
        pair_copy(payload, piece).wait()
        totals[payload][rows, :] += got[payload, rows, :].astype(F32)
        after_half(payload, piece)

    @pl.when(feeds)
    def _():
        first_rows, second_rows, first_far, first_near, second_far, second_near = feed_loads()
        turn(first_rows, summed.at[0], deep_a)
        for copy in first_far:
            copy.wait()
        other_product(deep_a, wide_a, 0)
        pair_copy(0, 0).start()
        small_step(1)
        for copy in first_near:
            copy.wait()
        own_product(0, deep_a, wide_b, 0)
        small_step(2)
        for piece in range(1, pieces):
            other_product(deep_a, wide_a, piece)
            pair_copy(0, piece).start()
        for copy in second_far:
            copy.start()
        add_pair(0, 0)
        for piece in range(1, pieces):
            own_product(0, deep_a, wide_b, piece)
        for copy in second_near:
            copy.start()
        for piece in range(1, pieces):
            add_pair(0, piece)
        small_step(3)
        turn(second_rows, summed.at[1], deep_b)
        for copy in second_far:
            copy.wait()
        for piece in range(pieces):
            other_product(deep_b, wide_a, piece)
            pair_copy(1, piece).start()
        for copy in second_near:
            copy.wait()
        stage(0, 0, 1)
        own_product(1, deep_b, wide_b, 0)
        add_pair(1, 0)
        stage(0, 1, 1)
        for piece in range(1, pieces):
            own_product(1, deep_b, wide_b, piece)
            add_pair(1, piece)
        for number in range(2, last_stage + 2):
            if number <= last_stage:
                stage(0, 0, number)
                stage(0, 1, number)
            stage(1, 0, number - 1)
            stage(1, 1, number - 1)
        for number in range(4, small_bits + 1):
            small_step(number)
        for payload in range(2):
            for part in range(2):
                wind_up(payload, part)
        for payload in range(2):
            for part in range(2):
                store(payload, part).wait()

    share = pltpu.make_async_copy(small_ref.at[:, pl.ds(SMALL_ROWS - 8, 8)], across_ref, share_sem)
    share.start()
    share.wait()


PIECES = 3


def part_cuts(mid, features, bits):
    if (mid // 2 >> bits) % 16 == 0:
        return [(0, mid // 2, 0, features), (mid // 2, mid // 2, 0, features)]
    return [(0, mid, 0, features // 2), (0, mid, features // 2, features // 2)]


def summed_gradients(kept_first, kept_second, kept_rows, back_first, back_second, sums, bias, mod_weight, dp_count):
    micros, half, hidden = back_first.shape
    features = kept_rows.shape[2]
    mid = hidden // 2
    small_bits = dp_count.bit_length() - 1
    bits = small_bits - 1
    anywhere = pl.BlockSpec(memory_space=pl.ANY)
    inside = pl.BlockSpec(memory_space=pltpu.VMEM)
    dma = pltpu.SemaphoreType.DMA
    tokens = micros * half
    _, rows, _, columns = part_cuts(mid, features, bits)[0]
    return pl.pallas_call(
        gradient_kernel,
        in_specs=[anywhere] * 5 + [inside] * 3,
        out_specs=[anywhere] * 2 + [inside, anywhere],
        out_shape=(
            shape((2, mid, features), BF16),
            shape((2, mid, features), BF16),
            shape((dp_count // 2, SMALL_ROWS, features), F32),
            shape((dp_count // 2, 8, features), F32),
        ),
        scratch_shapes=[
            pltpu.VMEM((tokens, mid), BF16),
            pltpu.VMEM((tokens, mid), BF16),
            pltpu.VMEM((features, tokens), BF16),
            pltpu.VMEM((features, tokens), BF16),
            pltpu.VMEM((mid, features), F32),
            pltpu.VMEM((mid, features), F32),
            pltpu.VMEM((mid, features), BF16),
            pltpu.VMEM((2, mid, features), BF16),
            pltpu.VMEM((2, 2, rows - (rows >> bits), columns), BF16),
            pltpu.VMEM((2, 2, rows - (rows >> bits), columns), BF16),
            pltpu.VMEM((2, 2, mid, features), BF16),
            pltpu.VMEM((2, SMALL_ROWS, features), F32),
            dma((14 * micros,)),
            dma((2, mid // features)),
            dma((2, mid // features)),
            dma((2, 2, PIECES, bits)),
            dma((2, 2, PIECES, bits)),
            dma((2, 2, PIECES, bits)),
            dma((2, 2, PIECES, bits)),
            dma((2, 2, PIECES, bits + 1)),
            dma((2, 2, PIECES, bits + 1)),
            dma((small_bits,)),
            dma((small_bits,)),
            dma((2, 2)),
            dma,
        ],
        compiler_params=pltpu.CompilerParams(vmem_limit_bytes=62 << 20, collective_id=1, has_side_effects=True),
        name="summed_gradients",
    )(kept_first, kept_second, kept_rows, back_first, back_second, sums, bias, mod_weight)


def small_places(small_ref, mod_weight_grad, mod_bias_grad, gain_grad, first_bias_grad, second_bias_grad):
    count = small_ref.shape[0]
    cond = mod_weight_grad.shape[0]
    features = gain_grad.shape[1]
    pairs = [small_ref[i] for i in range(count)]
    total = sum(pairs[1:], pairs[0])
    embedded = jnp.concatenate(embedded_of(small_ref, cond, 0), 0)
    conditions = embedded * (1.0 / (1.0 + jnp.exp(-embedded)))
    for k in range(3):
        rows = jnp.concatenate([pair[3 * m + k : 3 * m + k + 1] for pair in pairs for m in range(MICROS)], 0)
        lanes = slice(k * features, (k + 1) * features)
        mod_weight_grad[:, lanes] = lax.dot_general(
            conditions, rows, (((0,), (0,)), ((), ())), precision=HIGH, preferred_element_type=F32
        )
        mod_bias_grad[:, lanes] = sum((total[3 * m + k : 3 * m + k + 1] for m in range(1, MICROS)), total[k : k + 1])
    base = 3 * MICROS
    gain_grad[...] = total[base : base + 1]
    blocks = first_bias_grad.shape[1] // features
    for block in range(blocks):
        first_bias_grad[:, block * features : (block + 1) * features] = total[base + 1 + block : base + 2 + block]
    second_bias_grad[...] = total[base + 1 + blocks : base + 2 + blocks]


def attention_place_kernel(
    first_ref, small_ref, grad_in, grad_out, mod_weight_grad, mod_bias_grad, gain_grad, first_bias_grad,
    second_bias_grad, taken, turned, straight, zeros, load_sem, store_sem, zero_sem,
):
    features = grad_in.shape[0]
    width = features // 2
    parts = grad_out.shape[0] // width

    def load(index):
        rows = pl.ds((index // 2) * width, width)
        return pltpu.make_async_copy(first_ref.at[index % 2, rows], taken.at[index], load_sem.at[index])

    def store(index):
        if index < 6:
            source, target = turned.at[index], grad_in.at[:, pl.ds(index * width, width)]
        else:
            side = index - 6
            source, target = straight.at[side], grad_in.at[pl.ds(side * width, width), pl.ds(3 * features, features)]
        return pltpu.make_async_copy(source, target, store_sem.at[index])

    def clear(index):
        return pltpu.make_async_copy(zeros, grad_out.at[pl.ds(index * width, width)], zero_sem.at[index])

    for index in range(8):
        load(index).start()
    zeros[...] = jnp.zeros_like(zeros)
    for index in range(parts):
        clear(index).start()
    for index in range(8):
        load(index).wait()
        if index < 6:
            turned[index] = taken[index].T.astype(F32)
        else:
            straight[index - 6] = taken[index].astype(F32)
        store(index).start()
    small_places(small_ref, mod_weight_grad, mod_bias_grad, gain_grad, first_bias_grad, second_bias_grad)
    for index in range(8):
        store(index).wait()
    for index in range(parts):
        clear(index).wait()


def feed_place_kernel(
    first_ref, second_ref, small_ref, grad_in, grad_out, mod_weight_grad, mod_bias_grad, gain_grad, first_bias_grad,
    second_bias_grad, taken, straight, turned, load_sem, store_sem,
):
    features = grad_in.shape[0]
    width = features // 2

    def load(payload, index):
        source = (first_ref, second_ref)[payload]
        rows = pl.ds(((index % 4) // 2) * features, features)
        return pltpu.make_async_copy(
            source.at[index // 4, rows, pl.ds((index % 2) * width, width)], taken.at[payload, index],
            load_sem.at[payload, index],
        )

    def store(payload, index):
        if payload == 0:
            source, target = straight.at[index], grad_in.at[:, pl.ds(index * width, width)]
        else:
            source, target = turned.at[index], grad_out.at[pl.ds(index * width, width)]
        return pltpu.make_async_copy(source, target, store_sem.at[payload, index])

    for index in range(8):
        for payload in range(2):
            load(payload, index).start()
    for index in range(8):
        load(0, index).wait()
        straight[index] = taken[0, index].astype(F32)
        store(0, index).start()
        load(1, index).wait()
        turned[index] = taken[1, index].T.astype(F32)
        store(1, index).start()
    small_places(small_ref, mod_weight_grad, mod_bias_grad, gain_grad, first_bias_grad, second_bias_grad)
    for index in range(8):
        for payload in range(2):
            store(payload, index).wait()


MICROS = 4


def embedded_of(small_ref, cond, group):
    seqs = MICROS // 2
    return [
        small_ref[
            chip, SMALL_ROWS - 4 + core : SMALL_ROWS - 3 + core, (group * seqs + i) * cond : (group * seqs + i + 1) * cond
        ]
        for chip in range(small_ref.shape[0])
        for i in range(seqs)
        for core in range(2)
    ]


def place_gradients(attends, first, second, small, cond, hidden):
    features = first.shape[2]
    width = features // 2
    anywhere = pl.BlockSpec(memory_space=pl.ANY)
    inside = pl.BlockSpec(memory_space=pltpu.VMEM)
    dma = pltpu.SemaphoreType.DMA
    small_dims = ((cond, 3 * features), (1, 3 * features), (1, features), (1, hidden), (1, features))
    outputs = dict(
        out_specs=[anywhere] * 2 + [inside] * 5,
        out_shape=(shape((features, hidden), F32), shape((hidden, features), F32))
        + tuple(shape(dims, F32) for dims in small_dims),
        compiler_params=params(),
    )
    tall, wide = (features, width), (width, features)

    def attention_half():
        return tuple(
            pl.pallas_call(
                attention_place_kernel,
                in_specs=[anywhere, inside],
                scratch_shapes=[
                    pltpu.VMEM((8,) + wide, BF16),
                    pltpu.VMEM((6,) + tall, F32),
                    pltpu.VMEM((2,) + wide, F32),
                    pltpu.VMEM(wide, F32),
                    dma((8,)),
                    dma((8,)),
                    dma((hidden // width,)),
                ],
                name="place_attention",
                **outputs,
            )(first, small)
        )

    def feed_half():
        return tuple(
            pl.pallas_call(
                feed_place_kernel,
                in_specs=[anywhere, anywhere, inside],
                scratch_shapes=[
                    pltpu.VMEM((2, 8) + tall, BF16),
                    pltpu.VMEM((8,) + tall, F32),
                    pltpu.VMEM((8,) + wide, F32),
                    dma((2, 8)),
                    dma((2, 8)),
                ],
                name="place_feed",
                **outputs,
            )(first, second, small)
        )

    return lax.cond(attends, attention_half, feed_half)


def table_kernel(small_ref, own_ref, one_ref, two_ref, three_ref, table_grad, embed_grad):
    steps, cond = table_grad.shape
    across = sum((ref[:, 2:4, :] for ref in (one_ref, two_ref, three_ref)), own_ref[:, 2:4, :])
    count = across.shape[0]
    embed_grad[...] = sum((across[i, 1] for i in range(1, count)), across[0, 1])
    embedded = jnp.concatenate(embedded_of(small_ref, cond, 0), 0)
    chosen = jnp.concatenate(embedded_of(small_ref, cond, 1), 0)[:, 0:1]
    gradients = []
    for chip in range(count):
        row = across[chip, 0:1]
        gradients += [row[:, m * cond : (m + 1) * cond] for m in range(MICROS)]
    squash = 1.0 / (1.0 + jnp.exp(-embedded))
    gradient = jnp.concatenate(gradients, 0) * (squash * (1.0 + embedded * (1.0 - squash)))
    places = lax.broadcasted_iota(jnp.int32, (chosen.shape[0], steps), 1).astype(F32)
    onehot = jnp.where(places == chosen, 1.0, 0.0)
    table_grad[...] = lax.dot_general(
        onehot, gradient, (((0,), (0,)), ((), ())), precision=HIGH, preferred_element_type=F32
    )


def table_gradients(small, across, steps, cond):
    return pl.pallas_call(
        table_kernel,
        out_shape=(shape((steps, cond), F32), shape((small.shape[2],), F32)),
        compiler_params=params(),
        name="table_gradients",
    )(small, *across)


def rope_tables(length):
    position = np.arange(length, dtype=np.float32)[None, :]
    column = np.arange(HALF, dtype=np.float32)[:, None]
    angles = position * np.exp(column * np.float32(-2.0 * math.log(10000.0) / HEAD))
    return jnp.asarray(np.cos(angles)), jnp.asarray(np.sin(angles))


def shards(
    tokens, span_start, span_length, time_step, time_table, mask_embed, mod_weight, mod_bias,
    norm_gain, in_weight, in_bias, out_weight, out_bias, cotangent,
):
    sections = lax.axis_size("section")
    dp_count = lax.axis_size("dp")
    seqs, length, features = tokens.shape
    hidden = in_weight.shape[2]
    steps, cond = time_table.shape
    cosine, sine = rope_tables(length)
    states, stream, kept_first, kept_second, kept_rows, back_first, back_second, _, sums, bias = pipeline(
        tokens, cotangent, in_weight[0], out_weight[0], span_start, span_length, time_step, time_table,
        mask_embed[None], mod_weight[0], mod_bias, norm_gain, in_bias, out_bias, cosine, sine,
    )
    summed_first, summed_second, small, across = summed_gradients(
        kept_first, kept_second, kept_rows, back_first, back_second, sums, bias, mod_weight[0], dp_count
    )
    turns = [
        lax.ppermute(across, "section", [(s, (s + turn) % sections) for s in range(sections)])
        for turn in range(1, sections)
    ]
    grad_in, grad_out, grad_mod_weight, grad_mod_bias, grad_gain, grad_bias_first, grad_bias_second = place_gradients(
        lax.axis_index("section") % 2 == 0, summed_first, summed_second, small, cond, hidden
    )
    table_total, embed_total = table_gradients(small, [across] + turns, steps, cond)
    return (
        states[None],
        stream[None],
        table_total,
        embed_total,
        grad_mod_weight[None],
        grad_mod_bias,
        grad_gain,
        grad_in[None],
        grad_bias_first,
        grad_out[None],
        grad_bias_second,
    )


def solution(mesh):
    placed = (
        P("dp", None, None),
        P("dp"),
        P("dp"),
        P("dp"),
        P(),
        P(),
        P("section", None, None),
        P("section", None),
        P("section", None),
        P("section", None, None),
        P("section", None),
        P("section", None, None),
        P("section", None),
        P("dp", None, None),
    )
    return jax.shard_map(
        shards,
        mesh=mesh,
        in_specs=placed,
        out_specs=(
            P("section", "dp", None, None),
            P("section", "dp", None, None),
            P(),
            P(),
            P("section", None, None),
            P("section", None),
            P("section", None),
            P("section", None, None),
            P("section", None),
            P("section", None, None),
            P("section", None),
        ),
        check_vma=False,
    )
```
